32 devices in a mesh: macro: 8 (over z, y), micro: 4 (over x, core).
Axes of the slice: x: 2, y: 2, z: 4, core: 2. Of those that a mesh axis runs over, the one named last changes fastest.
Arguments:
- motion: float32 [3, 64, 32, 128], P(None, 'macro', 'micro'), may hold values from -6 to 6
- stiffness: bfloat16 [64, 32, 128], P('macro', 'micro'), may hold values from 0.5 to 5
- point_elem: int32 [4096], P(('macro', 'micro')), may hold values from 0 to 7039, as said below
- point_owner: int32 [4096], P(('macro', 'micro')), may hold values from 0 to 7, as said below
- point_pattern: int32 [4096], P(('macro', 'micro')), may hold values from 0 to 63
- history: bfloat16 [256, 4096], P(None, ('macro', 'micro')), may hold values from -6 to 6
- basis: bfloat16 [8, 6144, 256], P('macro'), may hold values from -0.375 to 0.375
- mode_map: bfloat16 [256, 6], replicated, may hold values from -2.5 to 2.5
- weights: float32 [1024], replicated, may hold values from 0.005 to 0.05
- patterns: int32 [64, 35], replicated, may hold values from 0 to 1073741823
Outputs:
- force: float32 [3, 64, 32, 128], P(None, 'macro', 'micro')
- tangent: float32 [36, 4096], P(None, ('macro', 'micro'))
The draws below stay inside these ranges and needn't reach their ends.
Inputs may be any that keep to these rules, and one draw needn't show every extreme that they name: `point_elem`: each row names an element of the block of the device that holds the row, with i < 7 and j < 7; the rows of one device name distinct elements. `point_owner`: the RVE of a row is hosted by the device with this macro index and the same micro index as the row's device; at most 32 rows of one device name the same host.
All inputs are finite; a program needn't handle non-finite values.
Results may differ from the reference program's by a relative error of at most 0.0004.
Values may be sent and summed in bfloat16 or wider, within the bound.
No kernel may reach another device: no remote copies, remote signals or barrier semaphores. Data moves between devices by JAX's collectives and lax.ppermute only.
A program may use at most 64 MiB of HBM per device.

```python
import math
import jax
import jax.numpy as jnp
import numpy as np
from jax import lax

CX = 8
CY = 8
CZ = 128
P_DEV = 128
MODES = 256
HYPER = 1024
PATTERNS = 64
FLAGW = 35
CAP = 32
NX = 64
NY = 32
POINTS = 4096
N_MACRO = 8
N_MICRO = 4


def draw_point_elem(key, part):
    key = jax.random.fold_in(key, 11)
    blocks = POINTS // P_DEV
    interior = (CX - 1) * (CY - 1) * CZ
    special = jax.random.randint(jax.random.fold_in(key, 5), (), 0, blocks)
    block_base = jax.random.fold_in(key, 101)

    def block_draw(block_id):
        block_key = jax.random.fold_in(block_base, block_id)
        scores = jax.random.permutation(block_key, interior)
        ladder = jnp.arange(interior, dtype=jnp.int32)
        forced = (block_id == special) & ((ladder == 0) | (ladder == interior - 1))
        scores = jnp.where(forced, -1, scores)
        picked = jnp.argsort(scores, stable=True)[:P_DEV]
        picked = picked[jax.random.permutation(jax.random.fold_in(block_key, 1), P_DEV)]
        plane_x = picked // ((CY - 1) * CZ)
        plane_y = picked // CZ % (CY - 1)
        depth_z = picked % CZ
        return ((plane_x * CY + plane_y) * CZ + depth_z).astype(jnp.int32)
    return jax.vmap(block_draw)(jnp.arange(blocks, dtype=jnp.int32)).reshape(-1)


def draw_point_owner(key, part):
    key = jax.random.fold_in(key, 23)
    blocks = POINTS // P_DEV
    hosts = NX // CX
    columns = blocks // hosts
    capacity = 2 * P_DEV // hosts
    slot_total = capacity * hosts
    busy_base = jax.random.fold_in(key, 3)
    block_base = jax.random.fold_in(key, 101)

    def block_draw(block_id):
        column = block_id % columns
        busiest = jax.random.randint(jax.random.fold_in(busy_base, column), (), 0, hosts)
        block_key = jax.random.fold_in(block_base, block_id)
        scores = jax.random.permutation(block_key, slot_total)
        host_of = jnp.arange(slot_total, dtype=jnp.int32) // capacity
        scores = jnp.where(host_of == busiest, -1, scores)
        picked = jnp.argsort(scores, stable=True)[:P_DEV] // capacity
        picked = picked[jax.random.permutation(jax.random.fold_in(block_key, 1), P_DEV)]
        return picked.astype(jnp.int32)
    return jax.vmap(block_draw)(jnp.arange(blocks, dtype=jnp.int32)).reshape(-1)


def touch_ends(values, rng, smallest, largest):
    longest = values.shape.index(max(values.shape))
    spots = []
    for shift in (0, 1):
        where = [jax.random.randint(jax.random.fold_in(rng, axis), (), 0, length) for axis, length in enumerate(values.shape)]
        where[longest] = (where[longest] + shift) % values.shape[longest]
        spots.append(tuple(where))
    return values.at[spots[0]].set(smallest).at[spots[1]].set(largest)


def steps_of(key, dims, split, least, high):
    gain, own = 1.0, jax.random.fold_in(key, 6)
    for axis_at, parts in split:
        draws = jnp.exp(jax.random.uniform(jax.random.fold_in(own, axis_at), (parts,), jnp.float32, least / len(split), high / len(split)))
        gain = gain * jnp.repeat(draws, dims[axis_at] // parts).reshape([-1 if axis == axis_at else 1 for axis in range(len(dims))])
    return gain


def bell_draw(stream_key, extent, deviation, limit, cuts=(), kind=jnp.bfloat16):
    values = deviation * jax.random.normal(stream_key, extent, jnp.float32)
    if cuts:
        values = values * steps_of(stream_key, extent, cuts, -0.22, 0.18)
    return jnp.clip(values, -limit, limit).astype(kind)


def setup_inputs(seed: int = 0) -> dict:
    arg_keys = jax.random.split(jax.random.key(seed), 11)
    return {
        "motion": bell_draw(arg_keys[0], (3, NX, NY, CZ), 1.0, 6.0, ((1, 8), (2, 4)), jnp.float32),
        "stiffness": jnp.clip(jnp.exp(math.log(5.0) - 2.3025851 * jax.random.uniform(arg_keys[1], (NX, NY, CZ), jnp.float32) ** steps_of(arg_keys[1], (NX, NY, CZ), ((0, 8), (1, 4)), -0.2, 0.2)), 0.5, 5.0).astype(jnp.bfloat16),
        "point_elem": draw_point_elem(jax.random.fold_in(arg_keys[10], 71), 0),
        "point_owner": draw_point_owner(jax.random.fold_in(arg_keys[10], 71), 0),
        "point_pattern": touch_ends(jax.random.randint(arg_keys[4], (POINTS,), 0, PATTERNS), jax.random.fold_in(arg_keys[4], 1), 0, PATTERNS - 1).astype(jnp.int32),
        "history": bell_draw(arg_keys[5], (MODES, POINTS), 1.0, 6.0, ((1, 32),)),
        "basis": bell_draw(arg_keys[6], (N_MACRO, 6 * HYPER, MODES), MODES ** -0.5, 0.375, ((0, 8),)),
        "mode_map": bell_draw(arg_keys[7], (MODES, 6), 6 ** -0.5, 2.5),
        "weights": jnp.clip(jnp.exp(jax.random.uniform(arg_keys[8], (HYPER,), jnp.float32, math.log(0.005), math.log(0.05))), 0.005, 0.05),
        "patterns": touch_ends(jax.random.randint(arg_keys[9], (PATTERNS, FLAGW), 0, 2 ** 30), jax.random.fold_in(arg_keys[9], 1), 0, (2 ** 30) - 1).astype(jnp.int32),
    }


BULK_MODULUS = 1.0
SHEAR_MODULUS = 0.5
YIELD_STRESS = 1.5
HARDENING = 0.2
DEVIATOR = np.array([[2.0 / 3, -1.0 / 3, -1.0 / 3, 0, 0, 0], [-1.0 / 3, 2.0 / 3, -1.0 / 3, 0, 0, 0], [-1.0 / 3, -1.0 / 3, 2.0 / 3, 0, 0, 0], [0, 0, 0, 0.5, 0, 0], [0, 0, 0, 0, 0.5, 0], [0, 0, 0, 0, 0, 0.5]], np.float32)

def element_strains(node_field):
    diff_x = node_field[:, 1:, :, :] - node_field[:, :-1, :, :]
    grad_x = (diff_x[:, :, :-1, :-1] + diff_x[:, :, 1:, :-1] + diff_x[:, :, :-1, 1:] + diff_x[:, :, 1:, 1:]) * 0.25
    diff_y = node_field[:, :, 1:, :] - node_field[:, :, :-1, :]
    grad_y = (diff_y[:, :-1, :, :-1] + diff_y[:, 1:, :, :-1] + diff_y[:, :-1, :, 1:] + diff_y[:, 1:, :, 1:]) * 0.25
    diff_z = node_field[:, :, :, 1:] - node_field[:, :, :, :-1]
    grad_z = (diff_z[:, :-1, :-1, :] + diff_z[:, 1:, :-1, :] + diff_z[:, :-1, 1:, :] + diff_z[:, 1:, 1:, :]) * 0.25
    return jnp.stack([grad_x[0], grad_y[1], grad_z[2], grad_z[1] + grad_y[2], grad_z[0] + grad_x[2], grad_y[0] + grad_x[1]])

def elastic_stress(strain, stiff_field):
    volume = strain[0] + strain[1] + strain[2]
    normal = [stiff_field * (BULK_MODULUS * volume + 2.0 * SHEAR_MODULUS * (strain[c] - volume / 3.0)) for c in range(3)]
    shears = [stiff_field * (SHEAR_MODULUS * strain[c]) for c in range(3, 6)]
    return jnp.stack(normal + shears)

def nodal_forces(padded_stress):
    shape_x, shape_y, shape_z = (padded_stress.shape[1], padded_stress.shape[2], padded_stress.shape[3])
    force_x = 0.0
    force_y = 0.0
    force_z = 0.0
    for a in (0, 1):
        for b in (0, 1):
            for c in (0, 1):
                corner_stress = padded_stress[:, 1 - a:shape_x - a, 1 - b:shape_y - b, 1 - c:shape_z - c]
                sign_x, sign_y, sign_z = (2.0 * a - 1.0, 2.0 * b - 1.0, 2.0 * c - 1.0)
                force_x = force_x + sign_x * corner_stress[0] + sign_y * corner_stress[5] + sign_z * corner_stress[4]
                force_y = force_y + sign_x * corner_stress[5] + sign_y * corner_stress[1] + sign_z * corner_stress[3]
                force_z = force_z + sign_x * corner_stress[4] + sign_y * corner_stress[3] + sign_z * corner_stress[2]
    return 0.25 * jnp.stack([force_x, force_y, force_z])

def model_tables(basis_rows, mode_map, weights):
    hyper_count = weights.shape[0]
    localized = jnp.dot(basis_rows, mode_map, preferred_element_type=jnp.float32).reshape(6, hyper_count, 6)
    shaped = jnp.einsum('cd,dqj->cqj', jnp.asarray(DEVIATOR), localized, precision=lax.Precision.HIGHEST)
    deviator_table = jnp.einsum('cqi,cqj->ijq', localized, shaped, precision=lax.Precision.HIGHEST).reshape(36, hyper_count)
    traced = localized[0] + localized[1] + localized[2]
    volume_table = jnp.einsum('q,qi,qj->ij', weights, traced, traced, precision=lax.Precision.HIGHEST).reshape(36)
    return (deviator_table, volume_table)

def branch_flags(pattern_ids, patterns, hyper_count):
    matches = pattern_ids[None, :] == jnp.arange(patterns.shape[0], dtype=jnp.int32)[:, None]
    packed = lax.optimization_barrier(jnp.sum(jnp.where(matches[:, None, :], patterns[:, :, None], 0), axis=0))
    spread = jnp.repeat(packed, 30, axis=0)[:hyper_count]
    offset = (jnp.arange(hyper_count, dtype=jnp.int32) % 30)[:, None]
    return jnp.bitwise_and(jnp.right_shift(spread, offset), 1).astype(jnp.float32)

def modal_coefficients(mode_map, macro_strain, history):
    mapped = jnp.dot(mode_map, macro_strain, preferred_element_type=jnp.float32)
    return (mapped + history.astype(jnp.float32)).astype(jnp.bfloat16)

def micro_response(basis_rows, coefficients, pattern_ids, patterns, deviator_table, volume_table, weights):
    hyper_count = weights.shape[0]
    columns = coefficients.shape[1]
    point_strain = jnp.dot(basis_rows, coefficients, preferred_element_type=jnp.float32).reshape(6, hyper_count, columns)
    flag_bits = branch_flags(pattern_ids, patterns, hyper_count)
    volume = point_strain[0] + point_strain[1] + point_strain[2]
    deviator = [2.0 * SHEAR_MODULUS * (point_strain[c] - volume / 3.0) for c in range(3)]
    deviator = deviator + [SHEAR_MODULUS * point_strain[c] for c in range(3, 6)]
    magnitude = jnp.sqrt(deviator[0] ** 2 + deviator[1] ** 2 + deviator[2] ** 2 + 2.0 * (deviator[3] ** 2 + deviator[4] ** 2 + deviator[5] ** 2))
    bounded = jnp.maximum(magnitude, YIELD_STRESS)
    factor = (YIELD_STRESS + HARDENING * (bounded - YIELD_STRESS)) / bounded
    secant = 1.0 + flag_bits * (factor - 1.0)
    micro_stress = jnp.stack([BULK_MODULUS * volume + secant * deviator[c] for c in range(3)] + [secant * deviator[c] for c in range(3, 6)])
    plastic_stress = jnp.einsum('chr,h->cr', micro_stress, weights, precision=lax.Precision.HIGHEST)
    tangent = BULK_MODULUS * volume_table[:, None] + 2.0 * SHEAR_MODULUS * jnp.dot(deviator_table, weights[:, None] * secant, precision=lax.Precision.HIGHEST)
    return jnp.concatenate([plastic_stress, tangent], axis=0)

def reference(motion, stiffness, point_elem, point_owner, point_pattern, history, basis, mode_map, weights, patterns):
    node_field = jnp.pad(motion, ((0, 0), (0, 1), (0, 1), (0, 1)))
    strain = element_strains(node_field)
    stress = elastic_stress(strain, stiffness.astype(jnp.float32))
    block_id = jnp.arange(POINTS, dtype=jnp.int32) // P_DEV
    row_x = block_id // N_MICRO
    col_y = block_id % N_MICRO
    plane_x = point_elem // (CY * CZ)
    plane_y = point_elem // CZ % CY
    depth_z = point_elem % CZ
    global_x = row_x * CX + plane_x
    global_y = col_y * CY + plane_y
    macro_strain = strain[:, global_x, global_y, depth_z].astype(jnp.bfloat16)
    coefficients = modal_coefficients(mode_map, macro_strain, history)
    owners = point_owner.reshape(-1, P_DEV)
    positions = jnp.arange(P_DEV, dtype=jnp.int32)
    earlier = positions[None, :] < positions[:, None]
    same_host = owners[:, None, :] == owners[:, :, None]
    position = lax.optimization_barrier(jnp.sum(jnp.where(same_host & earlier[None], 1, 0), axis=2)).astype(jnp.int32).reshape(-1)
    slot_total = CAP * N_MACRO
    slot_index = position * N_MACRO + row_x
    storage = jnp.zeros((N_MACRO, N_MICRO, slot_total, MODES), jnp.bfloat16)
    storage = storage.at[point_owner, col_y, slot_index].set(coefficients.T)
    pattern_slots = jnp.zeros((N_MACRO, N_MICRO, slot_total), jnp.int32)
    pattern_slots = pattern_slots.at[point_owner, col_y, slot_index].set(point_pattern)

    def per_host(block_items):
        basis_rows, host_coeffs, host_ids = block_items
        deviator_table, volume_table = model_tables(basis_rows, mode_map, weights)
        outcome = micro_response(basis_rows, host_coeffs.reshape(-1, MODES).T, host_ids.reshape(-1), patterns, deviator_table, volume_table, weights)
        return outcome.reshape(42, N_MICRO, slot_total)
    results = lax.map(per_host, (basis, storage, pattern_slots))
    picked = results[point_owner, :, col_y, slot_index]
    plastic_stress = picked[:, :6].T
    tangent = picked[:, 6:].T
    stress = stress.at[:, global_x, global_y, depth_z].set(plastic_stress)
    padded_stress = jnp.pad(stress, ((0, 0), (1, 0), (1, 0), (1, 0)))
    force = nodal_forces(padded_stress)
    return (force, tangent)
```

```python
import functools

import jax
import jax.numpy as jnp
from jax import lax
from jax.experimental import pallas as pl
from jax.experimental.pallas import tpu as pltpu
from jax.sharding import PartitionSpec as P

YIELD_STRESS = 1.5
HARDENING = 0.2
F32 = jnp.float32
BF16 = jnp.bfloat16
VMEM = pltpu.VMEM
ROWS = 32
UPPER = [(i, j) for i in range(6) for j in range(i, 6)]


def whole(*arrays):
    return [pl.BlockSpec(value.shape, lambda s, n=len(value.shape): (0,) * n) for value in arrays]


def iota(shape, dim):
    return lax.broadcasted_iota(jnp.int32, shape, dim)


def dot_t(left, right):
    return lax.dot_general(left, right, (((1,), (1,)), ((), ())), preferred_element_type=F32)


def pieces(value, count):
    out = []
    for _ in range(count):
        piece = value.astype(BF16)
        out.append(piece)
        value = value - piece.astype(F32)
    return out


def next_z(field):
    last = field.ndim - 1
    size = field.shape[last]
    rolled = pltpu.roll(field, size - 1, last)
    return jnp.where(iota(field.shape, last) == size - 1, 0.0, rolled)


def previous_z(field):
    last = field.ndim - 1
    rolled = pltpu.roll(field, 1, last)
    return jnp.where(iota(field.shape, last) == 0, 0.0, rolled)


def strains(here, y_up):
    grads = []
    for base, upper in zip(here, y_up):
        base_z, upper_z = next_z(base), next_z(upper)
        four = [base, upper, base_z, upper_z]
        dx = [value[1:] - value[:-1] for value in four]
        grad_x = (dx[0] + dx[1] + dx[2] + dx[3]) * 0.25
        dy, dy_z = upper - base, upper_z - base_z
        grad_y = (dy[:-1] + dy[1:] + dy_z[:-1] + dy_z[1:]) * 0.25
        dz, dz_y = base_z - base, upper_z - upper
        grad_z = (dz[:-1] + dz[1:] + dz_y[:-1] + dz_y[1:]) * 0.25
        grads.append((grad_x, grad_y, grad_z))
    return [
        grads[0][0],
        grads[1][1],
        grads[2][2],
        grads[1][2] + grads[2][1],
        grads[0][2] + grads[2][0],
        grads[0][1] + grads[1][0],
    ]


def slots_of(owner, hosts, capacity):
    points = owner.shape[1]
    chosen = iota((hosts, points), 0) == owner
    host_hot = jnp.where(chosen, 1.0, 0.0)
    before = jnp.where(iota((points, points), 0) < iota((points, points), 1), 1.0, 0.0)
    counts = jnp.dot(host_hot.astype(BF16), before.astype(BF16), preferred_element_type=F32)
    position = jnp.sum(host_hot * counts, axis=0, keepdims=True).astype(jnp.int32)
    return host_hot, position, owner * capacity + position


def dispatch_kernel(
    hosts,
    capacity,
    direct,
    motion_ref,
    stiff_ref,
    elem_ref,
    owner_ref,
    pattern_ref,
    history_ref,
    map_ref,
    payload_ref,
    *rest,
):
    size_x, size_y, size_z = motion_ref.shape[1:]
    elem, owner = elem_ref[...], owner_ref[...]
    points = elem.shape[1]
    here = [motion_ref[m] for m in range(3)]
    y_up = [pltpu.roll(field, size_y - 1, 1) for field in here]
    strain = strains(here, y_up)
    rows = (size_x - 1) * size_y
    field = jnp.concatenate([value.reshape(rows, size_z) for value in strain], axis=0)
    column = elem // size_z
    depth = elem - column * size_z
    depth_hot = jnp.where(iota((size_z, points), 0) == depth, 1.0, 0.0).astype(BF16)
    picked = jnp.dot(field.astype(BF16), depth_hot, preferred_element_type=F32)
    column_hot = iota((rows, points), 0) == column
    macro_strain = jnp.concatenate(
        [
            jnp.sum(
                jnp.where(column_hot, picked[c * rows : (c + 1) * rows], 0.0),
                axis=0,
                keepdims=True,
            )
            for c in range(6)
        ],
        axis=0,
    ).astype(BF16)
    mapped = jnp.dot(map_ref[...], macro_strain, preferred_element_type=F32)
    coefficients = (mapped + history_ref[...].astype(F32)).astype(BF16)
    host_hot, position, slot = slots_of(owner, hosts, capacity)
    slot_total = hosts * capacity
    slot_hot = jnp.where(iota((slot_total, points), 0) == slot, 1.0, 0.0).astype(BF16)
    sent = dot_t(slot_hot, coefficients).astype(BF16)
    place = position + lax.axis_index("macro") * capacity
    modes = sent.shape[1]
    place_hot = jnp.where(iota((modes, points), 0) == place, 1.0, 0.0).astype(BF16)
    ids = dot_t((host_hot * pattern_ref[...].astype(F32)).astype(BF16), place_hot)
    if direct:
        for h in range(hosts):
            payload_ref[h, :capacity, :] = sent[h * capacity : (h + 1) * capacity]
            payload_ref[h, capacity:, :] = jnp.broadcast_to(ids[h : h + 1], (16, modes)).astype(BF16)
    else:
        payload_ref[...] = sent
        rest[0][...] = ids.astype(BF16)
        rest = rest[1:]
    up_ref, down_ref = rest
    stiffness = stiff_ref[...].astype(F32)
    for i in range(size_x):
        for m in range(3):
            up_ref[m, i : i + 1, :] = motion_ref[m, i, size_y - 1 : size_y, :]
            down_ref[m, i : i + 1, :] = motion_ref[m, i, 0:1, :]
        up_ref[3, i : i + 1, :] = stiffness[i, size_y - 1 : size_y, :]


def table_kernel(basis_ref, map_ref, weights_ref, patterns_ref, table_ref, const_ref, column_ref, bits_ref):
    hyper = basis_ref.shape[1]
    lanes = 128
    modes_map = map_ref[...]
    sums = jnp.zeros((48, lanes), F32)
    patterns = patterns_ref[...]
    parts = [((patterns >> (8 * k)) & 255).astype(F32).astype(BF16) for k in range(4)]
    words = patterns.shape[1]
    for b in range(hyper // lanes):
        part = pl.ds(b * lanes, lanes)
        local = [dot_t(modes_map, basis_ref[c, part, :]) for c in range(6)]
        trace = local[0] + local[1] + local[2]
        third = trace / 3.0
        shaped = [local[c] - third for c in range(3)] + [0.5 * local[c] for c in range(3, 6)]
        weight = weights_ref[b : b + 1, :]
        weighted_trace = weight * trace
        blocks = []
        for i in range(6):
            entry = local[0][i : i + 1] * shaped[0]
            for c in range(1, 6):
                entry = entry + local[c][i : i + 1] * shaped[c]
            entry = entry * weight
            blocks.append(entry)
            sums_i = entry + trace[i : i + 1] * weighted_trace
            sums = sums + jnp.concatenate(
                [jnp.zeros((8 * i, lanes), F32)] * (i > 0)
                + [sums_i]
                + [jnp.zeros((8 * (5 - i), lanes), F32)] * (i < 5),
                axis=0,
            )
        block = jnp.concatenate(blocks, axis=0)
        high, low = pieces(block, 2)
        table_ref[0:48, part] = high
        table_ref[48:96, part] = low
        square = (lanes, lanes)
        diagonal = jnp.where(iota(square, 0) == iota(square, 1), weight, 0.0)
        column_ref[part, :] = jnp.broadcast_to(jnp.sum(diagonal, axis=1, keepdims=True), square)
        start = 30 * iota((lanes, words), 1)
        index = iota((lanes, words), 0) + b * lanes
        word_hot = jnp.where((index >= start) & (index < start + 30), 1.0, 0.0).astype(BF16)
        bytes_of = [dot_t(word_hot, part_k) for part_k in parts]
        count = patterns.shape[0]
        row = iota((lanes, count), 0) + b * lanes
        offset = row - 30 * ((row * 2185) >> 16)
        value = jnp.where(
            offset < 16,
            jnp.where(offset < 8, bytes_of[0], bytes_of[1]),
            jnp.where(offset < 24, bytes_of[2], bytes_of[3]),
        ).astype(jnp.int32)
        bits_ref[part, :] = ((value >> (offset & 7)) & 1).astype(F32).astype(BF16)
    const_ref[...] = jnp.broadcast_to(jnp.sum(sums, axis=1, keepdims=True), const_ref.shape)


def micro_kernel(
    packed,
    capacity,
    received_ref,
    basis_ref,
    bits_ref,
    column_ref,
    table_ref,
    const_ref,
    answer_ref,
    state_ref,
    hot_ref,
    strain_ref,
    high_ref,
    low_ref,
    stress_ref,
    tangent_ref,
    result_ref,
):
    step = pl.program_id(0)
    hosts = received_ref.shape[0]
    slots = hosts * capacity
    block = basis_ref.shape[1]

    @pl.when(step == 0)
    def _():
        ids = jnp.zeros((1, slots), F32)
        for h in range(hosts):
            state_ref[h * capacity : (h + 1) * capacity, :] = received_ref[h, :capacity, :]
            ids = ids + received_ref[h, capacity:, :].astype(F32)[0:1]
        shape = hot_ref.shape
        hot_ref[...] = jnp.where(iota(shape, 0) == ids.astype(jnp.int32), 1.0, 0.0).astype(BF16)
        stress_ref[...] = jnp.zeros_like(stress_ref)
        tangent_ref[...] = jnp.zeros_like(tangent_ref)

    state = state_ref[...]
    rows = basis_ref[...].reshape(6 * block, basis_ref.shape[2])
    strain_ref[...] = dot_t(rows, state).reshape(6, block, slots)
    flags = jnp.dot(bits_ref[...], hot_ref[...], preferred_element_type=F32)
    strip = 16
    sums = [jnp.zeros((8, slots), F32)] * 7
    for r in range(0, block, strip):
        part = pl.ds(r, strip)
        e = [strain_ref[c, part, :] for c in range(6)]
        volume = e[0] + e[1] + e[2]
        third = volume * (1.0 / 3.0)
        d = [e[c] - third for c in range(3)]
        normal = d[0] * d[0] + d[1] * d[1] + d[2] * d[2]
        shear = e[3] * e[3] + e[4] * e[4] + e[5] * e[5]
        square = jnp.maximum(normal + 0.5 * shear, YIELD_STRESS * YIELD_STRESS)
        factor = (YIELD_STRESS * (1.0 - HARDENING)) * lax.rsqrt(square) + (HARDENING - 1.0)
        change = flags[r : r + strip] * factor
        high = change.astype(BF16)
        high_ref[part, :] = high
        low_ref[part, :] = (change - high.astype(F32)).astype(BF16)
        column = column_ref[part, :]
        weight = jnp.concatenate([column] * (slots // column.shape[1]), axis=1)
        scaled = weight + weight * change
        terms = [scaled * d[c] for c in range(3)] + [scaled * e[c] for c in range(3, 6)]
        terms.append(weight * volume)
        for n in range(7):
            sums[n] = sums[n] + (terms[n][:8] + terms[n][8:])
    for n in range(7):
        stress_ref[n] += sums[n]
    table = table_ref[...]
    first = jnp.dot(table, high_ref[...], preferred_element_type=F32)
    second = jnp.dot(table[:48], low_ref[...], preferred_element_type=F32)
    tangent_ref[...] += first[:48] + (first[48:] + second)

    @pl.when(step == pl.num_programs(0) - 1)
    def _():
        volume = jnp.sum(stress_ref[6], axis=0, keepdims=True)
        for c in range(6):
            total = jnp.sum(stress_ref[c], axis=0, keepdims=True)
            result_ref[c : c + 1, :] = total + volume if c < 3 else 0.5 * total
        const = const_ref[...]
        const = jnp.concatenate([const] * (slots // const.shape[1]), axis=1)
        tangent = tangent_ref[...] + const
        at = 6
        for i in range(6):
            result_ref[at : at + 6 - i, :] = tangent[8 * i + i : 8 * i + 6]
            at += 6 - i
        result_ref[at:, :] = jnp.zeros((ROWS - at, slots), F32)
        if packed:
            group_of = iota((8, 128), 1) // capacity
            for h in range(hosts):
                chunk = jnp.zeros((8, 128), F32)
                tile, place = divmod(h * capacity, 128)
                for g in range(4):
                    piece = result_ref[8 * g : 8 * g + 8, tile * 128 : (tile + 1) * 128]
                    shift = (g * capacity - place) % 128
                    if shift:
                        piece = pltpu.roll(piece, shift, 1)
                    chunk = jnp.where(group_of == g, piece, chunk)
                answer_ref[h] = chunk
        else:
            answer_ref[...] = result_ref[...]


def face_kernel(motion_ref, stiff_ref, low_ref, high_ref, up_ref, down_ref):
    size_x, size_y, _ = motion_ref.shape[1:]
    last = size_x - 1
    up_ref[...] = jnp.zeros_like(up_ref)
    down_ref[...] = jnp.zeros_like(down_ref)
    for m in range(3):
        up_ref[m, :size_y, :] = motion_ref[m, last]
        up_ref[m, size_y : size_y + 1, :] = low_ref[m, last : last + 1, :]
        up_ref[m, size_y + 1 : size_y + 2, :] = high_ref[m, last : last + 1, :]
        down_ref[m, :size_y, :] = motion_ref[m, 0]
        down_ref[m, size_y : size_y + 1, :] = low_ref[m, 0:1, :]
        down_ref[m, size_y + 1 : size_y + 2, :] = high_ref[m, 0:1, :]
    up_ref[3, :size_y, :] = stiff_ref[last].astype(F32)
    up_ref[3, size_y : size_y + 1, :] = low_ref[3, last : last + 1, :]


def assemble(stress):
    lower, upper = [], []
    for here, low in stress:
        here_z, low_z = previous_z(here), previous_z(low)
        lower.append((here, low, here_z, low_z))
    def at(c, sign_x, sign_y, sign_z):
        here, low, here_z, low_z = lower[c]
        if sign_z:
            near, far = here_z - here, low_z - low
        else:
            near, far = here_z + here, low_z + low
        both = far - near if sign_y else far + near
        return both[:-1] - both[1:] if sign_x else both[:-1] + both[1:]
    force = [
        at(0, 1, 0, 0) + at(5, 0, 1, 0) + at(4, 0, 0, 1),
        at(5, 1, 0, 0) + at(1, 0, 1, 0) + at(3, 0, 0, 1),
        at(4, 1, 0, 0) + at(3, 0, 1, 0) + at(2, 0, 0, 1),
    ]
    return [0.25 * value for value in force]


def elastic_kernel(
    motion_ref,
    stiff_ref,
    elem_ref,
    y_low_ref,
    y_high_ref,
    x_low_ref,
    x_high_ref,
    force_ref,
    node_ref,
    stiff_wide_ref,
    stress_ref,
):
    size_x, size_y, size_z = motion_ref.shape[1:]
    wide = node_ref.shape[2]
    node_ref[...] = jnp.zeros_like(node_ref)
    stiff_wide_ref[...] = jnp.zeros_like(stiff_wide_ref)
    stiffness = stiff_ref[...].astype(F32)
    for m in range(3):
        for i in range(size_x):
            node_ref[m, i + 1, 1 : size_y + 1, :] = motion_ref[m, i]
            node_ref[m, i + 1, 0:1, :] = y_low_ref[m, i : i + 1, :]
            node_ref[m, i + 1, size_y + 1 : size_y + 2, :] = y_high_ref[m, i : i + 1, :]
        for at, ref in ((0, x_low_ref), (size_x + 1, x_high_ref)):
            node_ref[m, at, 1 : size_y + 1, :] = ref[m, :size_y, :]
            node_ref[m, at, 0:1, :] = ref[m, size_y : size_y + 1, :]
            node_ref[m, at, size_y + 1 : size_y + 2, :] = ref[m, size_y + 1 : size_y + 2, :]
    for i in range(size_x):
        stiff_wide_ref[i + 1, 1 : size_y + 1, :] = stiffness[i]
        stiff_wide_ref[i + 1, 0:1, :] = y_low_ref[3, i : i + 1, :]
    stiff_wide_ref[0, 1 : size_y + 1, :] = x_low_ref[3, :size_y, :]
    stiff_wide_ref[0, 0:1, :] = x_low_ref[3, size_y : size_y + 1, :]
    here = [node_ref[m] for m in range(3)]
    y_up = [pltpu.roll(value, wide - 1, 1) for value in here]
    strain = strains(here, y_up)
    stiff = stiff_wide_ref[...]
    volume = strain[0] + strain[1] + strain[2]
    rest = volume - volume * (1.0 / 3.0)
    elem = elem_ref[...]
    points = elem.shape[1]
    column = elem // size_z
    depth = elem - column * size_z
    depth_hot = jnp.where(iota((size_z, points), 0) == depth, 1.0, 0.0).astype(BF16)
    column_hot = jnp.where(iota((size_x * size_y, points), 0) == column, 1.0, 0.0).astype(BF16)
    listed = dot_t(column_hot, depth_hot)
    for i in range(size_x):
        keep = 1.0 - listed[i * size_y : (i + 1) * size_y]
        stiff_wide_ref[i + 1, 1 : size_y + 1, :] = stiffness[i] * keep
    stiff = stiff_wide_ref[...]
    for c in range(6):
        value = stiff * (rest + strain[c]) if c < 3 else stiff * (0.5 * strain[c])
        stress_ref[c] = value
    pairs = [
        (stress_ref[c, :, 1 : size_y + 1, :], stress_ref[c, :, 0:size_y, :]) for c in range(6)
    ]
    force = assemble(pairs)
    for m in range(3):
        force_ref[m] = force[m]


def final_kernel(
    packed,
    hosts,
    capacity,
    answer_ref,
    elem_ref,
    owner_ref,
    elastic_ref,
    force_ref,
    tangent_ref,
    result_ref,
):
    size_x, size_y, size_z = elastic_ref.shape[1:]
    elem, owner = elem_ref[...], owner_ref[...]
    points = elem.shape[1]
    slot_total = hosts * capacity
    _, _, slot = slots_of(owner, hosts, capacity)
    if packed:
        group_of = iota((8, 128), 1) // capacity
        per_tile = 128 // capacity
        groups = []
        for g in range(4):
            tiles = []
            for t in range(hosts // per_tile):
                tile = jnp.zeros((8, 128), F32)
                for n in range(per_tile):
                    piece = answer_ref[t * per_tile + n]
                    shift = ((n - g) * capacity) % 128
                    if shift:
                        piece = pltpu.roll(piece, shift, 1)
                    tile = jnp.where(group_of == n, piece, tile)
                tiles.append(tile)
            groups.append(jnp.concatenate(tiles, axis=1))
        answer = jnp.concatenate(groups, axis=0)
    else:
        answer = answer_ref[...]
    slot_hot = jnp.where(iota((slot_total, points), 0) == slot, 1.0, 0.0).astype(BF16)
    parts = jnp.concatenate(pieces(answer, 3), axis=0)
    chosen = jnp.dot(parts, slot_hot, preferred_element_type=F32)
    result = chosen[:ROWS] + (chosen[ROWS : 2 * ROWS] + chosen[2 * ROWS :])
    result_ref[...] = result
    for i in range(6):
        for j in range(6):
            at = 6 + UPPER.index((min(i, j), max(i, j)))
            tangent_ref[6 * i + j : 6 * i + j + 1, :] = result_ref[at : at + 1, :]
    column = elem // size_z
    depth = elem - column * size_z
    columns = size_x * size_y
    depth_hot = jnp.where(iota((size_z, points), 0) == depth, 1.0, 0.0).astype(BF16)
    column_hot = iota((columns, points), 0) == column
    stress = []
    for c in range(6):
        placed = jnp.where(column_hot, result[c : c + 1], 0.0)
        high, low = pieces(placed, 2)
        field = dot_t(high, depth_hot) + dot_t(low, depth_hot)
        field = field.reshape(size_x, size_y, size_z)
        field = jnp.concatenate([jnp.zeros((1, size_y, size_z), F32), field], axis=0)
        low_y = pltpu.roll(field, 1, 1)
        low_y = jnp.where(iota(low_y.shape, 1) == 0, 0.0, low_y)
        stress.append((field, low_y))
    force = assemble(stress)
    for m in range(3):
        force_ref[m] = elastic_ref[m] + force[m]


def shape_of(shape, dtype=F32):
    return jax.ShapeDtypeStruct(shape, dtype)


def cost(flops, size):
    return pl.CostEstimate(flops=flops, bytes_accessed=size, transcendentals=0)


PARAMS = pltpu.CompilerParams(vmem_limit_bytes=40 * 2**20)


def call(kernel, name, out_shape, args, scratch=(), flops=10**8):
    return pl.pallas_call(
        kernel,
        grid=(1,),
        out_shape=out_shape,
        in_specs=whole(*args),
        out_specs=whole(*out_shape),
        scratch_shapes=scratch,
        compiler_params=PARAMS,
        cost_estimate=cost(flops, 2**20),
        name=name,
    )(*args)


def on_device(
    motion,
    stiffness,
    point_elem,
    point_owner,
    point_pattern,
    history,
    basis,
    mode_map,
    weights,
    patterns,
):
    size_x, size_y, size_z = motion.shape[1:]
    points = point_elem.shape[0]
    hosts = lax.axis_size("macro")
    sides = lax.axis_size("micro")
    capacity = 2 * points // hosts
    slots = capacity * hosts
    modes = mode_map.shape[0]
    hyper = weights.shape[0]
    lanes = 128
    direct = capacity % 16 == 0
    packed = capacity * 4 == lanes and slots % lanes == 0
    elem = point_elem.reshape(1, points)
    owner = point_owner.reshape(1, points)
    pattern = point_pattern.reshape(1, points)

    sent = (
        [shape_of((hosts, capacity + 16, modes), BF16)]
        if direct
        else [shape_of((slots, modes), BF16), shape_of((hosts, modes), BF16)]
    )
    *payload, y_up, y_down = call(
        functools.partial(dispatch_kernel, hosts, capacity, direct),
        "dispatch",
        sent + [shape_of((4, size_x, size_z)), shape_of((3, size_x, size_z))],
        (motion, stiffness, elem, owner, pattern, history, mode_map),
    )

    if direct:
        received = lax.all_to_all(payload[0], "macro", 0, 0, tiled=True)
        groups, group = hosts, capacity
    else:
        joined = jnp.concatenate(
            [payload[0].reshape(hosts, capacity, modes), payload[1][:, None, :]], axis=1
        )
        joined = lax.all_to_all(joined, "macro", 0, 0, tiled=True)
        ids = jnp.sum(joined[:, capacity, :].astype(F32), axis=0).astype(BF16)
        received = jnp.concatenate(
            [
                joined[:, :capacity, :].reshape(1, slots, modes),
                jnp.broadcast_to(ids[None, None, :], (1, 16, modes)),
            ],
            axis=1,
        )
        groups, group = 1, slots

    forward = [(i, i + 1) for i in range(sides - 1)]
    backward = [(i + 1, i) for i in range(sides - 1)]
    y_low = lax.ppermute(y_up, "micro", forward)
    y_high = lax.ppermute(y_down, "micro", backward)

    rows = basis.reshape(6, hyper, modes)
    map_rows = jnp.pad(mode_map.T, ((0, 2), (0, 0)))
    table, const, column, bits = call(
        table_kernel,
        "tables",
        [
            shape_of((96, hyper), BF16),
            shape_of((48, lanes)),
            shape_of((hyper, lanes)),
            shape_of((hyper, patterns.shape[0]), BF16),
        ],
        (rows, map_rows, weights.reshape(hyper // lanes, lanes), patterns),
    )

    x_up, x_down = call(
        face_kernel,
        "faces",
        [shape_of((4, 16, size_z)), shape_of((3, 16, size_z))],
        (motion, stiffness, y_low, y_high),
    )

    steps = 4
    block = hyper // steps
    answer = pl.pallas_call(
        functools.partial(micro_kernel, packed, group),
        grid=(steps,),
        out_shape=shape_of((hosts, 8, lanes)) if packed else shape_of((ROWS, slots)),
        in_specs=[
            pl.BlockSpec((groups, group + 16, modes), lambda s: (0, 0, 0)),
            pl.BlockSpec((6, block, modes), lambda s: (0, s, 0)),
            pl.BlockSpec((block, patterns.shape[0]), lambda s: (s, 0)),
            pl.BlockSpec((block, lanes), lambda s: (s, 0)),
            pl.BlockSpec((96, block), lambda s: (0, s)),
            pl.BlockSpec((48, lanes), lambda s: (0, 0)),
        ],
        out_specs=pl.BlockSpec((hosts, 8, lanes), lambda s: (0, 0, 0))
        if packed
        else pl.BlockSpec((ROWS, slots), lambda s: (0, 0)),
        scratch_shapes=[
            VMEM((slots, modes), BF16),
            VMEM((patterns.shape[0], slots), BF16),
            VMEM((6, block, slots), F32),
            VMEM((block, slots), BF16),
            VMEM((block, slots), BF16),
            VMEM((7, 8, slots), F32),
            VMEM((48, slots), F32),
            VMEM((ROWS, slots), F32),
        ],
        compiler_params=PARAMS,
        cost_estimate=cost(2 * 10**9, 4 * 2**20),
        name="micro_response",
    )(received, rows, bits, column, table, const)

    if packed:
        answered = lax.all_to_all(answer, "macro", 0, 0, tiled=True)
    else:
        answered = answer.reshape(ROWS, hosts, capacity).transpose(1, 0, 2)
        answered = lax.all_to_all(answered, "macro", 0, 0, tiled=True)
        answered = answered.transpose(1, 0, 2).reshape(ROWS, slots)

    forward = [(i, i + 1) for i in range(hosts - 1)]
    backward = [(i + 1, i) for i in range(hosts - 1)]
    x_low = lax.ppermute(x_up, "macro", forward)
    x_high = lax.ppermute(x_down, "macro", backward)

    (elastic,) = call(
        elastic_kernel,
        "elastic_forces",
        [shape_of(motion.shape)],
        (motion, stiffness, elem, y_low, y_high, x_low, x_high),
        [
            VMEM((3, size_x + 2, 16, size_z), F32),
            VMEM((size_x + 1, 16, size_z), F32),
            VMEM((6, size_x + 1, 16, size_z), F32),
        ],
    )

    force, tangent = call(
        functools.partial(final_kernel, packed, hosts, capacity),
        "final_forces",
        [shape_of(motion.shape), shape_of((36, points))],
        (answered, elem, owner, elastic),
        [VMEM((ROWS, points), F32)],
    )
    return (force, tangent)


def solution(mesh):
    return jax.shard_map(
        on_device,
        mesh=mesh,
        in_specs=(
            P(None, "macro", "micro", None),
            P("macro", "micro", None),
            P(("macro", "micro")),
            P(("macro", "micro")),
            P(("macro", "micro")),
            P(None, ("macro", "micro")),
            P("macro", None, None),
            P(),
            P(),
            P(),
        ),
        out_specs=(P(None, "macro", "micro", None), P(None, ("macro", "micro"))),
        check_vma=False,
    )
```

```python
import functools

import jax
import jax.numpy as jnp
from jax import lax
from jax.experimental import pallas as pl
from jax.experimental.pallas import tpu as pltpu
from jax.sharding import PartitionSpec as P

YIELD_STRESS = 1.5
HARDENING = 0.2
F32 = jnp.float32
BF16 = jnp.bfloat16
VMEM = pltpu.VMEM
ROWS = 32
UPPER = [(i, j) for i in range(6) for j in range(i, 6)]


def whole(*arrays):
    return [pl.BlockSpec(value.shape, lambda s, n=len(value.shape): (0,) * n) for value in arrays]


def in_hbm(value):
    return pltpu.with_memory_space_constraint(value, pltpu.HBM)


def iota(shape, dim):
    return lax.broadcasted_iota(jnp.int32, shape, dim)


def dot_t(left, right):
    return lax.dot_general(left, right, (((1,), (1,)), ((), ())), preferred_element_type=F32)


def pieces(value, count):
    out = []
    for _ in range(count):
        piece = value.astype(BF16)
        out.append(piece)
        value = value - piece.astype(F32)
    return out


def next_z(field):
    last = field.ndim - 1
    size = field.shape[last]
    rolled = pltpu.roll(field, size - 1, last)
    return jnp.where(iota(field.shape, last) == size - 1, 0.0, rolled)


def previous_z(field):
    last = field.ndim - 1
    rolled = pltpu.roll(field, 1, last)
    return jnp.where(iota(field.shape, last) == 0, 0.0, rolled)


def corners(field):
    y_up = pltpu.roll(field, field.shape[1] - 1, 1)
    return [field, y_up, next_z(field), next_z(y_up)]


def strains(lower, upper):
    grads = []
    for low, high in zip(lower, upper):
        dx = [b - a for a, b in zip(low, high)]
        grad_x = (dx[0] + dx[1] + dx[2] + dx[3]) * 0.25
        dy = [value[1] - value[0] for value in (low, high)]
        dy_z = [value[3] - value[2] for value in (low, high)]
        grad_y = (dy[0] + dy[1] + dy_z[0] + dy_z[1]) * 0.25
        dz = [value[2] - value[0] for value in (low, high)]
        dz_y = [value[3] - value[1] for value in (low, high)]
        grad_z = (dz[0] + dz[1] + dz_y[0] + dz_y[1]) * 0.25
        grads.append((grad_x, grad_y, grad_z))
    return [
        grads[0][0],
        grads[1][1],
        grads[2][2],
        grads[1][2] + grads[2][1],
        grads[0][2] + grads[2][0],
        grads[0][1] + grads[1][0],
    ]


def block_strains(fields):
    nodes = [corners(field) for field in fields]
    return strains(
        [[value[:-1] for value in four] for four in nodes],
        [[value[1:] for value in four] for four in nodes],
    )


def elastic_of(strain, stiffness):
    volume = strain[0] + strain[1] + strain[2]
    rest = volume - volume * (1.0 / 3.0)
    normal = [stiffness * (rest + strain[c]) for c in range(3)]
    return normal + [stiffness * (0.5 * strain[c]) for c in range(3, 6)]


def slots_of(owner, hosts, capacity):
    points = owner.shape[1]
    chosen = iota((hosts, points), 0) == owner
    host_hot = jnp.where(chosen, 1.0, 0.0)
    before = jnp.where(iota((points, points), 0) < iota((points, points), 1), 1.0, 0.0)
    counts = jnp.dot(host_hot.astype(BF16), before.astype(BF16), preferred_element_type=F32)
    position = jnp.sum(host_hot * counts, axis=0, keepdims=True).astype(jnp.int32)
    return host_hot, position, owner * capacity + position


def dispatch_kernel(
    hosts,
    capacity,
    direct,
    motion_ref,
    stiff_ref,
    elem_ref,
    owner_ref,
    pattern_ref,
    history_ref,
    map_ref,
    payload_ref,
    *rest,
):
    size_x, size_y, size_z = motion_ref.shape[1:]
    elem, owner = elem_ref[...], owner_ref[...]
    points = elem.shape[1]
    strain = block_strains([motion_ref[m] for m in range(3)])
    rows = (size_x - 1) * size_y
    field = jnp.concatenate([value.reshape(rows, size_z) for value in strain], axis=0)
    column = elem // size_z
    depth = elem - column * size_z
    depth_hot = jnp.where(iota((size_z, points), 0) == depth, 1.0, 0.0).astype(BF16)
    picked = jnp.dot(field.astype(BF16), depth_hot, preferred_element_type=F32)
    column_hot = iota((rows, points), 0) == column
    macro_strain = jnp.concatenate(
        [
            jnp.sum(
                jnp.where(column_hot, picked[c * rows : (c + 1) * rows], 0.0),
                axis=0,
                keepdims=True,
            )
            for c in range(6)
        ],
        axis=0,
    ).astype(BF16)
    mapped = lax.dot_general(
        map_ref[...], macro_strain, (((0,), (0,)), ((), ())), preferred_element_type=F32
    )
    coefficients = (mapped + history_ref[...].astype(F32)).astype(BF16)
    host_hot, position, slot = slots_of(owner, hosts, capacity)
    slot_total = hosts * capacity
    slot_hot = jnp.where(iota((slot_total, points), 0) == slot, 1.0, 0.0).astype(BF16)
    sent = dot_t(slot_hot, coefficients).astype(BF16)
    place = position + lax.axis_index("macro") * capacity
    modes = sent.shape[1]
    half = modes // 2
    place_hot = jnp.where(iota((modes, points), 0) == place, 1.0, 0.0).astype(BF16)
    ids = dot_t((host_hot * pattern_ref[...].astype(F32)).astype(BF16), place_hot)
    if direct:
        for h in range(hosts):
            mine = sent[h * capacity : (h + 1) * capacity]
            payload_ref[h, :capacity, :] = mine[:, :half]
            payload_ref[h, capacity : 2 * capacity, :] = mine[:, half:]
            row = iota((8, half), 0)
            low, high = ids[h : h + 1, :half], ids[h : h + 1, half:]
            tile = jnp.where(row == 0, low, jnp.where(row == 1, high, 0.0))
            payload_ref[h, 2 * capacity :, :] = tile.astype(BF16)
    else:
        payload_ref[...] = sent
        rest[0][...] = ids.astype(BF16)
        rest = rest[1:]
    first_ref, second_ref, face_ref = rest
    stiffness = stiff_ref[...].astype(F32)
    even = lax.rem(lax.axis_index("micro"), 2) == 0
    for i in range(size_x):
        for m in range(4):
            if m < 3:
                up, down = motion_ref[m, i, size_y - 1 : size_y, :], motion_ref[m, i, 0:1, :]
            else:
                up = down = stiffness[i, size_y - 1 : size_y, :]
            first_ref[m, i : i + 1, :] = jnp.where(even, up, down)
            second_ref[m, i : i + 1, :] = jnp.where(even, down, up)
    for m in range(3):
        face_ref[m] = motion_ref[m, size_x - 1]
        face_ref[4 + m] = motion_ref[m, 0]
    face_ref[3] = stiffness[size_x - 1]
    face_ref[7] = jnp.zeros_like(face_ref[7])


def table_kernel(
    map_ref,
    weights_ref,
    patterns_ref,
    basis_ref,
    table_ref,
    const_ref,
    column_ref,
    bits_ref,
    blocks_ref,
    sems,
):
    hyper = basis_ref.shape[1]
    lanes = 128
    count = hyper // lanes
    copies = [
        pltpu.make_async_copy(
            basis_ref.at[:, pl.ds(b * lanes, lanes), :], blocks_ref.at[b], sems.at[b]
        )
        for b in range(count)
    ]
    for copy in copies:
        copy.start()
    modes_map = map_ref[...]
    modes_map = jnp.concatenate(
        [modes_map.astype(F32), jnp.zeros((2, modes_map.shape[1]), F32)], axis=0
    ).astype(BF16)
    sums = jnp.zeros((48, lanes), F32)
    patterns = patterns_ref[...]
    parts = [((patterns >> (8 * k)) & 255).astype(F32).astype(BF16) for k in range(4)]
    words, total = patterns.shape
    for b in range(count):
        part = pl.ds(b * lanes, lanes)
        weight = weights_ref[b : b + 1, :]
        square = (lanes, lanes)
        diagonal = jnp.where(iota(square, 0) == iota(square, 1), weight, 0.0)
        column_ref[part, :] = jnp.broadcast_to(jnp.sum(diagonal, axis=1, keepdims=True), square)
        start = 30 * iota((lanes, words), 1)
        index = iota((lanes, words), 0) + b * lanes
        word_hot = jnp.where((index >= start) & (index < start + 30), 1.0, 0.0).astype(BF16)
        bytes_of = [
            jnp.dot(word_hot, part_k, preferred_element_type=F32) for part_k in parts
        ]
        row = iota((lanes, total), 0) + b * lanes
        offset = row - 30 * ((row * 2185) >> 16)
        value = jnp.where(
            offset < 16,
            jnp.where(offset < 8, bytes_of[0], bytes_of[1]),
            jnp.where(offset < 24, bytes_of[2], bytes_of[3]),
        ).astype(jnp.int32)
        bits_ref[part, :] = ((value >> (offset & 7)) & 1).astype(F32).astype(BF16)
    for b in range(count):
        part = pl.ds(b * lanes, lanes)
        copies[b].wait()
        local = [dot_t(modes_map, blocks_ref[b, c]) for c in range(6)]
        trace = local[0] + local[1] + local[2]
        third = trace / 3.0
        shaped = [local[c] - third for c in range(3)] + [0.5 * local[c] for c in range(3, 6)]
        weight = weights_ref[b : b + 1, :]
        weighted_trace = weight * trace
        blocks, adds = [], []
        for i in range(6):
            entry = local[0][i : i + 1] * shaped[0]
            for c in range(1, 6):
                entry = entry + local[c][i : i + 1] * shaped[c]
            entry = entry * weight
            blocks.append(entry)
            adds.append(entry + trace[i : i + 1] * weighted_trace)
        sums = sums + jnp.concatenate(adds, axis=0)
        high, low = pieces(jnp.concatenate(blocks, axis=0), 2)
        table_ref[0:48, part] = high
        table_ref[48:96, part] = low
    const_ref[...] = jnp.broadcast_to(jnp.sum(sums, axis=1, keepdims=True), const_ref.shape)


def sides_of(first_ref, second_ref, m, at):
    even = lax.rem(lax.axis_index("micro"), 2) == 0
    first, second = first_ref[m, at : at + 1, :], second_ref[m, at : at + 1, :]
    return jnp.where(even, second, first), jnp.where(even, first, second)


def micro_kernel(
    packed,
    hosts,
    capacity,
    received_ref,
    first_ref,
    second_ref,
    face_ref,
    const_ref,
    basis_ref,
    bits_ref,
    column_ref,
    table_ref,
    answer_ref,
    *rest,
):
    if packed:
        faces_ref = None
    else:
        faces_ref, *rest = rest
    (
        state_ref,
        hot_ref,
        basis_buf,
        bits_buf,
        column_buf,
        table_buf,
        even_ref,
        odd_ref,
        high_ref,
        low_ref,
        stress_ref,
        tangent_ref,
        result_ref,
        sems,
    ) = rest
    groups = received_ref.shape[0]
    slots = groups * capacity
    count, _, block, modes = basis_buf.shape
    half = modes // 2

    def basis_copy(n):
        return pltpu.make_async_copy(
            basis_ref.at[:, pl.ds(n * block, block), :], basis_buf.at[n], sems.at[n]
        )

    others = [
        pltpu.make_async_copy(bits_ref, bits_buf, sems.at[count]),
        pltpu.make_async_copy(column_ref, column_buf, sems.at[count + 1]),
        pltpu.make_async_copy(table_ref, table_buf, sems.at[count + 2]),
    ]
    basis_copy(0).start()
    for copy in others:
        copy.start()
    for n in range(1, count):
        basis_copy(n).start()

    ids = jnp.zeros((8, half), F32)
    for h in range(groups):
        own = pl.ds(h * capacity, capacity)
        state_ref[own, :half] = received_ref[h, :capacity, :]
        state_ref[own, half:] = received_ref[h, capacity : 2 * capacity, :]
        ids = ids + received_ref[h, 2 * capacity :, :].astype(F32)
    ids = jnp.concatenate([ids[0:1], ids[1:2]], axis=1).astype(jnp.int32)
    hot_ref[...] = jnp.where(iota(hot_ref.shape, 0) == ids, 1.0, 0.0).astype(BF16)
    stress_ref[...] = jnp.zeros_like(stress_ref)
    tangent_ref[...] = jnp.zeros_like(tangent_ref)

    def rows_of(n, target):
        rows = basis_buf[n].reshape(6 * block, modes)
        target[...] = dot_t(rows, state_ref[...]).reshape(6, block, slots)

    def respond(n, strain_ref):
        part = pl.ds(pl.multiple_of(n * block, block), block)
        flags = jnp.dot(bits_buf[part, :], hot_ref[...], preferred_element_type=F32)
        strip = 16
        sums = [jnp.zeros((8, slots), F32)] * 7
        for r in range(0, block, strip):
            at = pl.ds(r, strip)
            e = [strain_ref[c, at, :] for c in range(6)]
            volume = e[0] + e[1] + e[2]
            third = volume * (1.0 / 3.0)
            d = [e[c] - third for c in range(3)]
            normal = d[0] * d[0] + d[1] * d[1] + d[2] * d[2]
            shear = e[3] * e[3] + e[4] * e[4] + e[5] * e[5]
            square = jnp.maximum(normal + 0.5 * shear, YIELD_STRESS * YIELD_STRESS)
            factor = (YIELD_STRESS * (1.0 - HARDENING)) * lax.rsqrt(square) + (HARDENING - 1.0)
            change = flags[r : r + strip] * factor
            high = change.astype(BF16)
            high_ref[at, :] = high
            low_ref[at, :] = (change - high.astype(F32)).astype(BF16)
            column = column_buf[pl.ds(pl.multiple_of(n * block, block) + r, strip), :]
            weight = jnp.concatenate([column] * (slots // column.shape[1]), axis=1)
            scaled = weight + weight * change
            terms = [scaled * d[c] for c in range(3)] + [scaled * e[c] for c in range(3, 6)]
            terms.append(weight * volume)
            for k in range(7):
                sums[k] = sums[k] + (terms[k][:8] + terms[k][8:])
        for k in range(7):
            stress_ref[k] += sums[k]
        table = table_buf[:, part]
        one = jnp.dot(table, high_ref[...], preferred_element_type=F32)
        two = jnp.dot(table[:48], low_ref[...], preferred_element_type=F32)
        tangent_ref[...] += one[:48] + (one[48:] + two)

    basis_copy(0).wait()
    rows_of(0, even_ref)
    for copy in others:
        copy.wait()

    def pair(i, carry):
        n = 2 * i
        basis_copy(n + 1).wait()
        rows_of(n + 1, odd_ref)
        respond(n, even_ref)

        @pl.when(n + 2 < count)
        def _():
            basis_copy(n + 2).wait()

        rows_of(jnp.minimum(n + 2, count - 1), even_ref)
        respond(n + 1, odd_ref)
        return carry

    lax.fori_loop(0, count // 2, pair, 0)

    volume = jnp.sum(stress_ref[6], axis=0, keepdims=True)
    for c in range(6):
        total = jnp.sum(stress_ref[c], axis=0, keepdims=True)
        result_ref[c : c + 1, :] = total + volume if c < 3 else 0.5 * total
    const = const_ref[...]
    const = jnp.concatenate([const] * (slots // const.shape[1]), axis=1)
    tangent = tangent_ref[...] + const
    at = 6
    for i in range(6):
        result_ref[at : at + 6 - i, :] = tangent[8 * i + i : 8 * i + 6]
        at += 6 - i
    result_ref[at:, :] = jnp.zeros((ROWS - at, slots), F32)

    last = first_ref.shape[1] - 1

    def faces(write):
        for m in range(4):
            write(0, 8 * m, 8, face_ref[m])
            write(1, 8 * m, 8, face_ref[4 + m])
            up = sides_of(first_ref, second_ref, m, last)
            down = sides_of(first_ref, second_ref, m, 0)
            for n in range(2):
                write(0, 32 + 2 * m + n, 1, up[n])
                write(1, 32 + 2 * m + n, 1, down[n])

    if packed:
        here = lax.axis_index("macro")
        group_of = iota((8, 128), 1) // capacity
        for h in range(hosts):
            chunk = jnp.zeros((8, 128), F32)
            tile, place = divmod(h * capacity, 128)
            for g in range(4):
                piece = result_ref[8 * g : 8 * g + 8, tile * 128 : (tile + 1) * 128]
                shift = (g * capacity - place) % 128
                if shift:
                    piece = pltpu.roll(piece, shift, 1)
                chunk = jnp.where(group_of == g, piece, chunk)
            answer_ref[h, 0:8, :] = chunk
        chunks = [jnp.minimum(here + 1, hosts - 1), jnp.maximum(here - 1, 0)]

        def write(side, row, size, value):
            answer_ref[chunks[side], 8 + row : 8 + row + size, :] = value
    else:
        answer_ref[...] = result_ref[...]

        def write(side, row, size, value):
            faces_ref[side, row : row + size, :] = value

    faces(write)


def assemble(stress):
    ready = []
    for here, low in stress:
        ready.append((here, low, previous_z(here), previous_z(low)))

    def at(c, sign_x, sign_y, sign_z):
        here, low, here_z, low_z = ready[c]
        if sign_z:
            near, far = here_z - here, low_z - low
        else:
            near, far = here_z + here, low_z + low
        both = far - near if sign_y else far + near
        return both[:-1] - both[1:] if sign_x else both[:-1] + both[1:]

    force = [
        at(0, 1, 0, 0) + at(5, 0, 1, 0) + at(4, 0, 0, 1),
        at(5, 1, 0, 0) + at(1, 0, 1, 0) + at(3, 0, 0, 1),
        at(4, 1, 0, 0) + at(3, 0, 1, 0) + at(2, 0, 0, 1),
    ]
    return [0.25 * value for value in force]


def elastic_kernel(
    hosts,
    capacity,
    motion_ref,
    stiff_ref,
    elem_ref,
    owner_ref,
    first_ref,
    second_ref,
    force_ref,
    edge_ref,
    index_ref,
    node_ref,
    wide_ref,
    stress_ref,
):
    size_x, size_y, size_z = motion_ref.shape[1:]
    node_ref[...] = jnp.zeros_like(node_ref)
    wide_ref[...] = jnp.zeros_like(wide_ref)
    stiffness = stiff_ref[...].astype(F32)
    elem, owner = elem_ref[...], owner_ref[...]
    points = elem.shape[1]
    column = elem // size_z
    depth = elem - column * size_z
    index_ref[0:1, :] = slots_of(owner, hosts, capacity)[2]
    index_ref[1:2, :] = column
    index_ref[2:3, :] = depth
    index_ref[3:, :] = jnp.zeros((5, points), jnp.int32)
    depth_hot = jnp.where(iota((size_z, points), 0) == depth, 1.0, 0.0).astype(BF16)
    column_hot = jnp.where(iota((size_x * size_y, points), 0) == column, 1.0, 0.0).astype(BF16)
    listed = dot_t(column_hot, depth_hot)
    for i in range(size_x):
        for m in range(3):
            low, high = sides_of(first_ref, second_ref, m, i)
            node_ref[m, i, 0:1, :] = low
            node_ref[m, i, 1 : size_y + 1, :] = motion_ref[m, i]
            node_ref[m, i, size_y + 1 : size_y + 2, :] = high
        low, _ = sides_of(first_ref, second_ref, 3, i)
        wide_ref[i, 0:1, :] = low
        keep = 1.0 - listed[i * size_y : (i + 1) * size_y]
        wide_ref[i, 1 : size_y + 1, :] = stiffness[i] * keep
    for m in range(3):
        edge_ref[m] = node_ref[m, 0]
        edge_ref[3 + m] = node_ref[m, size_x - 1]
    edge_ref[6] = wide_ref[size_x - 1]
    strain = block_strains([node_ref[m] for m in range(3)])
    stress = elastic_of(strain, wide_ref[: size_x - 1])
    for c in range(6):
        stress_ref[c, 0] = jnp.zeros(stress_ref.shape[2:], F32)
        stress_ref[c, 1:size_x] = stress[c]
        stress_ref[c, size_x] = jnp.zeros(stress_ref.shape[2:], F32)
    force = assemble(
        [(stress_ref[c, :, 1 : size_y + 1, :], stress_ref[c, :, 0:size_y, :]) for c in range(6)]
    )
    for m in range(3):
        force_ref[m] = force[m]


def final_kernel(packed, hosts, capacity, answer_ref, *rest):
    if packed:
        faces_ref = None
    else:
        faces_ref, *rest = rest
    (
        elastic_ref,
        edge_ref,
        index_ref,
        force_ref,
        tangent_ref,
        result_ref,
        node_ref,
        wide_ref,
        stress_ref,
    ) = rest
    size_x, size_y, size_z = elastic_ref.shape[1:]
    slot, column, depth = index_ref[0:1, :], index_ref[1:2, :], index_ref[2:3, :]
    points = slot.shape[1]
    slot_total = hosts * capacity
    if packed:
        group_of = iota((8, 128), 1) // capacity
        per_tile = 128 // capacity
        groups = []
        for g in range(4):
            tiles = []
            for t in range(hosts // per_tile):
                tile = jnp.zeros((8, 128), F32)
                for n in range(per_tile):
                    piece = answer_ref[t * per_tile + n, 0:8, :]
                    shift = ((n - g) * capacity) % 128
                    if shift:
                        piece = pltpu.roll(piece, shift, 1)
                    tile = jnp.where(group_of == n, piece, tile)
                tiles.append(tile)
            groups.append(jnp.concatenate(tiles, axis=1))
        answer = jnp.concatenate(groups, axis=0)
    else:
        answer = answer_ref[...]
    slot_hot = jnp.where(iota((slot_total, points), 0) == slot, 1.0, 0.0).astype(BF16)
    parts = jnp.concatenate(pieces(answer, 3), axis=0)
    chosen = jnp.dot(parts, slot_hot, preferred_element_type=F32)
    result = chosen[:ROWS] + (chosen[ROWS : 2 * ROWS] + chosen[2 * ROWS :])
    result_ref[...] = result
    for i in range(6):
        for j in range(6):
            at = 6 + UPPER.index((min(i, j), max(i, j)))
            tangent_ref[6 * i + j : 6 * i + j + 1, :] = result_ref[at : at + 1, :]

    here = lax.axis_index("macro")
    inner = [here > 0, here < hosts - 1]
    from_chunk = [jnp.maximum(here - 1, 0), jnp.minimum(here + 1, hosts - 1)]

    def face(side, row, size):
        if packed:
            value = answer_ref[from_chunk[side], 8 + row : 8 + row + size, :]
        else:
            value = faces_ref[side, row : row + size, :]
        return jnp.where(inner[side], value, 0.0)

    node_ref[...] = jnp.zeros_like(node_ref)
    wide_ref[...] = jnp.zeros_like(wide_ref)
    for m in range(3):
        for side, at in ((0, 0), (1, 3)):
            node_ref[m, at, 0:1, :] = face(side, 32 + 2 * m, 1)
            node_ref[m, at, 1 : size_y + 1, :] = face(side, 8 * m, 8)
            node_ref[m, at, size_y + 1 : size_y + 2, :] = face(side, 33 + 2 * m, 1)
        node_ref[m, 1] = edge_ref[m]
        node_ref[m, 2] = edge_ref[3 + m]
    wide_ref[0, 0:1, :] = face(0, 38, 1)
    wide_ref[0, 1 : size_y + 1, :] = face(0, 24, 8)
    wide_ref[1] = edge_ref[6]
    lower, upper = [], []
    for m in range(3):
        four = corners(node_ref[m])
        lower.append([jnp.stack([value[0], value[2]]) for value in four])
        upper.append([jnp.stack([value[1], value[3]]) for value in four])
    edge = elastic_of(strains(lower, upper), wide_ref[...])
    rows = (size_x - 1) * size_y
    depth_hot = jnp.where(iota((size_z, points), 0) == depth, 1.0, 0.0).astype(BF16)
    column_hot = iota((rows, points), 0) == column
    stress_ref[:, 1:size_x, 0:1, :] = jnp.zeros((6, size_x - 1, 1, size_z), F32)
    for c in range(6):
        placed = jnp.where(column_hot, result[c : c + 1], 0.0)
        high, low = pieces(placed, 2)
        field = dot_t(high, depth_hot) + dot_t(low, depth_hot)
        stress_ref[c, 1:size_x, 1 : size_y + 1, :] = field.reshape(size_x - 1, size_y, size_z)
        stress_ref[c, 0] = edge[c][0]
        stress_ref[c, size_x] = edge[c][1]
    force = assemble(
        [(stress_ref[c, :, 1 : size_y + 1, :], stress_ref[c, :, 0:size_y, :]) for c in range(6)]
    )
    for m in range(3):
        force_ref[m] = elastic_ref[m] + force[m]


def shape_of(shape, dtype=F32):
    return jax.ShapeDtypeStruct(shape, dtype)


def call(kernel, name, out_shape, args, scratch=(), flops=10**8, raw=0):
    specs = whole(*args[: len(args) - raw]) + [pl.BlockSpec(memory_space=pl.ANY)] * raw
    return pl.pallas_call(
        kernel,
        grid=(1,),
        out_shape=out_shape,
        in_specs=specs,
        out_specs=whole(*out_shape),
        scratch_shapes=scratch,
        compiler_params=pltpu.CompilerParams(vmem_limit_bytes=24 * 2**20),
        cost_estimate=pl.CostEstimate(flops=flops, bytes_accessed=2**20, transcendentals=0),
        name=name,
    )(*args)


def on_device(
    motion,
    stiffness,
    point_elem,
    point_owner,
    point_pattern,
    history,
    basis,
    mode_map,
    weights,
    patterns,
):
    size_x, size_y, size_z = motion.shape[1:]
    points = point_elem.shape[0]
    hosts = lax.axis_size("macro")
    sides = lax.axis_size("micro")
    capacity = 2 * points // hosts
    slots = capacity * hosts
    modes = mode_map.shape[0]
    half = modes // 2
    hyper = weights.shape[0]
    lanes = 128
    direct = capacity % 16 == 0
    packed = capacity * 4 == lanes and slots % lanes == 0
    motion = in_hbm(motion)
    stiffness = in_hbm(stiffness)
    elem = in_hbm(point_elem.reshape(1, points))
    owner = in_hbm(point_owner.reshape(1, points))
    pattern = in_hbm(point_pattern.reshape(1, points))
    history = in_hbm(history)
    map_rows = in_hbm(mode_map.T)

    sent = (
        [shape_of((hosts, 2 * capacity + 8, half), BF16)]
        if direct
        else [shape_of((slots, modes), BF16), shape_of((hosts, modes), BF16)]
    )
    swap = shape_of((4, size_x, size_z))
    *payload, first, second, face = call(
        functools.partial(dispatch_kernel, hosts, capacity, direct),
        "dispatch",
        sent + [swap, swap, shape_of((8, size_y, size_z))],
        (motion, stiffness, elem, owner, pattern, history, map_rows),
    )

    if direct:
        received = lax.all_to_all(payload[0], "macro", 0, 0, tiled=True)
        groups, group = hosts, capacity
    else:
        rows, ids = payload
        joined = jnp.concatenate(
            [
                rows[:, :half].reshape(hosts, capacity, half),
                rows[:, half:].reshape(hosts, capacity, half),
                ids.reshape(hosts, 2, half),
            ],
            axis=1,
        )
        joined = lax.all_to_all(joined, "macro", 0, 0, tiled=True)
        ids = jnp.sum(joined[:, 2 * capacity :].astype(F32), axis=0).astype(BF16)
        received = jnp.concatenate(
            [
                joined[:, :capacity].reshape(1, slots, half),
                joined[:, capacity : 2 * capacity].reshape(1, slots, half),
                jnp.pad(ids, ((0, 6), (0, 0)))[None],
            ],
            axis=1,
        )
        groups, group = 1, slots

    def swapped(value, start):
        pairs = [(i, i + 1) for i in range(start, sides - 1, 2)]
        return lax.ppermute(value, "micro", pairs + [(b, a) for a, b in pairs])

    first, second = swapped(first, 0), swapped(second, 1)

    rows = in_hbm(basis.reshape(6, hyper, modes))
    count = hyper // lanes
    table, const, column, bits = call(
        table_kernel,
        "tables",
        [
            shape_of((96, hyper), BF16),
            shape_of((48, lanes)),
            shape_of((hyper, lanes)),
            shape_of((hyper, patterns.shape[0]), BF16),
        ],
        (map_rows, in_hbm(weights.reshape(count, lanes)), in_hbm(patterns.T), rows),
        [VMEM((count, 6, lanes, modes), BF16), pltpu.SemaphoreType.DMA((count,))],
        raw=1,
    )

    answer = call(
        functools.partial(micro_kernel, packed, hosts, group),
        "micro_response",
        [shape_of((hosts, 48, lanes))]
        if packed
        else [shape_of((ROWS, slots)), shape_of((2, 40, lanes))],
        (
            received,
            first,
            second,
            face,
            const,
            rows,
            bits,
            column,
            table,
        ),
        [
            VMEM((slots, modes), BF16),
            VMEM((patterns.shape[0], slots), BF16),
            VMEM((count, 6, lanes, modes), BF16),
            VMEM(bits.shape, BF16),
            VMEM(column.shape, F32),
            VMEM(table.shape, BF16),
            VMEM((6, lanes, slots), F32),
            VMEM((6, lanes, slots), F32),
            VMEM((lanes, slots), BF16),
            VMEM((lanes, slots), BF16),
            VMEM((7, 8, slots), F32),
            VMEM((48, slots), F32),
            VMEM((ROWS, slots), F32),
            pltpu.SemaphoreType.DMA((count + 3,)),
        ],
        raw=4,
    )

    if packed:
        answered = [lax.all_to_all(answer[0], "macro", 0, 0, tiled=True)]
    else:
        result, faces = answer
        here = lax.axis_index("macro")
        order = jnp.arange(hosts)[:, None, None]
        flat = result.reshape(ROWS, hosts, capacity).transpose(1, 0, 2).reshape(hosts, -1)
        tiles = pl.cdiv(flat.shape[1], lanes)
        flat = jnp.pad(flat, ((0, 0), (0, tiles * lanes - flat.shape[1])))
        joined = jnp.concatenate(
            [flat.reshape(hosts, tiles, lanes), jnp.where(order > here, faces[0], faces[1])], axis=1
        )
        joined = lax.all_to_all(joined, "macro", 0, 0, tiled=True)
        flat = joined[:, :tiles].reshape(hosts, -1)[:, : ROWS * capacity]
        result = flat.reshape(hosts, ROWS, capacity).transpose(1, 0, 2).reshape(ROWS, slots)
        low = lax.dynamic_index_in_dim(joined, jnp.maximum(here - 1, 0), 0, False)
        high = lax.dynamic_index_in_dim(joined, jnp.minimum(here + 1, hosts - 1), 0, False)
        answered = [result, jnp.stack([low[tiles:], high[tiles:]])]

    elastic = call(
        functools.partial(elastic_kernel, hosts, capacity),
        "elastic_forces",
        [shape_of(motion.shape), shape_of((7, 16, size_z)), shape_of((8, points), jnp.int32)],
        (motion, stiffness, elem, owner, first, second),
        [
            VMEM((3, size_x, 16, size_z), F32),
            VMEM((size_x, 16, size_z), F32),
            VMEM((6, size_x + 1, 16, size_z), F32),
        ],
    )

    force, tangent = call(
        functools.partial(final_kernel, packed, hosts, capacity),
        "final_forces",
        [shape_of(motion.shape), shape_of((36, points))],
        (*answered, *elastic),
        [
            VMEM((ROWS, points), F32),
            VMEM((3, 4, 16, size_z), F32),
            VMEM((2, 16, size_z), F32),
            VMEM((6, size_x + 1, 16, size_z), F32),
        ],
    )
    return (force, tangent)


def solution(mesh):
    return jax.shard_map(
        on_device,
        mesh=mesh,
        in_specs=(
            P(None, "macro", "micro", None),
            P("macro", "micro", None),
            P(("macro", "micro")),
            P(("macro", "micro")),
            P(("macro", "micro")),
            P(None, ("macro", "micro")),
            P("macro", None, None),
            P(),
            P(),
            P(),
        ),
        out_specs=(P(None, "macro", "micro", None), P(None, ("macro", "micro"))),
        check_vma=False,
    )
```

```python
import functools

import jax
import jax.numpy as jnp
from jax import lax
from jax.experimental import pallas as pl
from jax.experimental.pallas import tpu as pltpu
from jax.sharding import PartitionSpec as P

YIELD_STRESS = 1.5
HARDENING = 0.2
F32 = jnp.float32
BF16 = jnp.bfloat16
VMEM = pltpu.VMEM
ROWS = 32
UPPER = [(i, j) for i in range(6) for j in range(i, 6)]


def whole(*arrays):
    return [pl.BlockSpec(value.shape, lambda s, n=len(value.shape): (0,) * n) for value in arrays]


def in_hbm(value):
    return pltpu.with_memory_space_constraint(value, pltpu.HBM)


def iota(shape, dim):
    return lax.broadcasted_iota(jnp.int32, shape, dim)


def dot_t(left, right):
    return lax.dot_general(left, right, (((1,), (1,)), ((), ())), preferred_element_type=F32)


def pieces(value, count):
    out = []
    for _ in range(count):
        piece = value.astype(BF16)
        out.append(piece)
        value = value - piece.astype(F32)
    return out


def next_z(field):
    last = field.ndim - 1
    size = field.shape[last]
    rolled = pltpu.roll(field, size - 1, last)
    return jnp.where(iota(field.shape, last) == size - 1, 0.0, rolled)


def previous_z(field):
    last = field.ndim - 1
    rolled = pltpu.roll(field, 1, last)
    return jnp.where(iota(field.shape, last) == 0, 0.0, rolled)


def corners(field):
    y_up = pltpu.roll(field, field.shape[1] - 1, 1)
    return [field, y_up, next_z(field), next_z(y_up)]


def strains(lower, upper):
    grads = []
    for low, high in zip(lower, upper):
        dx = [b - a for a, b in zip(low, high)]
        grad_x = (dx[0] + dx[1] + dx[2] + dx[3]) * 0.25
        dy = [value[1] - value[0] for value in (low, high)]
        dy_z = [value[3] - value[2] for value in (low, high)]
        grad_y = (dy[0] + dy[1] + dy_z[0] + dy_z[1]) * 0.25
        dz = [value[2] - value[0] for value in (low, high)]
        dz_y = [value[3] - value[1] for value in (low, high)]
        grad_z = (dz[0] + dz[1] + dz_y[0] + dz_y[1]) * 0.25
        grads.append((grad_x, grad_y, grad_z))
    return [
        grads[0][0],
        grads[1][1],
        grads[2][2],
        grads[1][2] + grads[2][1],
        grads[0][2] + grads[2][0],
        grads[0][1] + grads[1][0],
    ]


def block_strains(fields):
    nodes = [corners(field) for field in fields]
    return strains(
        [[value[:-1] for value in four] for four in nodes],
        [[value[1:] for value in four] for four in nodes],
    )


def elastic_of(strain, stiffness):
    volume = strain[0] + strain[1] + strain[2]
    rest = volume - volume * (1.0 / 3.0)
    normal = [stiffness * (rest + strain[c]) for c in range(3)]
    return normal + [stiffness * (0.5 * strain[c]) for c in range(3, 6)]


def slots_of(owner, hosts, capacity):
    points = owner.shape[1]
    chosen = iota((hosts, points), 0) == owner
    host_hot = jnp.where(chosen, 1.0, 0.0)
    before = jnp.where(iota((points, points), 0) < iota((points, points), 1), 1.0, 0.0)
    counts = jnp.dot(host_hot.astype(BF16), before.astype(BF16), preferred_element_type=F32)
    position = jnp.sum(host_hot * counts, axis=0, keepdims=True).astype(jnp.int32)
    return host_hot, position, owner * capacity + position


def dispatch_kernel(
    hosts,
    capacity,
    direct,
    motion_ref,
    stiff_ref,
    elem_ref,
    owner_ref,
    pattern_ref,
    history_ref,
    map_ref,
    payload_ref,
    *rest,
):
    size_x, size_y, size_z = motion_ref.shape[1:]
    elem, owner = elem_ref[...], owner_ref[...]
    points = elem.shape[1]
    strain = block_strains([motion_ref[m] for m in range(3)])
    rows = (size_x - 1) * size_y
    field = jnp.concatenate([value.reshape(rows, size_z) for value in strain], axis=0)
    column = elem // size_z
    depth = elem - column * size_z
    depth_hot = jnp.where(iota((size_z, points), 0) == depth, 1.0, 0.0).astype(BF16)
    picked = jnp.dot(field.astype(BF16), depth_hot, preferred_element_type=F32)
    column_hot = iota((rows, points), 0) == column
    macro_strain = jnp.concatenate(
        [
            jnp.sum(
                jnp.where(column_hot, picked[c * rows : (c + 1) * rows], 0.0),
                axis=0,
                keepdims=True,
            )
            for c in range(6)
        ],
        axis=0,
    ).astype(BF16)
    mapped = lax.dot_general(
        map_ref[...], macro_strain, (((0,), (0,)), ((), ())), preferred_element_type=F32
    )
    coefficients = (mapped + history_ref[...].astype(F32)).astype(BF16)
    host_hot, position, slot = slots_of(owner, hosts, capacity)
    slot_total = hosts * capacity
    slot_hot = jnp.where(iota((slot_total, points), 0) == slot, 1.0, 0.0).astype(BF16)
    sent = dot_t(slot_hot, coefficients).astype(BF16)
    place = position + lax.axis_index("macro") * capacity
    modes = sent.shape[1]
    half = modes // 2
    place_hot = jnp.where(iota((modes, points), 0) == place, 1.0, 0.0).astype(BF16)
    ids = dot_t((host_hot * pattern_ref[...].astype(F32)).astype(BF16), place_hot)
    if direct:
        for h in range(hosts):
            mine = sent[h * capacity : (h + 1) * capacity]
            payload_ref[h, :capacity, :] = mine[:, :half]
            payload_ref[h, capacity : 2 * capacity, :] = mine[:, half:]
            row = iota((8, half), 0)
            low, high = ids[h : h + 1, :half], ids[h : h + 1, half:]
            tile = jnp.where(row == 0, low, jnp.where(row == 1, high, 0.0))
            payload_ref[h, 2 * capacity :, :] = tile.astype(BF16)
    else:
        payload_ref[...] = sent
        rest[0][...] = ids.astype(BF16)
        rest = rest[1:]
    first_ref, second_ref, x_first_ref, x_second_ref = rest
    stiffness = stiff_ref[...].astype(F32)
    even = lax.rem(lax.axis_index("micro"), 2) == 0
    for i in range(size_x):
        for m in range(4):
            if m < 3:
                up, down = motion_ref[m, i, size_y - 1 : size_y, :], motion_ref[m, i, 0:1, :]
            else:
                up = down = stiffness[i, size_y - 1 : size_y, :]
            first_ref[m, i : i + 1, :] = jnp.where(even, up, down)
            second_ref[m, i : i + 1, :] = jnp.where(even, down, up)
    even = lax.rem(lax.axis_index("macro"), 2) == 0
    for m in range(4):
        if m < 3:
            up, down = motion_ref[m, size_x - 1], motion_ref[m, 0]
        else:
            up = down = stiffness[size_x - 1]
        x_first_ref[m] = jnp.where(even, up, down)
        x_second_ref[m] = jnp.where(even, down, up)


def table_kernel(
    map_ref,
    weights_ref,
    patterns_ref,
    basis_ref,
    table_ref,
    const_ref,
    column_ref,
    bits_ref,
    blocks_ref,
    others_ref,
    sems,
):
    hyper = weights_ref.shape[1]
    lanes = 128
    kept, _, wide, modes = blocks_ref.shape
    count = hyper // wide
    copies = []
    for n in range(count):
        target = blocks_ref.at[n] if n < kept else others_ref.at[n - kept]
        copies.append(
            pltpu.make_async_copy(basis_ref.at[:, pl.ds(n * wide, wide), :], target, sems.at[n])
        )
        copies[n].start()
    weights = weights_ref[...]
    split = [piece.astype(F32) for piece in pieces(weights, 3)]
    row = iota((8, hyper), 0)
    stack = jnp.where(
        row == 0, split[0], jnp.where(row == 1, split[1], jnp.where(row == 2, split[2], 0.0))
    )
    column_ref[...] = lax.dot_general(
        stack.astype(BF16),
        jnp.ones((8, lanes), BF16),
        (((0,), (0,)), ((), ())),
        preferred_element_type=F32,
    )
    patterns = patterns_ref[...]
    words, total = patterns.shape
    parts = [((patterns >> (8 * k)) & 255).astype(F32) for k in range(4)]
    spare = -4 * words % 8
    parts = jnp.concatenate(parts + [jnp.zeros((spare, total), F32)] * (spare > 0), axis=0)
    place = iota((1, 4 * words + spare), 1)
    part = jnp.where(place >= words, 1, 0) + jnp.where(place >= 2 * words, 1, 0)
    part = part + jnp.where(place >= 3 * words, 1, 0)
    start = 30 * (place - words * part) + 8 * part
    size = jnp.where(part == 3, 6, 8)
    after = iota((hyper, 4 * words + spare), 0) - start
    byte_hot = jnp.where((after >= 0) & (after < size), 1.0, 0.0).astype(BF16)
    value = jnp.dot(byte_hot, parts.astype(BF16), preferred_element_type=F32).astype(jnp.int32)
    index = iota((hyper, total), 0)
    offset = index - 30 * ((index * 2185) >> 16)
    bits_ref[...] = ((value >> (offset & 7)) & 1).astype(F32).astype(BF16)

    modes_map = map_ref[...]
    modes_map = jnp.concatenate(
        [modes_map.astype(F32), jnp.zeros((2, modes), F32)], axis=0
    ).astype(BF16)
    sums = jnp.zeros((48, wide), F32)
    for n in range(count):
        copies[n].wait()
        source = blocks_ref.at[n] if n < kept else others_ref.at[n - kept]
        part = slice(n * wide, (n + 1) * wide)
        local = [dot_t(modes_map, source[c]) for c in range(6)]
        trace = local[0] + local[1] + local[2]
        third = trace / 3.0
        shaped = [local[c] - third for c in range(3)] + [0.5 * local[c] for c in range(3, 6)]
        weight = weights[:, part]
        shaped = [weight * value for value in shaped]
        weighted_trace = weight * trace
        blocks, adds = [], []
        for i in range(6):
            entry = local[0][i : i + 1] * shaped[0]
            for c in range(1, 6):
                entry = entry + local[c][i : i + 1] * shaped[c]
            blocks.append(entry)
            adds.append(entry + trace[i : i + 1] * weighted_trace)
        sums = sums + jnp.concatenate(adds, axis=0)
        high, low = pieces(jnp.concatenate(blocks, axis=0), 2)
        table_ref[0:48, part] = high
        table_ref[48:96, part] = low
    const_ref[...] = jnp.broadcast_to(jnp.sum(sums, axis=1, keepdims=True), const_ref.shape)


def sides_of(first_ref, second_ref, axis, m, at=None):
    even = lax.rem(lax.axis_index(axis), 2) == 0
    rows = slice(None) if at is None else slice(at, at + 1)
    first, second = first_ref[m, rows, :], second_ref[m, rows, :]
    return jnp.where(even, second, first), jnp.where(even, first, second)


def micro_kernel(
    packed,
    hosts,
    capacity,
    received_ref,
    first_ref,
    second_ref,
    const_ref,
    bits_ref,
    column_ref,
    table_ref,
    blocks_ref,
    basis_ref,
    answer_ref,
    *rest,
):
    if packed:
        corners_ref = None
    else:
        corners_ref, *rest = rest
    (
        state_ref,
        hot_ref,
        others_ref,
        strain_even,
        strain_odd,
        high_even,
        high_odd,
        low_even,
        low_odd,
        result_ref,
        sems,
    ) = rest
    strain_refs = (strain_even, strain_odd)
    high_refs = (high_even, high_odd)
    low_refs = (low_even, low_odd)
    groups = received_ref.shape[0]
    slots = groups * capacity
    kept, _, block, modes = blocks_ref.shape
    half = modes // 2
    count = kept + others_ref.shape[0]
    copies = []
    for n in range(count - kept):
        part = pl.ds((kept + n) * block, block)
        copies.append(
            pltpu.make_async_copy(basis_ref.at[:, part, :], others_ref.at[n], sems.at[n])
        )
        copies[n].start()

    ids = jnp.zeros((8, half), F32)
    for h in range(groups):
        own = pl.ds(h * capacity, capacity)
        state_ref[own, :half] = received_ref[h, :capacity, :]
        state_ref[own, half:] = received_ref[h, capacity : 2 * capacity, :]
        ids = ids + received_ref[h, 2 * capacity :, :].astype(F32)
    ids = jnp.concatenate([ids[0:1], ids[1:2]], axis=1).astype(jnp.int32)
    hot_ref[...] = jnp.where(iota(hot_ref.shape, 0) == ids, 1.0, 0.0).astype(BF16)

    def rows_of(n):
        if n >= kept:
            copies[n - kept].wait()
        source = blocks_ref.at[n] if n < kept else others_ref.at[n - kept]
        rows = source[...].reshape(6 * block, modes)
        strain_refs[n % 2][...] = dot_t(rows, state_ref[...]).reshape(6, block, slots)

    def tangent_of(n):
        table = table_ref[:, n * block : (n + 1) * block]
        one = jnp.dot(table, high_refs[n % 2][...], preferred_element_type=F32)
        two = jnp.dot(table[:48], low_refs[n % 2][...], preferred_element_type=F32)
        return one[:48] + (one[48:] + two)

    def respond(n, sums):
        sums = list(sums)
        strain_ref, high_ref, low_ref = (refs[n % 2] for refs in (strain_refs, high_refs, low_refs))
        part = pl.ds(n * block, block)
        flags = jnp.dot(bits_ref[part, :], hot_ref[...], preferred_element_type=F32)
        strip = 16
        for r in range(0, block, strip):
            at = pl.ds(r, strip)
            e = [strain_ref[c, at, :] for c in range(6)]
            volume = e[0] + e[1] + e[2]
            third = volume * (1.0 / 3.0)
            d = [e[c] - third for c in range(3)]
            normal = d[0] * d[0] + d[1] * d[1] + d[2] * d[2]
            shear = e[3] * e[3] + e[4] * e[4] + e[5] * e[5]
            square = jnp.maximum(normal + 0.5 * shear, YIELD_STRESS * YIELD_STRESS)
            factor = (YIELD_STRESS * (1.0 - HARDENING)) * lax.rsqrt(square) + (HARDENING - 1.0)
            change = flags[r : r + strip] * factor
            high = change.astype(BF16)
            high_ref[at, :] = high
            low_ref[at, :] = (change - high.astype(F32)).astype(BF16)
            column = column_ref[pl.ds(n * block + r, strip), :]
            weight = jnp.concatenate([column] * (slots // column.shape[1]), axis=1)
            scaled = weight + weight * change
            terms = [scaled * d[c] for c in range(3)] + [scaled * e[c] for c in range(3, 6)]
            terms.append(weight * volume)
            for k in range(7):
                sums[k] = sums[k] + (terms[k][:8] + terms[k][8:])
        return sums

    sums = [jnp.zeros((8, slots), F32)] * 7
    tangent = jnp.zeros((48, slots), F32)
    rows_of(0)
    for n in range(count):
        if n > 0:
            tangent = tangent + tangent_of(n - 1)
        sums = respond(n, sums)
        if n + 1 < count:
            rows_of(n + 1)
    tangent = tangent + tangent_of(count - 1)

    volume = jnp.sum(sums[6], axis=0, keepdims=True)
    for c in range(6):
        total = jnp.sum(sums[c], axis=0, keepdims=True)
        result_ref[c : c + 1, :] = total + volume if c < 3 else 0.5 * total
    const = const_ref[...]
    const = jnp.concatenate([const] * (slots // const.shape[1]), axis=1)
    tangent = tangent + const
    at = 6
    for i in range(6):
        result_ref[at : at + 6 - i, :] = tangent[8 * i + i : 8 * i + 6]
        at += 6 - i
    result_ref[at:, :] = jnp.zeros((ROWS - at, slots), F32)

    last = first_ref.shape[1] - 1

    def corner_rows(write):
        for m in range(4):
            up = sides_of(first_ref, second_ref, "micro", m, last)
            down = sides_of(first_ref, second_ref, "micro", m, 0)
            for n in range(2):
                write(0, 2 * m + n, up[n])
                write(1, 2 * m + n, down[n])

    if packed:
        here = lax.axis_index("macro")
        group_of = iota((8, 128), 1) // capacity
        for h in range(hosts):
            chunk = jnp.zeros((8, 128), F32)
            tile, place = divmod(h * capacity, 128)
            for g in range(4):
                piece = result_ref[8 * g : 8 * g + 8, tile * 128 : (tile + 1) * 128]
                shift = (g * capacity - place) % 128
                if shift:
                    piece = pltpu.roll(piece, shift, 1)
                chunk = jnp.where(group_of == g, piece, chunk)
            answer_ref[h, 0:8, :] = chunk
        chunks = [jnp.minimum(here + 1, hosts - 1), jnp.maximum(here - 1, 0)]

        def write(side, row, value):
            answer_ref[chunks[side], 8 + row : 9 + row, :] = value
    else:
        answer_ref[...] = result_ref[...]

        def write(side, row, value):
            corners_ref[side, row : row + 1, :] = value

    corner_rows(write)


def assemble(stress):
    ready = []
    for here, low in stress:
        ready.append((here, low, previous_z(here), previous_z(low)))

    def at(c, sign_x, sign_y, sign_z):
        here, low, here_z, low_z = ready[c]
        if sign_z:
            near, far = here_z - here, low_z - low
        else:
            near, far = here_z + here, low_z + low
        both = far - near if sign_y else far + near
        return both[:-1] - both[1:] if sign_x else both[:-1] + both[1:]

    force = [
        at(0, 1, 0, 0) + at(5, 0, 1, 0) + at(4, 0, 0, 1),
        at(5, 1, 0, 0) + at(1, 0, 1, 0) + at(3, 0, 0, 1),
        at(4, 1, 0, 0) + at(3, 0, 1, 0) + at(2, 0, 0, 1),
    ]
    return [0.25 * value for value in force]


def elastic_kernel(
    hosts,
    capacity,
    motion_ref,
    stiff_ref,
    elem_ref,
    owner_ref,
    first_ref,
    second_ref,
    force_ref,
    edge_ref,
    index_ref,
    node_ref,
    wide_ref,
    stress_ref,
):
    size_x, size_y, size_z = motion_ref.shape[1:]
    node_ref[...] = jnp.zeros_like(node_ref)
    wide_ref[...] = jnp.zeros_like(wide_ref)
    stiffness = stiff_ref[...].astype(F32)
    elem, owner = elem_ref[...], owner_ref[...]
    points = elem.shape[1]
    column = elem // size_z
    depth = elem - column * size_z
    index_ref[0:1, :] = slots_of(owner, hosts, capacity)[2]
    index_ref[1:2, :] = column
    index_ref[2:3, :] = depth
    index_ref[3:, :] = jnp.zeros((5, points), jnp.int32)
    depth_hot = jnp.where(iota((size_z, points), 0) == depth, 1.0, 0.0).astype(BF16)
    column_hot = jnp.where(iota((size_x * size_y, points), 0) == column, 1.0, 0.0).astype(BF16)
    listed = dot_t(column_hot, depth_hot)
    for i in range(size_x):
        for m in range(3):
            low, high = sides_of(first_ref, second_ref, "micro", m, i)
            node_ref[m, i, 0:1, :] = low
            node_ref[m, i, 1 : size_y + 1, :] = motion_ref[m, i]
            node_ref[m, i, size_y + 1 : size_y + 2, :] = high
        low, _ = sides_of(first_ref, second_ref, "micro", 3, i)
        wide_ref[i, 0:1, :] = low
        keep = 1.0 - listed[i * size_y : (i + 1) * size_y]
        wide_ref[i, 1 : size_y + 1, :] = stiffness[i] * keep
    for m in range(3):
        edge_ref[m] = node_ref[m, 0]
        edge_ref[3 + m] = node_ref[m, size_x - 1]
    edge_ref[6] = wide_ref[size_x - 1]
    strain = block_strains([node_ref[m] for m in range(3)])
    stress = elastic_of(strain, wide_ref[: size_x - 1])
    for c in range(6):
        stress_ref[c, 0] = jnp.zeros(stress_ref.shape[2:], F32)
        stress_ref[c, 1:size_x] = stress[c]
        stress_ref[c, size_x] = jnp.zeros(stress_ref.shape[2:], F32)
    force = assemble(
        [(stress_ref[c, :, 1 : size_y + 1, :], stress_ref[c, :, 0:size_y, :]) for c in range(6)]
    )
    for m in range(3):
        force_ref[m] = force[m]


def final_kernel(packed, hosts, capacity, answer_ref, *rest):
    if packed:
        corners_ref = None
    else:
        corners_ref, *rest = rest
    (
        second_ref,
        first_ref,
        elastic_ref,
        edge_ref,
        index_ref,
        force_ref,
        tangent_ref,
        result_ref,
        node_ref,
        wide_ref,
        stress_ref,
    ) = rest
    size_x, size_y, size_z = elastic_ref.shape[1:]
    slot, column, depth = index_ref[0:1, :], index_ref[1:2, :], index_ref[2:3, :]
    points = slot.shape[1]
    slot_total = hosts * capacity
    if packed:
        group_of = iota((8, 128), 1) // capacity
        per_tile = 128 // capacity
        groups = []
        for g in range(4):
            tiles = []
            for t in range(hosts // per_tile):
                tile = jnp.zeros((8, 128), F32)
                for n in range(per_tile):
                    piece = answer_ref[t * per_tile + n, 0:8, :]
                    shift = ((n - g) * capacity) % 128
                    if shift:
                        piece = pltpu.roll(piece, shift, 1)
                    tile = jnp.where(group_of == n, piece, tile)
                tiles.append(tile)
            groups.append(jnp.concatenate(tiles, axis=1))
        answer = jnp.concatenate(groups, axis=0)
    else:
        answer = answer_ref[...]
    slot_hot = jnp.where(iota((slot_total, points), 0) == slot, 1.0, 0.0).astype(BF16)
    parts = jnp.concatenate(pieces(answer, 3), axis=0)
    chosen = jnp.dot(parts, slot_hot, preferred_element_type=F32)
    result = chosen[:ROWS] + (chosen[ROWS : 2 * ROWS] + chosen[2 * ROWS :])
    result_ref[...] = result
    for i in range(6):
        for j in range(6):
            at = 6 + UPPER.index((min(i, j), max(i, j)))
            tangent_ref[6 * i + j : 6 * i + j + 1, :] = result_ref[at : at + 1, :]

    here = lax.axis_index("macro")
    inner = [here > 0, here < hosts - 1]
    from_chunk = [jnp.maximum(here - 1, 0), jnp.minimum(here + 1, hosts - 1)]

    def corner(side, row):
        if packed:
            value = answer_ref[from_chunk[side], 8 + row : 9 + row, :]
        else:
            value = corners_ref[side, row : row + 1, :]
        return jnp.where(inner[side], value, 0.0)

    node_ref[...] = jnp.zeros_like(node_ref)
    wide_ref[...] = jnp.zeros_like(wide_ref)
    for m in range(3):
        faces = sides_of(first_ref, second_ref, "macro", m)
        for side, at in ((0, 0), (1, 3)):
            node_ref[m, at, 0:1, :] = corner(side, 2 * m)
            node_ref[m, at, 1 : size_y + 1, :] = faces[side]
            node_ref[m, at, size_y + 1 : size_y + 2, :] = corner(side, 2 * m + 1)
        node_ref[m, 1] = edge_ref[m]
        node_ref[m, 2] = edge_ref[3 + m]
    wide_ref[0, 0:1, :] = corner(0, 6)
    wide_ref[0, 1 : size_y + 1, :] = sides_of(first_ref, second_ref, "macro", 3)[0]
    wide_ref[1] = edge_ref[6]
    lower, upper = [], []
    for m in range(3):
        four = corners(node_ref[m])
        lower.append([jnp.stack([value[0], value[2]]) for value in four])
        upper.append([jnp.stack([value[1], value[3]]) for value in four])
    edge = elastic_of(strains(lower, upper), wide_ref[...])
    rows = (size_x - 1) * size_y
    depth_hot = jnp.where(iota((size_z, points), 0) == depth, 1.0, 0.0).astype(BF16)
    column_hot = iota((rows, points), 0) == column
    stress_ref[:, 1:size_x, 0:1, :] = jnp.zeros((6, size_x - 1, 1, size_z), F32)
    for c in range(6):
        placed = jnp.where(column_hot, result[c : c + 1], 0.0)
        high, low = pieces(placed, 2)
        field = dot_t(high, depth_hot) + dot_t(low, depth_hot)
        stress_ref[c, 1:size_x, 1 : size_y + 1, :] = field.reshape(size_x - 1, size_y, size_z)
        stress_ref[c, 0] = edge[c][0]
        stress_ref[c, size_x] = edge[c][1]
    force = assemble(
        [(stress_ref[c, :, 1 : size_y + 1, :], stress_ref[c, :, 0:size_y, :]) for c in range(6)]
    )
    for m in range(3):
        force_ref[m] = elastic_ref[m] + force[m]


def shape_of(shape, dtype=F32):
    return jax.ShapeDtypeStruct(shape, dtype)


def call(kernel, name, out_shape, args, scratch=(), flops=10**8, raw=0):
    specs = whole(*args[: len(args) - raw]) + [pl.BlockSpec(memory_space=pl.ANY)] * raw
    return pl.pallas_call(
        kernel,
        grid=(1,),
        out_shape=out_shape,
        in_specs=specs,
        out_specs=whole(*out_shape),
        scratch_shapes=scratch,
        compiler_params=pltpu.CompilerParams(vmem_limit_bytes=24 * 2**20),
        cost_estimate=pl.CostEstimate(flops=flops, bytes_accessed=2**20, transcendentals=0),
        name=name,
    )(*args)


def on_device(
    motion,
    stiffness,
    point_elem,
    point_owner,
    point_pattern,
    history,
    basis,
    mode_map,
    weights,
    patterns,
):
    size_x, size_y, size_z = motion.shape[1:]
    points = point_elem.shape[0]
    hosts = lax.axis_size("macro")
    capacity = 2 * points // hosts
    slots = capacity * hosts
    modes = mode_map.shape[0]
    half = modes // 2
    hyper = weights.shape[0]
    lanes = 128
    direct = capacity % 16 == 0
    packed = capacity * 4 == lanes and slots % lanes == 0
    motion = in_hbm(motion)
    stiffness = in_hbm(stiffness)
    elem = in_hbm(point_elem.reshape(1, points))
    owner = in_hbm(point_owner.reshape(1, points))
    pattern = in_hbm(point_pattern.reshape(1, points))
    history = in_hbm(history)
    map_rows = in_hbm(mode_map.T)

    sent = (
        [shape_of((hosts, 2 * capacity + 8, half), BF16)]
        if direct
        else [shape_of((slots, modes), BF16), shape_of((hosts, modes), BF16)]
    )
    swap, x_swap = shape_of((4, size_x, size_z)), shape_of((4, size_y, size_z))
    *payload, first, second, x_first, x_second = call(
        functools.partial(dispatch_kernel, hosts, capacity, direct),
        "dispatch",
        sent + [swap, swap, x_swap, x_swap],
        (motion, stiffness, elem, owner, pattern, history, map_rows),
    )

    if direct:
        received = lax.all_to_all(payload[0], "macro", 0, 0, tiled=True)
        groups, group = hosts, capacity
    else:
        rows, ids = payload
        joined = jnp.concatenate(
            [
                rows[:, :half].reshape(hosts, capacity, half),
                rows[:, half:].reshape(hosts, capacity, half),
                ids.reshape(hosts, 2, half),
            ],
            axis=1,
        )
        joined = lax.all_to_all(joined, "macro", 0, 0, tiled=True)
        ids = jnp.sum(joined[:, 2 * capacity :].astype(F32), axis=0).astype(BF16)
        received = jnp.concatenate(
            [
                joined[:, :capacity].reshape(1, slots, half),
                joined[:, capacity : 2 * capacity].reshape(1, slots, half),
                jnp.pad(ids, ((0, 6), (0, 0)))[None],
            ],
            axis=1,
        )
        groups, group = 1, slots

    def swapped(value, axis, start):
        pairs = [(i, i + 1) for i in range(start, lax.axis_size(axis) - 1, 2)]
        return lax.ppermute(value, axis, pairs + [(b, a) for a, b in pairs])

    first, second = swapped(first, "micro", 0), swapped(second, "micro", 1)
    x_first, x_second = swapped(x_first, "macro", 0), swapped(x_second, "macro", 1)

    rows = in_hbm(basis.reshape(6, hyper, modes))
    wide, kept = 256, 2
    table, const, column, bits, blocks = call(
        table_kernel,
        "tables",
        [
            shape_of((96, hyper), BF16),
            shape_of((48, lanes)),
            shape_of((hyper, lanes)),
            shape_of((hyper, patterns.shape[0]), BF16),
            shape_of((kept, 6, wide, modes), BF16),
        ],
        (map_rows, in_hbm(weights.reshape(1, hyper)), in_hbm(patterns.T), rows),
        [
            VMEM((hyper // wide - kept, 6, wide, modes), BF16),
            pltpu.SemaphoreType.DMA((hyper // wide,)),
        ],
        raw=1,
    )

    answer = call(
        functools.partial(micro_kernel, packed, hosts, group),
        "micro_response",
        [shape_of((hosts, 16, lanes))]
        if packed
        else [shape_of((ROWS, slots)), shape_of((2, 8, lanes))],
        (
            received,
            first,
            second,
            const,
            bits,
            column,
            table,
            blocks,
            rows,
        ),
        [
            VMEM((slots, modes), BF16),
            VMEM((patterns.shape[0], slots), BF16),
            VMEM((hyper // wide - kept, 6, wide, modes), BF16),
            *[VMEM((6, wide, slots), F32)] * 2,
            *[VMEM((wide, slots), BF16)] * 4,
            VMEM((ROWS, slots), F32),
            pltpu.SemaphoreType.DMA((hyper // wide - kept,)),
        ],
        raw=1,
    )

    if packed:
        answered = [lax.all_to_all(answer[0], "macro", 0, 0, tiled=True)]
    else:
        result, edges = answer
        here = lax.axis_index("macro")
        order = jnp.arange(hosts)[:, None, None]
        flat = result.reshape(ROWS, hosts, capacity).transpose(1, 0, 2).reshape(hosts, -1)
        tiles = pl.cdiv(flat.shape[1], lanes)
        flat = jnp.pad(flat, ((0, 0), (0, tiles * lanes - flat.shape[1])))
        joined = jnp.concatenate(
            [flat.reshape(hosts, tiles, lanes), jnp.where(order > here, edges[0], edges[1])], axis=1
        )
        joined = lax.all_to_all(joined, "macro", 0, 0, tiled=True)
        flat = joined[:, :tiles].reshape(hosts, -1)[:, : ROWS * capacity]
        result = flat.reshape(hosts, ROWS, capacity).transpose(1, 0, 2).reshape(ROWS, slots)
        low = lax.dynamic_index_in_dim(joined, jnp.maximum(here - 1, 0), 0, False)
        high = lax.dynamic_index_in_dim(joined, jnp.minimum(here + 1, hosts - 1), 0, False)
        answered = [result, jnp.stack([low[tiles:], high[tiles:]])]

    elastic = call(
        functools.partial(elastic_kernel, hosts, capacity),
        "elastic_forces",
        [shape_of(motion.shape), shape_of((7, 16, size_z)), shape_of((8, points), jnp.int32)],
        (motion, stiffness, elem, owner, first, second),
        [
            VMEM((3, size_x, 16, size_z), F32),
            VMEM((size_x, 16, size_z), F32),
            VMEM((6, size_x + 1, 16, size_z), F32),
        ],
    )

    force, tangent = call(
        functools.partial(final_kernel, packed, hosts, capacity),
        "final_forces",
        [shape_of(motion.shape), shape_of((36, points))],
        (*answered, x_second, x_first, *elastic),
        [
            VMEM((ROWS, points), F32),
            VMEM((3, 4, 16, size_z), F32),
            VMEM((2, 16, size_z), F32),
            VMEM((6, size_x + 1, 16, size_z), F32),
        ],
    )
    return (force, tangent)


def solution(mesh):
    return jax.shard_map(
        on_device,
        mesh=mesh,
        in_specs=(
            P(None, "macro", "micro", None),
            P("macro", "micro", None),
            P(("macro", "micro")),
            P(("macro", "micro")),
            P(("macro", "micro")),
            P(None, ("macro", "micro")),
            P("macro", None, None),
            P(),
            P(),
            P(),
        ),
        out_specs=(P(None, "macro", "micro", None), P(None, ("macro", "micro"))),
        check_vma=False,
    )
```

```python
import functools

import jax
import jax.numpy as jnp
from jax import lax
from jax.experimental import pallas as pl
from jax.experimental.pallas import tpu as pltpu
from jax.sharding import PartitionSpec as P

YIELD_STRESS = 1.5
HARDENING = 0.2
F32 = jnp.float32
BF16 = jnp.bfloat16
VMEM = pltpu.VMEM
ROWS = 32
UPPER = [(i, j) for i in range(6) for j in range(i, 6)]


def whole(*arrays):
    return [pl.BlockSpec(value.shape, lambda s, n=len(value.shape): (0,) * n) for value in arrays]


def in_hbm(value):
    return pltpu.with_memory_space_constraint(value, pltpu.HBM)


def iota(shape, dim):
    return lax.broadcasted_iota(jnp.int32, shape, dim)


def dot_t(left, right):
    return lax.dot_general(left, right, (((1,), (1,)), ((), ())), preferred_element_type=F32)


def pieces(value, count):
    out = []
    for _ in range(count):
        piece = value.astype(BF16)
        out.append(piece)
        value = value - piece.astype(F32)
    return out


def next_z(field):
    last = field.ndim - 1
    size = field.shape[last]
    rolled = pltpu.roll(field, size - 1, last)
    return jnp.where(iota(field.shape, last) == size - 1, 0.0, rolled)


def previous_z(field):
    last = field.ndim - 1
    rolled = pltpu.roll(field, 1, last)
    return jnp.where(iota(field.shape, last) == 0, 0.0, rolled)


def corners(field):
    y_up = pltpu.roll(field, field.shape[1] - 1, 1)
    return [field, y_up, next_z(field), next_z(y_up)]


def strains(lower, upper):
    grads = []
    for low, high in zip(lower, upper):
        dx = [b - a for a, b in zip(low, high)]
        grad_x = (dx[0] + dx[1] + dx[2] + dx[3]) * 0.25
        dy = [value[1] - value[0] for value in (low, high)]
        dy_z = [value[3] - value[2] for value in (low, high)]
        grad_y = (dy[0] + dy[1] + dy_z[0] + dy_z[1]) * 0.25
        dz = [value[2] - value[0] for value in (low, high)]
        dz_y = [value[3] - value[1] for value in (low, high)]
        grad_z = (dz[0] + dz[1] + dz_y[0] + dz_y[1]) * 0.25
        grads.append((grad_x, grad_y, grad_z))
    return [
        grads[0][0],
        grads[1][1],
        grads[2][2],
        grads[1][2] + grads[2][1],
        grads[0][2] + grads[2][0],
        grads[0][1] + grads[1][0],
    ]


def block_strains(fields):
    nodes = [corners(field) for field in fields]
    return strains(
        [[value[:-1] for value in four] for four in nodes],
        [[value[1:] for value in four] for four in nodes],
    )


def elastic_of(strain, stiffness):
    volume = strain[0] + strain[1] + strain[2]
    rest = volume - volume * (1.0 / 3.0)
    normal = [stiffness * (rest + strain[c]) for c in range(3)]
    return normal + [stiffness * (0.5 * strain[c]) for c in range(3, 6)]


def slots_of(owner, hosts, capacity):
    points = owner.shape[1]
    chosen = iota((hosts, points), 0) == owner
    host_hot = jnp.where(chosen, 1.0, 0.0)
    before = jnp.where(iota((points, points), 0) < iota((points, points), 1), 1.0, 0.0)
    counts = jnp.dot(host_hot.astype(BF16), before.astype(BF16), preferred_element_type=F32)
    position = jnp.sum(host_hot * counts, axis=0, keepdims=True).astype(jnp.int32)
    return host_hot, position, owner * capacity + position


def dispatch_kernel(hosts, capacity, direct, *refs):
    inputs, basis_ref, payload_out, refs = refs[:7], refs[7], refs[8], list(refs[9:])
    ids_ref = None if direct else refs.pop(0)
    first_ref, second_ref, x_first_ref, x_second_ref, blocks_ref = refs[:5]
    buffers, payload_ref, sems = refs[5:12], refs[12], refs[13]
    arrivals = [
        pltpu.make_async_copy(value, buffer, sems.at[n])
        for n, (value, buffer) in enumerate(zip(inputs, buffers))
    ]
    for copy in arrivals:
        copy.start()
    kept, _, wide, _ = blocks_ref.shape
    later = [
        pltpu.make_async_copy(
            basis_ref.at[:, pl.ds(n * wide, wide), :], blocks_ref.at[n], sems.at[8 + n]
        )
        for n in range(kept)
    ]
    for copy in later:
        copy.start()
    owner_ref, elem_ref, motion_ref, map_ref, history_ref, pattern_ref, stiff_ref = buffers
    size_x, size_y, size_z = motion_ref.shape[1:]
    arrivals[0].wait()
    owner = owner_ref[...]
    points = owner.shape[1]
    host_hot, position, slot = slots_of(owner, hosts, capacity)
    slot_total = hosts * capacity
    slot_hot = jnp.where(iota((slot_total, points), 0) == slot, 1.0, 0.0).astype(BF16)
    arrivals[1].wait()
    elem = elem_ref[...]
    column = elem // size_z
    depth = elem - column * size_z
    depth_hot = jnp.where(iota((size_z, points), 0) == depth, 1.0, 0.0).astype(BF16)
    rows = (size_x - 1) * size_y
    column_hot = iota((rows, points), 0) == column
    arrivals[2].wait()
    strain = block_strains([motion_ref[m] for m in range(3)])
    field = jnp.concatenate([value.reshape(rows, size_z) for value in strain], axis=0)
    picked = jnp.dot(field.astype(BF16), depth_hot, preferred_element_type=F32)
    macro_strain = jnp.concatenate(
        [
            jnp.sum(
                jnp.where(column_hot, picked[c * rows : (c + 1) * rows], 0.0),
                axis=0,
                keepdims=True,
            )
            for c in range(6)
        ],
        axis=0,
    ).astype(BF16)
    for copy in arrivals[3:]:
        copy.wait()
    mapped = lax.dot_general(
        map_ref[...], macro_strain, (((0,), (0,)), ((), ())), preferred_element_type=F32
    )
    coefficients = (mapped + history_ref[...].astype(F32)).astype(BF16)
    sent = dot_t(slot_hot, coefficients).astype(BF16)
    place = position + lax.axis_index("macro") * capacity
    modes = sent.shape[1]
    half = modes // 2
    place_hot = jnp.where(iota((modes, points), 0) == place, 1.0, 0.0).astype(BF16)
    ids = dot_t((host_hot * pattern_ref[...].astype(F32)).astype(BF16), place_hot)
    if direct:
        for h in range(hosts):
            mine = sent[h * capacity : (h + 1) * capacity]
            payload_ref[h, :capacity, :] = mine[:, :half]
            payload_ref[h, capacity : 2 * capacity, :] = mine[:, half:]
            row = iota((8, half), 0)
            low, high = ids[h : h + 1, :half], ids[h : h + 1, half:]
            tile = jnp.where(row == 0, low, jnp.where(row == 1, high, 0.0))
            payload_ref[h, 2 * capacity :, :] = tile.astype(BF16)
    else:
        payload_ref[...] = sent
        ids_ref[...] = ids.astype(BF16)
    leave = pltpu.make_async_copy(payload_ref, payload_out, sems.at[7])
    leave.start()
    stiffness = stiff_ref[...].astype(F32)
    even = lax.rem(lax.axis_index("micro"), 2) == 0
    for i in range(size_x):
        for m in range(4):
            if m < 3:
                up, down = motion_ref[m, i, size_y - 1 : size_y, :], motion_ref[m, i, 0:1, :]
            else:
                up = down = stiffness[i, size_y - 1 : size_y, :]
            first_ref[m, i : i + 1, :] = jnp.where(even, up, down)
            second_ref[m, i : i + 1, :] = jnp.where(even, down, up)
    even = lax.rem(lax.axis_index("macro"), 2) == 0
    for m in range(4):
        if m < 3:
            up, down = motion_ref[m, size_x - 1], motion_ref[m, 0]
        else:
            up = down = stiffness[size_x - 1]
        x_first_ref[m] = jnp.where(even, up, down)
        x_second_ref[m] = jnp.where(even, down, up)
    leave.wait()
    for copy in later:
        copy.wait()


def table_kernel(
    map_ref,
    weights_ref,
    patterns_ref,
    blocks_ref,
    basis_ref,
    table_ref,
    const_ref,
    column_ref,
    bits_ref,
    others_ref,
    sems,
):
    hyper = weights_ref.shape[1]
    lanes = 128
    kept, _, wide, modes = blocks_ref.shape
    count = hyper // wide
    copies = []
    for n in range(kept, count):
        copy = pltpu.make_async_copy(
            basis_ref.at[:, pl.ds(n * wide, wide), :], others_ref.at[n - kept], sems.at[n - kept]
        )
        copy.start()
        copies.append(copy)
    weights = weights_ref[...]
    split = [piece.astype(F32) for piece in pieces(weights, 3)]
    row = iota((8, hyper), 0)
    stack = jnp.where(
        row == 0, split[0], jnp.where(row == 1, split[1], jnp.where(row == 2, split[2], 0.0))
    )
    column_ref[...] = lax.dot_general(
        stack.astype(BF16),
        jnp.ones((8, lanes), BF16),
        (((0,), (0,)), ((), ())),
        preferred_element_type=F32,
    )
    patterns = patterns_ref[...]
    words, total = patterns.shape
    parts = [((patterns >> (8 * k)) & 255).astype(F32) for k in range(4)]
    spare = -4 * words % 8
    parts = jnp.concatenate(parts + [jnp.zeros((spare, total), F32)] * (spare > 0), axis=0)
    parts = jnp.concatenate([parts, jnp.zeros((parts.shape[0], lanes - total), F32)], axis=1)
    place = iota((1, 4 * words + spare), 1)
    part = jnp.where(place >= words, 1, 0) + jnp.where(place >= 2 * words, 1, 0)
    part = part + jnp.where(place >= 3 * words, 1, 0)
    start = 30 * (place - words * part) + 8 * part
    size = jnp.where(part == 3, 6, 8)
    after = iota((hyper, 4 * words + spare), 0) - start
    byte_hot = jnp.where((after >= 0) & (after < size), 1.0, 0.0).astype(BF16)
    value = jnp.dot(byte_hot, parts.astype(BF16), preferred_element_type=F32).astype(jnp.int32)
    index = iota((hyper, lanes), 0)
    offset = index - 30 * ((index * 2185) >> 16)
    bits_ref[...] = ((value >> (offset & 7)) & 1).astype(F32).astype(BF16)

    modes_map = map_ref[...]
    modes_map = jnp.concatenate(
        [modes_map.astype(F32), jnp.zeros((2, modes), F32)], axis=0
    ).astype(BF16)
    sums = jnp.zeros((48, wide), F32)
    for n in range(count):
        if n >= kept:
            copies[n - kept].wait()
        source = blocks_ref.at[n] if n < kept else others_ref.at[n - kept]
        part = slice(n * wide, (n + 1) * wide)
        local = [dot_t(modes_map, source[c]) for c in range(6)]
        trace = local[0] + local[1] + local[2]
        third = trace / 3.0
        shaped = [local[c] - third for c in range(3)] + [0.5 * local[c] for c in range(3, 6)]
        weight = weights[:, part]
        shaped = [weight * value for value in shaped]
        weighted_trace = weight * trace
        blocks, adds = [], []
        for i in range(6):
            entry = local[0][i : i + 1] * shaped[0]
            for c in range(1, 6):
                entry = entry + local[c][i : i + 1] * shaped[c]
            blocks.append(entry)
            adds.append(entry + trace[i : i + 1] * weighted_trace)
        sums = sums + jnp.concatenate(adds, axis=0)
        high, low = pieces(jnp.concatenate(blocks, axis=0), 2)
        table_ref[0:48, part] = high
        table_ref[48:96, part] = low
    const_ref[...] = jnp.broadcast_to(jnp.sum(sums, axis=1, keepdims=True), const_ref.shape)


def sides_of(first_ref, second_ref, axis, m, at=None):
    even = lax.rem(lax.axis_index(axis), 2) == 0
    rows = slice(None) if at is None else slice(at, at + 1)
    first, second = first_ref[m, rows, :], second_ref[m, rows, :]
    return jnp.where(even, second, first), jnp.where(even, first, second)


def micro_kernel(
    packed,
    hosts,
    capacity,
    received_ref,
    first_ref,
    second_ref,
    const_ref,
    bits_ref,
    column_ref,
    table_ref,
    blocks_ref,
    basis_ref,
    answer_ref,
    *rest,
):
    if packed:
        corners_ref = None
    else:
        corners_ref, *rest = rest
    (
        state_ref,
        hot_ref,
        others_ref,
        flags_ref,
        high_ref,
        low_ref,
        result_ref,
        sems,
    ) = rest
    groups = received_ref.shape[0]
    slots = groups * capacity
    kept, _, block, modes = blocks_ref.shape
    half = modes // 2
    count = kept + others_ref.shape[0]
    copies = []
    for n in range(count - kept):
        part = pl.ds((kept + n) * block, block)
        copies.append(
            pltpu.make_async_copy(basis_ref.at[:, part, :], others_ref.at[n], sems.at[n])
        )
        copies[n].start()

    ids = jnp.zeros((8, half), F32)
    for h in range(groups):
        own = pl.ds(h * capacity, capacity)
        state_ref[own, :half] = received_ref[h, :capacity, :]
        state_ref[own, half:] = received_ref[h, capacity : 2 * capacity, :]
        ids = ids + received_ref[h, 2 * capacity :, :].astype(F32)
    ids = jnp.concatenate([ids[0:1], ids[1:2]], axis=1).astype(jnp.int32)
    hot_ref[...] = jnp.where(iota(hot_ref.shape, 0) == ids, 1.0, 0.0).astype(BF16)

    def solve(*accumulators):
        mains, spares = accumulators[:8], accumulators[8:12]
        tangent_high, tangent_low = accumulators[12:]
        hyper = bits_ref.shape[0]
        both = range(2)
        for unit in both:
            pltpu.matmul_push_rhs(hot_ref[...], 0, unit)
        empty = jnp.zeros((128, modes - bits_ref.shape[1]), BF16)

        def flags_of(j):
            rows = jnp.concatenate([bits_ref[128 * j : 128 * j + 128, :], empty], axis=1)
            pltpu.matmul_acc_lhs(spares[j % 4], rows, load_staged_rhs=0 if j < 2 else None)

        blocks_of_flags = hyper // 128
        for j in range(blocks_of_flags + 2):
            if j < blocks_of_flags:
                flags_of(j)
            if j >= 2:
                flags_ref[128 * (j - 2) : 128 * (j - 1), :] = pltpu.matmul_pop(spares[(j - 2) % 4])
        for unit in both:
            pltpu.matmul_push_rhs(state_ref[...], 0, unit, transpose=True)
        strip = 16
        strips = hyper // strip

        def issue(i):
            n, r = divmod(i * strip, block)
            if n >= kept and r == 0:
                copies[n - kept].wait()
            source = blocks_ref.at[n] if n < kept else others_ref.at[n - kept]
            rows = jnp.concatenate([source[c, r : r + strip, :] for c in range(6)], axis=0)
            pltpu.matmul_acc_lhs(mains[i % 8], rows, load_staged_rhs=0 if i < 2 else None)

        def respond(i, sums):
            strain = pltpu.matmul_pop(mains[i % 8])
            e = [strain[c * strip : (c + 1) * strip] for c in range(6)]
            at = slice(i * strip, (i + 1) * strip)
            volume = e[0] + e[1] + e[2]
            third = volume * (1.0 / 3.0)
            d = [e[c] - third for c in range(3)]
            normal = d[0] * d[0] + d[1] * d[1] + d[2] * d[2]
            shear = e[3] * e[3] + e[4] * e[4] + e[5] * e[5]
            square = jnp.maximum(normal + 0.5 * shear, YIELD_STRESS * YIELD_STRESS)
            factor = (YIELD_STRESS * (1.0 - HARDENING)) * lax.rsqrt(square) + (HARDENING - 1.0)
            change = flags_ref[at, :] * factor
            high = change.astype(BF16)
            high_ref[at, :] = high
            low_ref[at, :] = (change - high.astype(F32)).astype(BF16)
            column = column_ref[at, :]
            weight = jnp.concatenate([column] * (slots // column.shape[1]), axis=1)
            scaled = weight + weight * change
            terms = [scaled * d[c] for c in range(3)] + [scaled * e[c] for c in range(3, 6)]
            terms.append(weight * volume)
            return [total + (term[:8] + term[8:]) for total, term in zip(sums, terms)]

        sums = [jnp.zeros((8, slots), F32)] * 7
        ahead = 7
        for i in range(ahead):
            issue(i)
        for i in range(strips):
            if i + ahead < strips:
                issue(i + ahead)
            sums = respond(i, sums)
        for n in range(hyper // modes):
            part = slice(n * modes, (n + 1) * modes)
            pltpu.matmul_push_rhs(high_ref[part, :], 0, 0)
            pltpu.matmul_push_rhs(low_ref[part, :], 0, 1)
            pltpu.matmul_acc_lhs(tangent_high, table_ref[:, part], load_staged_rhs=0)
            pltpu.matmul_acc_lhs(tangent_low, table_ref[0:48, part], load_staged_rhs=0)
        both_parts = pltpu.matmul_pop(tangent_high)
        tangent = both_parts[:48] + (both_parts[48:] + pltpu.matmul_pop(tangent_low))
        return tangent, sums

    tangent, sums = pl.run_scoped(
        solve,
        *[pltpu.ACC(n % 2)((96, slots), F32) for n in range(8)],
        *[pltpu.ACC(n % 2)((128, slots), F32) for n in range(4)],
        pltpu.ACC(0)((96, slots), F32),
        pltpu.ACC(1)((48, slots), F32),
    )

    volume = jnp.sum(sums[6], axis=0, keepdims=True)
    for c in range(6):
        total = jnp.sum(sums[c], axis=0, keepdims=True)
        result_ref[c : c + 1, :] = total + volume if c < 3 else 0.5 * total
    const = const_ref[...]
    const = jnp.concatenate([const] * (slots // const.shape[1]), axis=1)
    tangent = tangent + const
    at = 6
    for i in range(6):
        result_ref[at : at + 6 - i, :] = tangent[8 * i + i : 8 * i + 6]
        at += 6 - i
    result_ref[at:, :] = jnp.zeros((ROWS - at, slots), F32)

    last = first_ref.shape[1] - 1

    def corner_rows(write):
        for m in range(4):
            up = sides_of(first_ref, second_ref, "micro", m, last)
            down = sides_of(first_ref, second_ref, "micro", m, 0)
            for n in range(2):
                write(0, 2 * m + n, up[n])
                write(1, 2 * m + n, down[n])

    if packed:
        here = lax.axis_index("macro")
        group_of = iota((8, 128), 1) // capacity
        for h in range(hosts):
            chunk = jnp.zeros((8, 128), F32)
            tile, place = divmod(h * capacity, 128)
            for g in range(4):
                piece = result_ref[8 * g : 8 * g + 8, tile * 128 : (tile + 1) * 128]
                shift = (g * capacity - place) % 128
                if shift:
                    piece = pltpu.roll(piece, shift, 1)
                chunk = jnp.where(group_of == g, piece, chunk)
            answer_ref[h, 0:8, :] = chunk
        chunks = [jnp.minimum(here + 1, hosts - 1), jnp.maximum(here - 1, 0)]

        def write(side, row, value):
            answer_ref[chunks[side], 8 + row : 9 + row, :] = value
    else:
        answer_ref[...] = result_ref[...]

        def write(side, row, value):
            corners_ref[side, row : row + 1, :] = value

    corner_rows(write)


def assemble(stress):
    ready = []
    for here, low in stress:
        ready.append((here, low, previous_z(here), previous_z(low)))

    def at(c, sign_x, sign_y, sign_z):
        here, low, here_z, low_z = ready[c]
        if sign_z:
            near, far = here_z - here, low_z - low
        else:
            near, far = here_z + here, low_z + low
        both = far - near if sign_y else far + near
        return both[:-1] - both[1:] if sign_x else both[:-1] + both[1:]

    force = [
        at(0, 1, 0, 0) + at(5, 0, 1, 0) + at(4, 0, 0, 1),
        at(5, 1, 0, 0) + at(1, 0, 1, 0) + at(3, 0, 0, 1),
        at(4, 1, 0, 0) + at(3, 0, 1, 0) + at(2, 0, 0, 1),
    ]
    return [0.25 * value for value in force]


def elastic_kernel(
    hosts,
    capacity,
    motion_ref,
    stiff_ref,
    elem_ref,
    owner_ref,
    first_ref,
    second_ref,
    force_ref,
    edge_ref,
    index_ref,
    node_ref,
    wide_ref,
    stress_ref,
):
    size_x, size_y, size_z = motion_ref.shape[1:]
    node_ref[...] = jnp.zeros_like(node_ref)
    wide_ref[...] = jnp.zeros_like(wide_ref)
    stiffness = stiff_ref[...].astype(F32)
    elem, owner = elem_ref[...], owner_ref[...]
    points = elem.shape[1]
    column = elem // size_z
    depth = elem - column * size_z
    index_ref[0:1, :] = slots_of(owner, hosts, capacity)[2]
    index_ref[1:2, :] = column
    index_ref[2:3, :] = depth
    index_ref[3:, :] = jnp.zeros((5, points), jnp.int32)
    depth_hot = jnp.where(iota((size_z, points), 0) == depth, 1.0, 0.0).astype(BF16)
    column_hot = jnp.where(iota((size_x * size_y, points), 0) == column, 1.0, 0.0).astype(BF16)
    listed = dot_t(column_hot, depth_hot)
    for i in range(size_x):
        for m in range(3):
            low, high = sides_of(first_ref, second_ref, "micro", m, i)
            node_ref[m, i, 0:1, :] = low
            node_ref[m, i, 1 : size_y + 1, :] = motion_ref[m, i]
            node_ref[m, i, size_y + 1 : size_y + 2, :] = high
        low, _ = sides_of(first_ref, second_ref, "micro", 3, i)
        wide_ref[i, 0:1, :] = low
        keep = 1.0 - listed[i * size_y : (i + 1) * size_y]
        wide_ref[i, 1 : size_y + 1, :] = stiffness[i] * keep
    for m in range(3):
        edge_ref[m] = node_ref[m, 0]
        edge_ref[3 + m] = node_ref[m, size_x - 1]
    edge_ref[6] = wide_ref[size_x - 1]
    strain = block_strains([node_ref[m] for m in range(3)])
    stress = elastic_of(strain, wide_ref[: size_x - 1])
    for c in range(6):
        stress_ref[c, 0] = jnp.zeros(stress_ref.shape[2:], F32)
        stress_ref[c, 1:size_x] = stress[c]
        stress_ref[c, size_x] = jnp.zeros(stress_ref.shape[2:], F32)
    force = assemble(
        [(stress_ref[c, :, 1 : size_y + 1, :], stress_ref[c, :, 0:size_y, :]) for c in range(6)]
    )
    for m in range(3):
        force_ref[m] = force[m]


def final_kernel(packed, hosts, capacity, answer_ref, *rest):
    if packed:
        corners_ref = None
    else:
        corners_ref, *rest = rest
    (
        second_ref,
        first_ref,
        elastic_ref,
        edge_ref,
        index_ref,
        force_ref,
        tangent_ref,
        result_ref,
        node_ref,
        wide_ref,
        stress_ref,
    ) = rest
    size_x, size_y, size_z = elastic_ref.shape[1:]
    slot, column, depth = index_ref[0:1, :], index_ref[1:2, :], index_ref[2:3, :]
    points = slot.shape[1]
    slot_total = hosts * capacity
    if packed:
        group_of = iota((8, 128), 1) // capacity
        per_tile = 128 // capacity
        groups = []
        for g in range(4):
            tiles = []
            for t in range(hosts // per_tile):
                tile = jnp.zeros((8, 128), F32)
                for n in range(per_tile):
                    piece = answer_ref[t * per_tile + n, 0:8, :]
                    shift = ((n - g) * capacity) % 128
                    if shift:
                        piece = pltpu.roll(piece, shift, 1)
                    tile = jnp.where(group_of == n, piece, tile)
                tiles.append(tile)
            groups.append(jnp.concatenate(tiles, axis=1))
        answer = jnp.concatenate(groups, axis=0)
    else:
        answer = answer_ref[...]
    slot_hot = jnp.where(iota((slot_total, points), 0) == slot, 1.0, 0.0).astype(BF16)
    parts = jnp.concatenate(pieces(answer, 3), axis=0)
    chosen = jnp.dot(parts, slot_hot, preferred_element_type=F32)
    result = chosen[:ROWS] + (chosen[ROWS : 2 * ROWS] + chosen[2 * ROWS :])
    result_ref[...] = result
    for i in range(6):
        for j in range(6):
            at = 6 + UPPER.index((min(i, j), max(i, j)))
            tangent_ref[6 * i + j : 6 * i + j + 1, :] = result_ref[at : at + 1, :]

    here = lax.axis_index("macro")
    inner = [here > 0, here < hosts - 1]
    from_chunk = [jnp.maximum(here - 1, 0), jnp.minimum(here + 1, hosts - 1)]

    def corner(side, row):
        if packed:
            value = answer_ref[from_chunk[side], 8 + row : 9 + row, :]
        else:
            value = corners_ref[side, row : row + 1, :]
        return jnp.where(inner[side], value, 0.0)

    node_ref[...] = jnp.zeros_like(node_ref)
    wide_ref[...] = jnp.zeros_like(wide_ref)
    for m in range(3):
        faces = sides_of(first_ref, second_ref, "macro", m)
        for side, at in ((0, 0), (1, 3)):
            node_ref[m, at, 0:1, :] = corner(side, 2 * m)
            node_ref[m, at, 1 : size_y + 1, :] = faces[side]
            node_ref[m, at, size_y + 1 : size_y + 2, :] = corner(side, 2 * m + 1)
        node_ref[m, 1] = edge_ref[m]
        node_ref[m, 2] = edge_ref[3 + m]
    wide_ref[0, 0:1, :] = corner(0, 6)
    wide_ref[0, 1 : size_y + 1, :] = sides_of(first_ref, second_ref, "macro", 3)[0]
    wide_ref[1] = edge_ref[6]
    lower, upper = [], []
    for m in range(3):
        four = corners(node_ref[m])
        lower.append([jnp.stack([value[0], value[2]]) for value in four])
        upper.append([jnp.stack([value[1], value[3]]) for value in four])
    edge = elastic_of(strains(lower, upper), wide_ref[...])
    rows = (size_x - 1) * size_y
    depth_hot = jnp.where(iota((size_z, points), 0) == depth, 1.0, 0.0).astype(BF16)
    column_hot = iota((rows, points), 0) == column
    stress_ref[:, 1:size_x, 0:1, :] = jnp.zeros((6, size_x - 1, 1, size_z), F32)
    placed = [jnp.where(column_hot, result[c : c + 1], 0.0) for c in range(6)]
    placed = jnp.concatenate(pieces(jnp.concatenate(placed, axis=0), 2), axis=0)
    fields = dot_t(placed, depth_hot)
    for c in range(6):
        field = fields[c * rows : (c + 1) * rows] + fields[(6 + c) * rows : (7 + c) * rows]
        stress_ref[c, 1:size_x, 1 : size_y + 1, :] = field.reshape(size_x - 1, size_y, size_z)
        stress_ref[c, 0] = edge[c][0]
        stress_ref[c, size_x] = edge[c][1]
    force = assemble(
        [(stress_ref[c, :, 1 : size_y + 1, :], stress_ref[c, :, 0:size_y, :]) for c in range(6)]
    )
    for m in range(3):
        force_ref[m] = elastic_ref[m] + force[m]


def shape_of(shape, dtype=F32):
    return jax.ShapeDtypeStruct(shape, dtype)


def call(kernel, name, out_shape, args, scratch=(), flops=10**8, raw=0, raw_out=0):
    specs = whole(*args[: len(args) - raw]) + [pl.BlockSpec(memory_space=pl.ANY)] * raw
    return pl.pallas_call(
        kernel,
        grid=(1,),
        out_shape=out_shape,
        in_specs=specs,
        out_specs=[pl.BlockSpec(memory_space=pl.ANY)] * raw_out + whole(*out_shape[raw_out:]),
        scratch_shapes=scratch,
        compiler_params=pltpu.CompilerParams(vmem_limit_bytes=24 * 2**20),
        cost_estimate=pl.CostEstimate(flops=flops, bytes_accessed=2**20, transcendentals=0),
        name=name,
    )(*args)


def on_device(
    motion,
    stiffness,
    point_elem,
    point_owner,
    point_pattern,
    history,
    basis,
    mode_map,
    weights,
    patterns,
):
    size_x, size_y, size_z = motion.shape[1:]
    points = point_elem.shape[0]
    hosts = lax.axis_size("macro")
    capacity = 2 * points // hosts
    slots = capacity * hosts
    modes = mode_map.shape[0]
    half = modes // 2
    hyper = weights.shape[0]
    lanes = 128
    direct = capacity % 16 == 0
    packed = capacity * 4 == lanes and slots % lanes == 0
    motion = in_hbm(motion)
    stiffness = in_hbm(stiffness)
    elem = in_hbm(point_elem.reshape(1, points))
    owner = in_hbm(point_owner.reshape(1, points))
    pattern = in_hbm(point_pattern.reshape(1, points))
    history = in_hbm(history)
    map_rows = in_hbm(mode_map.T)

    rows = in_hbm(basis.reshape(6, hyper, modes))
    wide, kept = 256, 2
    sent = (
        [shape_of((hosts, 2 * capacity + 8, half), BF16)]
        if direct
        else [shape_of((slots, modes), BF16), shape_of((hosts, modes), BF16)]
    )
    swap, x_swap = shape_of((4, size_x, size_z)), shape_of((4, size_y, size_z))
    arguments = (owner, elem, motion, map_rows, history, pattern, stiffness)
    *payload, first, second, x_first, x_second, blocks = call(
        functools.partial(dispatch_kernel, hosts, capacity, direct),
        "dispatch",
        sent + [swap, swap, x_swap, x_swap, shape_of((kept, 6, wide, modes), BF16)],
        (*arguments, rows),
        [VMEM(value.shape, value.dtype) for value in (*arguments, sent[0])]
        + [pltpu.SemaphoreType.DMA((8 + kept,))],
        raw=8,
        raw_out=1,
    )

    if direct:
        received = lax.all_to_all(payload[0], "macro", 0, 0, tiled=True)
        groups, group = hosts, capacity
    else:
        slot_rows, ids = payload
        joined = jnp.concatenate(
            [
                slot_rows[:, :half].reshape(hosts, capacity, half),
                slot_rows[:, half:].reshape(hosts, capacity, half),
                ids.reshape(hosts, 2, half),
            ],
            axis=1,
        )
        joined = lax.all_to_all(joined, "macro", 0, 0, tiled=True)
        ids = jnp.sum(joined[:, 2 * capacity :].astype(F32), axis=0).astype(BF16)
        received = jnp.concatenate(
            [
                joined[:, :capacity].reshape(1, slots, half),
                joined[:, capacity : 2 * capacity].reshape(1, slots, half),
                jnp.pad(ids, ((0, 6), (0, 0)))[None],
            ],
            axis=1,
        )
        groups, group = 1, slots

    def swapped(value, axis, start):
        pairs = [(i, i + 1) for i in range(start, lax.axis_size(axis) - 1, 2)]
        return lax.ppermute(value, axis, pairs + [(b, a) for a, b in pairs])

    first, second = swapped(first, "micro", 0), swapped(second, "micro", 1)
    x_first, x_second = swapped(x_first, "macro", 0), swapped(x_second, "macro", 1)

    table, const, column, bits = call(
        table_kernel,
        "tables",
        [
            shape_of((96, hyper), BF16),
            shape_of((48, lanes)),
            shape_of((hyper, lanes)),
            shape_of((hyper, lanes), BF16),
        ],
        (map_rows, in_hbm(weights.reshape(1, hyper)), in_hbm(patterns.T), blocks, rows),
        [
            VMEM((hyper // wide - kept, 6, wide, modes), BF16),
            pltpu.SemaphoreType.DMA((hyper // wide - kept,)),
        ],
        raw=1,
    )

    answer = call(
        functools.partial(micro_kernel, packed, hosts, group),
        "micro_response",
        [shape_of((hosts, 16, lanes))]
        if packed
        else [shape_of((ROWS, slots)), shape_of((2, 8, lanes))],
        (
            received,
            first,
            second,
            const,
            bits,
            column,
            table,
            blocks,
            rows,
        ),
        [
            VMEM((slots, modes), BF16),
            VMEM((modes, slots), BF16),
            VMEM((hyper // wide - kept, 6, wide, modes), BF16),
            VMEM((hyper, slots), F32),
            *[VMEM((hyper, slots), BF16)] * 2,
            VMEM((ROWS, slots), F32),
            pltpu.SemaphoreType.DMA((hyper // wide - kept,)),
        ],
        raw=1,
    )

    if packed:
        answered = [lax.all_to_all(answer[0], "macro", 0, 0, tiled=True)]
    else:
        result, edges = answer
        here = lax.axis_index("macro")
        order = jnp.arange(hosts)[:, None, None]
        flat = result.reshape(ROWS, hosts, capacity).transpose(1, 0, 2).reshape(hosts, -1)
        tiles = pl.cdiv(flat.shape[1], lanes)
        flat = jnp.pad(flat, ((0, 0), (0, tiles * lanes - flat.shape[1])))
        joined = jnp.concatenate(
            [flat.reshape(hosts, tiles, lanes), jnp.where(order > here, edges[0], edges[1])], axis=1
        )
        joined = lax.all_to_all(joined, "macro", 0, 0, tiled=True)
        flat = joined[:, :tiles].reshape(hosts, -1)[:, : ROWS * capacity]
        result = flat.reshape(hosts, ROWS, capacity).transpose(1, 0, 2).reshape(ROWS, slots)
        low = lax.dynamic_index_in_dim(joined, jnp.maximum(here - 1, 0), 0, False)
        high = lax.dynamic_index_in_dim(joined, jnp.minimum(here + 1, hosts - 1), 0, False)
        answered = [result, jnp.stack([low[tiles:], high[tiles:]])]

    elastic = call(
        functools.partial(elastic_kernel, hosts, capacity),
        "elastic_forces",
        [shape_of(motion.shape), shape_of((7, 16, size_z)), shape_of((8, points), jnp.int32)],
        (motion, stiffness, elem, owner, first, second),
        [
            VMEM((3, size_x, 16, size_z), F32),
            VMEM((size_x, 16, size_z), F32),
            VMEM((6, size_x + 1, 16, size_z), F32),
        ],
    )

    force, tangent = call(
        functools.partial(final_kernel, packed, hosts, capacity),
        "final_forces",
        [shape_of(motion.shape), shape_of((36, points))],
        (*answered, x_second, x_first, *elastic),
        [
            VMEM((ROWS, points), F32),
            VMEM((3, 4, 16, size_z), F32),
            VMEM((2, 16, size_z), F32),
            VMEM((6, size_x + 1, 16, size_z), F32),
        ],
    )
    return (force, tangent)


def solution(mesh):
    return jax.shard_map(
        on_device,
        mesh=mesh,
        in_specs=(
            P(None, "macro", "micro", None),
            P("macro", "micro", None),
            P(("macro", "micro")),
            P(("macro", "micro")),
            P(("macro", "micro")),
            P(None, ("macro", "micro")),
            P("macro", None, None),
            P(),
            P(),
            P(),
        ),
        out_specs=(P(None, "macro", "micro", None), P(None, ("macro", "micro"))),
        check_vma=False,
    )
```

```python
import functools

import jax
import jax.numpy as jnp
from jax import lax
from jax.experimental import pallas as pl
from jax.experimental.pallas import tpu as pltpu
from jax.sharding import PartitionSpec as P

YIELD_STRESS = 1.5
HARDENING = 0.2
F32 = jnp.float32
BF16 = jnp.bfloat16
VMEM = pltpu.VMEM
ROWS = 32
UPPER = [(i, j) for i in range(6) for j in range(i, 6)]


def whole(*arrays):
    return [pl.BlockSpec(value.shape, lambda s, n=len(value.shape): (0,) * n) for value in arrays]


def in_hbm(value):
    return pltpu.with_memory_space_constraint(value, pltpu.HBM)


def iota(shape, dim):
    return lax.broadcasted_iota(jnp.int32, shape, dim)


def dot_t(left, right):
    return lax.dot_general(left, right, (((1,), (1,)), ((), ())), preferred_element_type=F32)


def pieces(value, count):
    out = []
    for _ in range(count):
        piece = value.astype(BF16)
        out.append(piece)
        value = value - piece.astype(F32)
    return out


def next_z(field):
    last = field.ndim - 1
    size = field.shape[last]
    rolled = pltpu.roll(field, size - 1, last)
    return jnp.where(iota(field.shape, last) == size - 1, 0.0, rolled)


def previous_z(field):
    last = field.ndim - 1
    rolled = pltpu.roll(field, 1, last)
    return jnp.where(iota(field.shape, last) == 0, 0.0, rolled)


def corners(field):
    y_up = pltpu.roll(field, field.shape[1] - 1, 1)
    return [field, y_up, next_z(field), next_z(y_up)]


def strains(lower, upper):
    grads = []
    for low, high in zip(lower, upper):
        dx = [b - a for a, b in zip(low, high)]
        grad_x = (dx[0] + dx[1] + dx[2] + dx[3]) * 0.25
        dy = [value[1] - value[0] for value in (low, high)]
        dy_z = [value[3] - value[2] for value in (low, high)]
        grad_y = (dy[0] + dy[1] + dy_z[0] + dy_z[1]) * 0.25
        dz = [value[2] - value[0] for value in (low, high)]
        dz_y = [value[3] - value[1] for value in (low, high)]
        grad_z = (dz[0] + dz[1] + dz_y[0] + dz_y[1]) * 0.25
        grads.append((grad_x, grad_y, grad_z))
    return [
        grads[0][0],
        grads[1][1],
        grads[2][2],
        grads[1][2] + grads[2][1],
        grads[0][2] + grads[2][0],
        grads[0][1] + grads[1][0],
    ]


def block_strains(fields):
    nodes = [corners(field) for field in fields]
    return strains(
        [[value[:-1] for value in four] for four in nodes],
        [[value[1:] for value in four] for four in nodes],
    )


def elastic_of(strain, stiffness):
    volume = strain[0] + strain[1] + strain[2]
    rest = volume - volume * (1.0 / 3.0)
    normal = [stiffness * (rest + strain[c]) for c in range(3)]
    return normal + [stiffness * (0.5 * strain[c]) for c in range(3, 6)]


def slots_of(owner, hosts, capacity):
    points = owner.shape[1]
    chosen = iota((hosts, points), 0) == owner
    host_hot = jnp.where(chosen, 1.0, 0.0)
    before = jnp.where(iota((points, points), 0) < iota((points, points), 1), 1.0, 0.0)
    counts = jnp.dot(host_hot.astype(BF16), before.astype(BF16), preferred_element_type=F32)
    position = jnp.sum(host_hot * counts, axis=0, keepdims=True).astype(jnp.int32)
    return host_hot, position, owner * capacity + position


def dispatch_kernel(hosts, capacity, direct, *refs):
    inputs, basis_ref, payload_out, refs = refs[:7], refs[7], refs[8], list(refs[9:])
    ids_ref = None if direct else refs.pop(0)
    first_ref, second_ref, x_first_ref, x_second_ref, blocks_ref = refs[:5]
    buffers, payload_ref, sems = refs[5:12], refs[12], refs[13]
    arrivals = [
        pltpu.make_async_copy(value, buffer, sems.at[n])
        for n, (value, buffer) in enumerate(zip(inputs, buffers))
    ]
    for copy in arrivals:
        copy.start()
    kept, _, wide, _ = blocks_ref.shape
    later = [
        pltpu.make_async_copy(
            basis_ref.at[:, pl.ds(n * wide, wide), :], blocks_ref.at[n], sems.at[8 + n]
        )
        for n in range(kept)
    ]
    for copy in later:
        copy.start()
    owner_ref, elem_ref, motion_ref, map_ref, history_ref, pattern_ref, stiff_ref = buffers
    size_x, size_y, size_z = motion_ref.shape[1:]
    for copy in arrivals:
        copy.wait()
    owner = owner_ref[...]
    points = owner.shape[1]
    host_hot, position, slot = slots_of(owner, hosts, capacity)
    slot_total = hosts * capacity
    slot_hot = jnp.where(iota((slot_total, points), 0) == slot, 1.0, 0.0).astype(BF16)
    elem = elem_ref[...]
    column = elem // size_z
    depth = elem - column * size_z
    depth_hot = jnp.where(iota((size_z, points), 0) == depth, 1.0, 0.0).astype(BF16)
    rows = (size_x - 1) * size_y
    column_hot = iota((rows, points), 0) == column
    strain = block_strains([motion_ref[m] for m in range(3)])
    field = jnp.concatenate([value.reshape(rows, size_z) for value in strain], axis=0)
    picked = jnp.dot(field.astype(BF16), depth_hot, preferred_element_type=F32)
    macro_strain = jnp.concatenate(
        [
            jnp.sum(
                jnp.where(column_hot, picked[c * rows : (c + 1) * rows], 0.0),
                axis=0,
                keepdims=True,
            )
            for c in range(6)
        ],
        axis=0,
    ).astype(BF16)
    held = dot_t(slot_hot, history_ref[...])
    slot_strain = dot_t(slot_hot, macro_strain).astype(BF16)
    mapped = jnp.dot(slot_strain, map_ref[...], preferred_element_type=F32)
    sent = (mapped + held).astype(BF16)
    place = position + lax.axis_index("macro") * capacity
    modes = sent.shape[1]
    half = modes // 2
    place_hot = jnp.where(iota((modes, points), 0) == place, 1.0, 0.0).astype(BF16)
    ids = dot_t((host_hot * pattern_ref[...].astype(F32)).astype(BF16), place_hot)
    if direct:
        for h in range(hosts):
            mine = sent[h * capacity : (h + 1) * capacity]
            payload_ref[h, :capacity, :] = mine[:, :half]
            payload_ref[h, capacity : 2 * capacity, :] = mine[:, half:]
            row = iota((8, half), 0)
            low, high = ids[h : h + 1, :half], ids[h : h + 1, half:]
            tile = jnp.where(row == 0, low, jnp.where(row == 1, high, 0.0))
            payload_ref[h, 2 * capacity :, :] = tile.astype(BF16)
    else:
        payload_ref[...] = sent
        ids_ref[...] = ids.astype(BF16)
    leave = pltpu.make_async_copy(payload_ref, payload_out, sems.at[7])
    leave.start()
    stiffness = stiff_ref[...].astype(F32)
    even = lax.rem(lax.axis_index("micro"), 2) == 0
    for i in range(size_x):
        for m in range(4):
            if m < 3:
                up, down = motion_ref[m, i, size_y - 1 : size_y, :], motion_ref[m, i, 0:1, :]
            else:
                up = down = stiffness[i, size_y - 1 : size_y, :]
            first_ref[m, i : i + 1, :] = jnp.where(even, up, down)
            second_ref[m, i : i + 1, :] = jnp.where(even, down, up)
    even = lax.rem(lax.axis_index("macro"), 2) == 0
    for m in range(4):
        if m < 3:
            up, down = motion_ref[m, size_x - 1], motion_ref[m, 0]
        else:
            up = down = stiffness[size_x - 1]
        x_first_ref[m] = jnp.where(even, up, down)
        x_second_ref[m] = jnp.where(even, down, up)
    leave.wait()
    for copy in later:
        copy.wait()


def table_kernel(
    blocks_ref,
    map_in,
    weights_in,
    patterns_in,
    basis_ref,
    table_ref,
    const_ref,
    column_ref,
    bits_ref,
    others_ref,
    map_ref,
    weights_ref,
    patterns_ref,
    sems,
):
    pairs = ((weights_in, weights_ref), (patterns_in, patterns_ref), (map_in, map_ref))
    arrivals = [pltpu.make_async_copy(*pair, sems.at[n]) for n, pair in enumerate(pairs)]
    for copy in arrivals:
        copy.start()
    hyper = weights_ref.shape[1]
    lanes = 128
    kept, _, wide, modes = blocks_ref.shape
    count = hyper // wide
    copies = []
    for n in range(kept, count):
        copy = pltpu.make_async_copy(
            basis_ref.at[:, pl.ds(n * wide, wide), :], others_ref.at[n - kept], sems.at[3 + n - kept]
        )
        copy.start()
        copies.append(copy)
    for copy in arrivals:
        copy.wait()
    weights = weights_ref[...]
    split = [piece.astype(F32) for piece in pieces(weights, 3)]
    row = iota((8, hyper), 0)
    stack = jnp.where(
        row == 0, split[0], jnp.where(row == 1, split[1], jnp.where(row == 2, split[2], 0.0))
    )
    column_ref[...] = lax.dot_general(
        stack.astype(BF16),
        jnp.ones((8, lanes), BF16),
        (((0,), (0,)), ((), ())),
        preferred_element_type=F32,
    )
    patterns = patterns_ref[...]
    words, total = patterns.shape
    parts = [((patterns >> (8 * k)) & 255).astype(F32) for k in range(4)]
    spare = -4 * words % 8
    parts = jnp.concatenate(parts + [jnp.zeros((spare, total), F32)] * (spare > 0), axis=0)
    parts = jnp.concatenate([parts, jnp.zeros((parts.shape[0], lanes - total), F32)], axis=1)
    place = iota((1, 4 * words + spare), 1)
    part = jnp.where(place >= words, 1, 0) + jnp.where(place >= 2 * words, 1, 0)
    part = part + jnp.where(place >= 3 * words, 1, 0)
    start = 30 * (place - words * part) + 8 * part
    size = jnp.where(part == 3, 6, 8)
    after = iota((hyper, 4 * words + spare), 0) - start
    byte_hot = jnp.where((after >= 0) & (after < size), 1.0, 0.0).astype(BF16)
    value = jnp.dot(byte_hot, parts.astype(BF16), preferred_element_type=F32).astype(jnp.int32)
    index = iota((hyper, lanes), 0)
    offset = index - 30 * ((index * 2185) >> 16)
    bits_ref[...] = ((value >> (offset & 7)) & 1).astype(F32).astype(BF16)

    modes_map = map_ref[...]
    modes_map = jnp.concatenate(
        [modes_map.astype(F32), jnp.zeros((2, modes), F32)], axis=0
    ).astype(BF16)
    sums = jnp.zeros((48, wide), F32)
    for n in range(count):
        if n >= kept:
            copies[n - kept].wait()
        source = blocks_ref.at[n] if n < kept else others_ref.at[n - kept]
        part = slice(n * wide, (n + 1) * wide)
        local = [dot_t(modes_map, source[c]) for c in range(6)]
        trace = local[0] + local[1] + local[2]
        third = trace / 3.0
        shaped = [local[c] - third for c in range(3)] + [0.5 * local[c] for c in range(3, 6)]
        weight = weights[:, part]
        shaped = [weight * value for value in shaped]
        weighted_trace = weight * trace
        blocks, adds = [], []
        for i in range(6):
            entry = local[0][i : i + 1] * shaped[0]
            for c in range(1, 6):
                entry = entry + local[c][i : i + 1] * shaped[c]
            blocks.append(entry)
            adds.append(entry + trace[i : i + 1] * weighted_trace)
        sums = sums + jnp.concatenate(adds, axis=0)
        high, low = pieces(jnp.concatenate(blocks, axis=0), 2)
        table_ref[0:48, part] = high
        table_ref[48:96, part] = low
    const_ref[...] = jnp.broadcast_to(jnp.sum(sums, axis=1, keepdims=True), const_ref.shape)


def sides_of(first_ref, second_ref, axis, m, at=None):
    even = lax.rem(lax.axis_index(axis), 2) == 0
    rows = slice(None) if at is None else slice(at, at + 1)
    first, second = first_ref[m, rows, :], second_ref[m, rows, :]
    return jnp.where(even, second, first), jnp.where(even, first, second)


def micro_kernel(
    packed,
    hosts,
    capacity,
    received_ref,
    first_ref,
    second_ref,
    const_ref,
    bits_ref,
    column_ref,
    table_ref,
    blocks_ref,
    basis_ref,
    answer_ref,
    *rest,
):
    if packed:
        corners_ref = None
    else:
        corners_ref, *rest = rest
    (
        state_ref,
        hot_ref,
        others_ref,
        flags_ref,
        high_ref,
        low_ref,
        result_ref,
        sems,
    ) = rest
    groups = received_ref.shape[0]
    slots = groups * capacity
    kept, _, block, modes = blocks_ref.shape
    half = modes // 2
    count = kept + others_ref.shape[0]
    copies = []
    for n in range(count - kept):
        part = pl.ds((kept + n) * block, block)
        copies.append(
            pltpu.make_async_copy(basis_ref.at[:, part, :], others_ref.at[n], sems.at[n])
        )
        copies[n].start()

    ids = jnp.zeros((8, half), F32)
    for h in range(groups):
        own = pl.ds(h * capacity, capacity)
        state_ref[own, :half] = received_ref[h, :capacity, :]
        state_ref[own, half:] = received_ref[h, capacity : 2 * capacity, :]
        ids = ids + received_ref[h, 2 * capacity :, :].astype(F32)
    ids = jnp.concatenate([ids[0:1], ids[1:2]], axis=1).astype(jnp.int32)
    hot_ref[...] = jnp.where(iota(hot_ref.shape, 0) == ids, 1.0, 0.0).astype(BF16)

    def solve(*accumulators):
        mains, spares = accumulators[:8], accumulators[8:12]
        tangent_high, tangent_low = accumulators[12:]
        hyper = bits_ref.shape[0]
        both = range(2)
        for unit in both:
            pltpu.matmul_push_rhs(hot_ref[...], 0, unit)
        empty = jnp.zeros((128, modes - bits_ref.shape[1]), BF16)

        def flags_of(j):
            rows = jnp.concatenate([bits_ref[128 * j : 128 * j + 128, :], empty], axis=1)
            pltpu.matmul_acc_lhs(spares[j % 4], rows, load_staged_rhs=0 if j < 2 else None)

        blocks_of_flags = hyper // 128
        for j in range(blocks_of_flags + 2):
            if j < blocks_of_flags:
                flags_of(j)
            if j >= 2:
                flags_ref[128 * (j - 2) : 128 * (j - 1), :] = pltpu.matmul_pop(spares[(j - 2) % 4])
        for unit in both:
            pltpu.matmul_push_rhs(state_ref[...], 0, unit, transpose=True)
        strip = 16
        strips = hyper // strip

        def issue(i):
            n, r = divmod(i * strip, block)
            if n >= kept and r == 0:
                copies[n - kept].wait()
            source = blocks_ref.at[n] if n < kept else others_ref.at[n - kept]
            rows = jnp.concatenate([source[c, r : r + strip, :] for c in range(6)], axis=0)
            pltpu.matmul_acc_lhs(mains[i % 8], rows, load_staged_rhs=0 if i < 2 else None)

        def respond(i, sums):
            strain = pltpu.matmul_pop(mains[i % 8])
            e = [strain[c * strip : (c + 1) * strip] for c in range(6)]
            at = slice(i * strip, (i + 1) * strip)
            volume = e[0] + e[1] + e[2]
            third = volume * (1.0 / 3.0)
            d = [e[c] - third for c in range(3)]
            normal = d[0] * d[0] + d[1] * d[1] + d[2] * d[2]
            shear = e[3] * e[3] + e[4] * e[4] + e[5] * e[5]
            square = jnp.maximum(normal + 0.5 * shear, YIELD_STRESS * YIELD_STRESS)
            factor = (YIELD_STRESS * (1.0 - HARDENING)) * lax.rsqrt(square) + (HARDENING - 1.0)
            change = flags_ref[at, :] * factor
            high = change.astype(BF16)
            high_ref[at, :] = high
            low_ref[at, :] = (change - high.astype(F32)).astype(BF16)
            column = column_ref[at, :]
            weight = jnp.concatenate([column] * (slots // column.shape[1]), axis=1)
            scaled = weight + weight * change
            terms = [scaled * d[c] for c in range(3)] + [scaled * e[c] for c in range(3, 6)]
            terms.append(weight * volume)
            return [total + (term[:8] + term[8:]) for total, term in zip(sums, terms)]

        sums = [jnp.zeros((8, slots), F32)] * 7
        ahead = 7
        for i in range(ahead):
            issue(i)
        for i in range(strips):
            if i + ahead < strips:
                issue(i + ahead)
            sums = respond(i, sums)
        for n in range(hyper // modes):
            part = slice(n * modes, (n + 1) * modes)
            pltpu.matmul_push_rhs(high_ref[part, :], 0, 0)
            pltpu.matmul_push_rhs(low_ref[part, :], 0, 1)
            pltpu.matmul_acc_lhs(tangent_high, table_ref[:, part], load_staged_rhs=0)
            pltpu.matmul_acc_lhs(tangent_low, table_ref[0:48, part], load_staged_rhs=0)
        both_parts = pltpu.matmul_pop(tangent_high)
        tangent = both_parts[:48] + (both_parts[48:] + pltpu.matmul_pop(tangent_low))
        return tangent, sums

    tangent, sums = pl.run_scoped(
        solve,
        *[pltpu.ACC(n % 2)((96, slots), F32) for n in range(8)],
        *[pltpu.ACC(n % 2)((128, slots), F32) for n in range(4)],
        pltpu.ACC(0)((96, slots), F32),
        pltpu.ACC(1)((48, slots), F32),
    )

    volume = jnp.sum(sums[6], axis=0, keepdims=True)
    for c in range(6):
        total = jnp.sum(sums[c], axis=0, keepdims=True)
        result_ref[c : c + 1, :] = total + volume if c < 3 else 0.5 * total
    const = const_ref[...]
    const = jnp.concatenate([const] * (slots // const.shape[1]), axis=1)
    tangent = tangent + const
    at = 6
    for i in range(6):
        result_ref[at : at + 6 - i, :] = tangent[8 * i + i : 8 * i + 6]
        at += 6 - i
    result_ref[at:, :] = jnp.zeros((ROWS - at, slots), F32)

    last = first_ref.shape[1] - 1

    def corner_rows(write):
        for m in range(4):
            up = sides_of(first_ref, second_ref, "micro", m, last)
            down = sides_of(first_ref, second_ref, "micro", m, 0)
            for n in range(2):
                write(0, 2 * m + n, up[n])
                write(1, 2 * m + n, down[n])

    if packed:
        here = lax.axis_index("macro")
        group_of = iota((8, 128), 1) // capacity
        for h in range(hosts):
            chunk = jnp.zeros((8, 128), F32)
            tile, place = divmod(h * capacity, 128)
            for g in range(4):
                piece = result_ref[8 * g : 8 * g + 8, tile * 128 : (tile + 1) * 128]
                shift = (g * capacity - place) % 128
                if shift:
                    piece = pltpu.roll(piece, shift, 1)
                chunk = jnp.where(group_of == g, piece, chunk)
            answer_ref[h, 0:8, :] = chunk
        chunks = [jnp.minimum(here + 1, hosts - 1), jnp.maximum(here - 1, 0)]

        def write(side, row, value):
            answer_ref[chunks[side], 8 + row : 9 + row, :] = value
    else:
        answer_ref[...] = result_ref[...]

        def write(side, row, value):
            corners_ref[side, row : row + 1, :] = value

    corner_rows(write)


def assemble(stress):
    ready = []
    for here, low in stress:
        ready.append((here, low, previous_z(here), previous_z(low)))

    def at(c, sign_x, sign_y, sign_z):
        here, low, here_z, low_z = ready[c]
        if sign_z:
            near, far = here_z - here, low_z - low
        else:
            near, far = here_z + here, low_z + low
        both = far - near if sign_y else far + near
        return both[:-1] - both[1:] if sign_x else both[:-1] + both[1:]

    force = [
        at(0, 1, 0, 0) + at(5, 0, 1, 0) + at(4, 0, 0, 1),
        at(5, 1, 0, 0) + at(1, 0, 1, 0) + at(3, 0, 0, 1),
        at(4, 1, 0, 0) + at(3, 0, 1, 0) + at(2, 0, 0, 1),
    ]
    return [0.25 * value for value in force]


def elastic_kernel(
    hosts,
    capacity,
    motion_ref,
    stiff_ref,
    elem_ref,
    owner_ref,
    first_ref,
    second_ref,
    force_ref,
    edge_ref,
    index_ref,
    node_ref,
    wide_ref,
    stress_ref,
):
    size_x, size_y, size_z = motion_ref.shape[1:]
    node_ref[...] = jnp.zeros_like(node_ref)
    wide_ref[...] = jnp.zeros_like(wide_ref)
    stiffness = stiff_ref[...].astype(F32)
    elem, owner = elem_ref[...], owner_ref[...]
    points = elem.shape[1]
    column = elem // size_z
    depth = elem - column * size_z
    index_ref[0:1, :] = slots_of(owner, hosts, capacity)[2]
    index_ref[1:2, :] = column
    index_ref[2:3, :] = depth
    index_ref[3:, :] = jnp.zeros((5, points), jnp.int32)
    depth_hot = jnp.where(iota((size_z, points), 0) == depth, 1.0, 0.0).astype(BF16)
    column_hot = jnp.where(iota((size_x * size_y, points), 0) == column, 1.0, 0.0).astype(BF16)
    listed = dot_t(column_hot, depth_hot)
    for i in range(size_x):
        for m in range(3):
            low, high = sides_of(first_ref, second_ref, "micro", m, i)
            node_ref[m, i, 0:1, :] = low
            node_ref[m, i, 1 : size_y + 1, :] = motion_ref[m, i]
            node_ref[m, i, size_y + 1 : size_y + 2, :] = high
        low, _ = sides_of(first_ref, second_ref, "micro", 3, i)
        wide_ref[i, 0:1, :] = low
        keep = 1.0 - listed[i * size_y : (i + 1) * size_y]
        wide_ref[i, 1 : size_y + 1, :] = stiffness[i] * keep
    for m in range(3):
        edge_ref[m] = node_ref[m, 0]
        edge_ref[3 + m] = node_ref[m, size_x - 1]
    edge_ref[6] = wide_ref[size_x - 1]
    strain = block_strains([node_ref[m] for m in range(3)])
    stress = elastic_of(strain, wide_ref[: size_x - 1])
    for c in range(6):
        stress_ref[c, 0] = jnp.zeros(stress_ref.shape[2:], F32)
        stress_ref[c, 1:size_x] = stress[c]
        stress_ref[c, size_x] = jnp.zeros(stress_ref.shape[2:], F32)
    force = assemble(
        [(stress_ref[c, :, 1 : size_y + 1, :], stress_ref[c, :, 0:size_y, :]) for c in range(6)]
    )
    for m in range(3):
        force_ref[m] = force[m]


def final_kernel(packed, hosts, capacity, answer_ref, *rest):
    if packed:
        corners_ref = None
    else:
        corners_ref, *rest = rest
    (
        second_ref,
        first_ref,
        elastic_ref,
        edge_ref,
        index_ref,
        force_ref,
        tangent_ref,
        result_ref,
        node_ref,
        wide_ref,
        stress_ref,
    ) = rest
    size_x, size_y, size_z = elastic_ref.shape[1:]
    slot, column, depth = index_ref[0:1, :], index_ref[1:2, :], index_ref[2:3, :]
    points = slot.shape[1]
    slot_total = hosts * capacity
    if packed:
        group_of = iota((8, 128), 1) // capacity
        per_tile = 128 // capacity
        groups = []
        for g in range(4):
            tiles = []
            for t in range(hosts // per_tile):
                tile = jnp.zeros((8, 128), F32)
                for n in range(per_tile):
                    piece = answer_ref[t * per_tile + n, 0:8, :]
                    shift = ((n - g) * capacity) % 128
                    if shift:
                        piece = pltpu.roll(piece, shift, 1)
                    tile = jnp.where(group_of == n, piece, tile)
                tiles.append(tile)
            groups.append(jnp.concatenate(tiles, axis=1))
        answer = jnp.concatenate(groups, axis=0)
    else:
        answer = answer_ref[...]
    slot_hot = jnp.where(iota((slot_total, points), 0) == slot, 1.0, 0.0).astype(BF16)
    parts = jnp.concatenate(pieces(answer, 3), axis=0)
    chosen = jnp.dot(parts, slot_hot, preferred_element_type=F32)
    result = chosen[:ROWS] + (chosen[ROWS : 2 * ROWS] + chosen[2 * ROWS :])
    result_ref[...] = result
    for i in range(6):
        for j in range(6):
            at = 6 + UPPER.index((min(i, j), max(i, j)))
            tangent_ref[6 * i + j : 6 * i + j + 1, :] = result_ref[at : at + 1, :]

    here = lax.axis_index("macro")
    inner = [here > 0, here < hosts - 1]
    from_chunk = [jnp.maximum(here - 1, 0), jnp.minimum(here + 1, hosts - 1)]

    def corner(side, row):
        if packed:
            value = answer_ref[from_chunk[side], 8 + row : 9 + row, :]
        else:
            value = corners_ref[side, row : row + 1, :]
        return jnp.where(inner[side], value, 0.0)

    node_ref[...] = jnp.zeros_like(node_ref)
    wide_ref[...] = jnp.zeros_like(wide_ref)
    for m in range(3):
        faces = sides_of(first_ref, second_ref, "macro", m)
        for side, at in ((0, 0), (1, 3)):
            node_ref[m, at, 0:1, :] = corner(side, 2 * m)
            node_ref[m, at, 1 : size_y + 1, :] = faces[side]
            node_ref[m, at, size_y + 1 : size_y + 2, :] = corner(side, 2 * m + 1)
        node_ref[m, 1] = edge_ref[m]
        node_ref[m, 2] = edge_ref[3 + m]
    wide_ref[0, 0:1, :] = corner(0, 6)
    wide_ref[0, 1 : size_y + 1, :] = sides_of(first_ref, second_ref, "macro", 3)[0]
    wide_ref[1] = edge_ref[6]
    lower, upper = [], []
    for m in range(3):
        four = corners(node_ref[m])
        lower.append([jnp.stack([value[0], value[2]]) for value in four])
        upper.append([jnp.stack([value[1], value[3]]) for value in four])
    edge = elastic_of(strains(lower, upper), wide_ref[...])
    rows = (size_x - 1) * size_y
    depth_hot = jnp.where(iota((size_z, points), 0) == depth, 1.0, 0.0).astype(BF16)
    column_hot = iota((rows, points), 0) == column
    stress_ref[:, 1:size_x, 0:1, :] = jnp.zeros((6, size_x - 1, 1, size_z), F32)
    placed = [jnp.where(column_hot, result[c : c + 1], 0.0) for c in range(6)]
    placed = jnp.concatenate(pieces(jnp.concatenate(placed, axis=0), 2), axis=0)
    fields = dot_t(placed, depth_hot)
    for c in range(6):
        field = fields[c * rows : (c + 1) * rows] + fields[(6 + c) * rows : (7 + c) * rows]
        stress_ref[c, 1:size_x, 1 : size_y + 1, :] = field.reshape(size_x - 1, size_y, size_z)
        stress_ref[c, 0] = edge[c][0]
        stress_ref[c, size_x] = edge[c][1]
    force = assemble(
        [(stress_ref[c, :, 1 : size_y + 1, :], stress_ref[c, :, 0:size_y, :]) for c in range(6)]
    )
    for m in range(3):
        force_ref[m] = elastic_ref[m] + force[m]


def shape_of(shape, dtype=F32):
    return jax.ShapeDtypeStruct(shape, dtype)


def call(kernel, name, out_shape, args, scratch=(), flops=10**8, raw=0, raw_out=0):
    specs = whole(*args[: len(args) - raw]) + [pl.BlockSpec(memory_space=pl.ANY)] * raw
    return pl.pallas_call(
        kernel,
        grid=(1,),
        out_shape=out_shape,
        in_specs=specs,
        out_specs=[pl.BlockSpec(memory_space=pl.ANY)] * raw_out + whole(*out_shape[raw_out:]),
        scratch_shapes=scratch,
        compiler_params=pltpu.CompilerParams(vmem_limit_bytes=24 * 2**20),
        cost_estimate=pl.CostEstimate(flops=flops, bytes_accessed=2**20, transcendentals=0),
        name=name,
    )(*args)


def on_device(
    motion,
    stiffness,
    point_elem,
    point_owner,
    point_pattern,
    history,
    basis,
    mode_map,
    weights,
    patterns,
):
    size_x, size_y, size_z = motion.shape[1:]
    points = point_elem.shape[0]
    hosts = lax.axis_size("macro")
    capacity = 2 * points // hosts
    slots = capacity * hosts
    modes = mode_map.shape[0]
    half = modes // 2
    hyper = weights.shape[0]
    lanes = 128
    direct = capacity % 16 == 0
    packed = capacity * 4 == lanes and slots % lanes == 0
    motion = in_hbm(motion)
    stiffness = in_hbm(stiffness)
    elem = in_hbm(point_elem.reshape(1, points))
    owner = in_hbm(point_owner.reshape(1, points))
    pattern = in_hbm(point_pattern.reshape(1, points))
    history = in_hbm(history)
    map_rows = in_hbm(mode_map.T)

    rows = in_hbm(basis.reshape(6, hyper, modes))
    wide, kept = 256, 2
    sent = (
        [shape_of((hosts, 2 * capacity + 8, half), BF16)]
        if direct
        else [shape_of((slots, modes), BF16), shape_of((hosts, modes), BF16)]
    )
    swap, x_swap = shape_of((4, size_x, size_z)), shape_of((4, size_y, size_z))
    arguments = (owner, elem, motion, map_rows, history, pattern, stiffness)
    *payload, first, second, x_first, x_second, blocks = call(
        functools.partial(dispatch_kernel, hosts, capacity, direct),
        "dispatch",
        sent + [swap, swap, x_swap, x_swap, shape_of((kept, 6, wide, modes), BF16)],
        (*arguments, rows),
        [VMEM(value.shape, value.dtype) for value in (*arguments, sent[0])]
        + [pltpu.SemaphoreType.DMA((8 + kept,))],
        raw=8,
        raw_out=1,
    )

    if direct:
        received = lax.all_to_all(payload[0], "macro", 0, 0, tiled=True)
        groups, group = hosts, capacity
    else:
        slot_rows, ids = payload
        joined = jnp.concatenate(
            [
                slot_rows[:, :half].reshape(hosts, capacity, half),
                slot_rows[:, half:].reshape(hosts, capacity, half),
                ids.reshape(hosts, 2, half),
            ],
            axis=1,
        )
        joined = lax.all_to_all(joined, "macro", 0, 0, tiled=True)
        ids = jnp.sum(joined[:, 2 * capacity :].astype(F32), axis=0).astype(BF16)
        received = jnp.concatenate(
            [
                joined[:, :capacity].reshape(1, slots, half),
                joined[:, capacity : 2 * capacity].reshape(1, slots, half),
                jnp.pad(ids, ((0, 6), (0, 0)))[None],
            ],
            axis=1,
        )
        groups, group = 1, slots

    def swapped(value, axis, start):
        pairs = [(i, i + 1) for i in range(start, lax.axis_size(axis) - 1, 2)]
        return lax.ppermute(value, axis, pairs + [(b, a) for a, b in pairs])

    first, second = swapped(first, "micro", 0), swapped(second, "micro", 1)
    x_first, x_second = swapped(x_first, "macro", 0), swapped(x_second, "macro", 1)

    small = (map_rows, in_hbm(weights.reshape(1, hyper)), in_hbm(patterns.T))
    table, const, column, bits = call(
        table_kernel,
        "tables",
        [
            shape_of((96, hyper), BF16),
            shape_of((48, lanes)),
            shape_of((hyper, lanes)),
            shape_of((hyper, lanes), BF16),
        ],
        (blocks, *small, rows),
        [
            VMEM((hyper // wide - kept, 6, wide, modes), BF16),
            *[VMEM(value.shape, value.dtype) for value in small],
            pltpu.SemaphoreType.DMA((3 + hyper // wide - kept,)),
        ],
        raw=4,
    )

    answer = call(
        functools.partial(micro_kernel, packed, hosts, group),
        "micro_response",
        [shape_of((hosts, 16, lanes))]
        if packed
        else [shape_of((ROWS, slots)), shape_of((2, 8, lanes))],
        (
            received,
            first,
            second,
            const,
            bits,
            column,
            table,
            blocks,
            rows,
        ),
        [
            VMEM((slots, modes), BF16),
            VMEM((modes, slots), BF16),
            VMEM((hyper // wide - kept, 6, wide, modes), BF16),
            VMEM((hyper, slots), F32),
            *[VMEM((hyper, slots), BF16)] * 2,
            VMEM((ROWS, slots), F32),
            pltpu.SemaphoreType.DMA((hyper // wide - kept,)),
        ],
        raw=1,
    )

    if packed:
        answered = [lax.all_to_all(answer[0], "macro", 0, 0, tiled=True)]
    else:
        result, edges = answer
        here = lax.axis_index("macro")
        order = jnp.arange(hosts)[:, None, None]
        flat = result.reshape(ROWS, hosts, capacity).transpose(1, 0, 2).reshape(hosts, -1)
        tiles = pl.cdiv(flat.shape[1], lanes)
        flat = jnp.pad(flat, ((0, 0), (0, tiles * lanes - flat.shape[1])))
        joined = jnp.concatenate(
            [flat.reshape(hosts, tiles, lanes), jnp.where(order > here, edges[0], edges[1])], axis=1
        )
        joined = lax.all_to_all(joined, "macro", 0, 0, tiled=True)
        flat = joined[:, :tiles].reshape(hosts, -1)[:, : ROWS * capacity]
        result = flat.reshape(hosts, ROWS, capacity).transpose(1, 0, 2).reshape(ROWS, slots)
        low = lax.dynamic_index_in_dim(joined, jnp.maximum(here - 1, 0), 0, False)
        high = lax.dynamic_index_in_dim(joined, jnp.minimum(here + 1, hosts - 1), 0, False)
        answered = [result, jnp.stack([low[tiles:], high[tiles:]])]

    elastic = call(
        functools.partial(elastic_kernel, hosts, capacity),
        "elastic_forces",
        [shape_of(motion.shape), shape_of((7, 16, size_z)), shape_of((8, points), jnp.int32)],
        (motion, stiffness, elem, owner, first, second),
        [
            VMEM((3, size_x, 16, size_z), F32),
            VMEM((size_x, 16, size_z), F32),
            VMEM((6, size_x + 1, 16, size_z), F32),
        ],
    )

    force, tangent = call(
        functools.partial(final_kernel, packed, hosts, capacity),
        "final_forces",
        [shape_of(motion.shape), shape_of((36, points))],
        (*answered, x_second, x_first, *elastic),
        [
            VMEM((ROWS, points), F32),
            VMEM((3, 4, 16, size_z), F32),
            VMEM((2, 16, size_z), F32),
            VMEM((6, size_x + 1, 16, size_z), F32),
        ],
    )
    return (force, tangent)


def solution(mesh):
    return jax.shard_map(
        on_device,
        mesh=mesh,
        in_specs=(
            P(None, "macro", "micro", None),
            P("macro", "micro", None),
            P(("macro", "micro")),
            P(("macro", "micro")),
            P(("macro", "micro")),
            P(None, ("macro", "micro")),
            P("macro", None, None),
            P(),
            P(),
            P(),
        ),
        out_specs=(P(None, "macro", "micro", None), P(None, ("macro", "micro"))),
        check_vma=False,
    )
```

```python
import functools

import jax
import jax.numpy as jnp
from jax import lax
from jax.experimental import pallas as pl
from jax.experimental.pallas import tpu as pltpu
from jax.sharding import PartitionSpec as P

YIELD_STRESS = 1.5
HARDENING = 0.2
F32 = jnp.float32
BF16 = jnp.bfloat16
VMEM = pltpu.VMEM
ROWS = 32
UPPER = [(i, j) for i in range(6) for j in range(i, 6)]


def whole(*arrays):
    return [pl.BlockSpec(value.shape, lambda s, n=len(value.shape): (0,) * n) for value in arrays]


def in_hbm(value):
    return pltpu.with_memory_space_constraint(value, pltpu.HBM)


def iota(shape, dim):
    return lax.broadcasted_iota(jnp.int32, shape, dim)


def dot_t(left, right):
    return lax.dot_general(left, right, (((1,), (1,)), ((), ())), preferred_element_type=F32)


def pieces(value, count):
    out = []
    for _ in range(count):
        piece = value.astype(BF16)
        out.append(piece)
        value = value - piece.astype(F32)
    return out


def next_z(field):
    last = field.ndim - 1
    size = field.shape[last]
    rolled = pltpu.roll(field, size - 1, last)
    return jnp.where(iota(field.shape, last) == size - 1, 0.0, rolled)


def previous_z(field):
    last = field.ndim - 1
    rolled = pltpu.roll(field, 1, last)
    return jnp.where(iota(field.shape, last) == 0, 0.0, rolled)


def corners(field):
    y_up = pltpu.roll(field, field.shape[1] - 1, 1)
    return [field, y_up, next_z(field), next_z(y_up)]


def strains(lower, upper):
    grads = []
    for low, high in zip(lower, upper):
        dx = [b - a for a, b in zip(low, high)]
        grad_x = (dx[0] + dx[1] + dx[2] + dx[3]) * 0.25
        dy = [value[1] - value[0] for value in (low, high)]
        dy_z = [value[3] - value[2] for value in (low, high)]
        grad_y = (dy[0] + dy[1] + dy_z[0] + dy_z[1]) * 0.25
        dz = [value[2] - value[0] for value in (low, high)]
        dz_y = [value[3] - value[1] for value in (low, high)]
        grad_z = (dz[0] + dz[1] + dz_y[0] + dz_y[1]) * 0.25
        grads.append((grad_x, grad_y, grad_z))
    return [
        grads[0][0],
        grads[1][1],
        grads[2][2],
        grads[1][2] + grads[2][1],
        grads[0][2] + grads[2][0],
        grads[0][1] + grads[1][0],
    ]


def block_strains(fields):
    nodes = [corners(field) for field in fields]
    return strains(
        [[value[:-1] for value in four] for four in nodes],
        [[value[1:] for value in four] for four in nodes],
    )


def elastic_of(strain, stiffness):
    volume = strain[0] + strain[1] + strain[2]
    rest = volume - volume * (1.0 / 3.0)
    normal = [stiffness * (rest + strain[c]) for c in range(3)]
    return normal + [stiffness * (0.5 * strain[c]) for c in range(3, 6)]


def slots_of(owner, hosts, capacity):
    points = owner.shape[1]
    chosen = iota((hosts, points), 0) == owner
    host_hot = jnp.where(chosen, 1.0, 0.0)
    before = jnp.where(iota((points, points), 0) < iota((points, points), 1), 1.0, 0.0)
    counts = jnp.dot(host_hot.astype(BF16), before.astype(BF16), preferred_element_type=F32)
    position = jnp.sum(host_hot * counts, axis=0, keepdims=True).astype(jnp.int32)
    return host_hot, position, owner * capacity + position


def dispatch_kernel(hosts, capacity, direct, *refs):
    inputs, basis_ref, payload_out, refs = refs[:9], refs[9], refs[10], list(refs[11:])
    ids_ref = None if direct else refs.pop(0)
    first_ref, second_ref, x_first_ref, x_second_ref, blocks_ref = refs[:5]
    buffers, payload_ref, sems = refs[8:14] + refs[5:8], refs[14], refs[15]
    arrivals = [
        pltpu.make_async_copy(value, buffer, sems.at[n])
        for n, (value, buffer) in enumerate(zip(inputs, buffers))
    ]
    for copy in arrivals:
        copy.start()
    kept, _, wide, _ = blocks_ref.shape
    later = [
        pltpu.make_async_copy(
            basis_ref.at[:, pl.ds(n * wide, wide), :], blocks_ref.at[n], sems.at[10 + n]
        )
        for n in range(kept)
    ]
    for copy in later:
        copy.start()
    owner_ref, elem_ref, motion_ref, history_ref, pattern_ref, stiff_ref, map_ref, _, _ = buffers
    size_x, size_y, size_z = motion_ref.shape[1:]
    for copy in arrivals:
        copy.wait()
    owner = owner_ref[...]
    points = owner.shape[1]
    host_hot, position, slot = slots_of(owner, hosts, capacity)
    slot_total = hosts * capacity
    slot_hot = jnp.where(iota((slot_total, points), 0) == slot, 1.0, 0.0).astype(BF16)
    elem = elem_ref[...]
    column = elem // size_z
    depth = elem - column * size_z
    depth_hot = jnp.where(iota((size_z, points), 0) == depth, 1.0, 0.0).astype(BF16)
    rows = (size_x - 1) * size_y
    column_hot = iota((rows, points), 0) == column
    strain = block_strains([motion_ref[m] for m in range(3)])
    field = jnp.concatenate([value.reshape(rows, size_z) for value in strain], axis=0)
    picked = jnp.dot(field.astype(BF16), depth_hot, preferred_element_type=F32)
    macro_strain = jnp.concatenate(
        [
            jnp.sum(
                jnp.where(column_hot, picked[c * rows : (c + 1) * rows], 0.0),
                axis=0,
                keepdims=True,
            )
            for c in range(6)
        ],
        axis=0,
    ).astype(BF16)
    held = dot_t(slot_hot, history_ref[...])
    slot_strain = dot_t(slot_hot, macro_strain).astype(BF16)
    mapped = jnp.dot(slot_strain, map_ref[...], preferred_element_type=F32)
    sent = (mapped + held).astype(BF16)
    place = position + lax.axis_index("macro") * capacity
    modes = sent.shape[1]
    half = modes // 2
    place_hot = jnp.where(iota((modes, points), 0) == place, 1.0, 0.0).astype(BF16)
    ids = dot_t((host_hot * pattern_ref[...].astype(F32)).astype(BF16), place_hot)
    if direct:
        for h in range(hosts):
            mine = sent[h * capacity : (h + 1) * capacity]
            payload_ref[h, :capacity, :] = mine[:, :half]
            payload_ref[h, capacity : 2 * capacity, :] = mine[:, half:]
            row = iota((8, half), 0)
            low, high = ids[h : h + 1, :half], ids[h : h + 1, half:]
            tile = jnp.where(row == 0, low, jnp.where(row == 1, high, 0.0))
            payload_ref[h, 2 * capacity :, :] = tile.astype(BF16)
    else:
        payload_ref[...] = sent
        ids_ref[...] = ids.astype(BF16)
    leave = pltpu.make_async_copy(payload_ref, payload_out, sems.at[9])
    leave.start()
    stiffness = stiff_ref[...].astype(F32)
    even = lax.rem(lax.axis_index("micro"), 2) == 0
    for i in range(size_x):
        for m in range(4):
            if m < 3:
                up, down = motion_ref[m, i, size_y - 1 : size_y, :], motion_ref[m, i, 0:1, :]
            else:
                up = down = stiffness[i, size_y - 1 : size_y, :]
            first_ref[m, i : i + 1, :] = jnp.where(even, up, down)
            second_ref[m, i : i + 1, :] = jnp.where(even, down, up)
    even = lax.rem(lax.axis_index("macro"), 2) == 0
    for m in range(4):
        if m < 3:
            up, down = motion_ref[m, size_x - 1], motion_ref[m, 0]
        else:
            up = down = stiffness[size_x - 1]
        x_first_ref[m] = jnp.where(even, up, down)
        x_second_ref[m] = jnp.where(even, down, up)
    leave.wait()
    for copy in later:
        copy.wait()


def table_kernel(
    blocks_ref,
    map_ref,
    weights_ref,
    patterns_ref,
    basis_ref,
    table_ref,
    const_ref,
    bits_ref,
    others_ref,
    sems,
):
    hyper = weights_ref.shape[1]
    lanes = 128
    kept, _, wide, modes = blocks_ref.shape
    count = hyper // wide
    copies = []
    for n in range(kept, count):
        copy = pltpu.make_async_copy(
            basis_ref.at[:, pl.ds(n * wide, wide), :], others_ref.at[n - kept], sems.at[n - kept]
        )
        copy.start()
        copies.append(copy)
    weights = weights_ref[...]
    split = [piece.astype(F32) for piece in pieces(weights, 3)]
    row = iota((8, hyper), 0)
    stack = jnp.where(
        row == 0, split[0], jnp.where(row == 1, split[1], jnp.where(row == 2, split[2], 0.0))
    )
    choice = jnp.where(iota((8, lanes), 1) == iota((8, lanes), 0) + patterns_ref.shape[1], 1.0, 0.0)
    weight_lanes = lax.dot_general(
        stack.astype(BF16),
        choice.astype(BF16),
        (((0,), (0,)), ((), ())),
        preferred_element_type=F32,
    )
    patterns = patterns_ref[...]
    words, total = patterns.shape
    parts = [((patterns >> (8 * k)) & 255).astype(F32) for k in range(4)]
    spare = -4 * words % 8
    parts = jnp.concatenate(parts + [jnp.zeros((spare, total), F32)] * (spare > 0), axis=0)
    parts = jnp.concatenate([parts, jnp.zeros((parts.shape[0], lanes - total), F32)], axis=1)
    place = iota((1, 4 * words + spare), 1)
    part = jnp.where(place >= words, 1, 0) + jnp.where(place >= 2 * words, 1, 0)
    part = part + jnp.where(place >= 3 * words, 1, 0)
    start = 30 * (place - words * part) + 8 * part
    size = jnp.where(part == 3, 6, 8)
    after = iota((hyper, 4 * words + spare), 0) - start
    byte_hot = jnp.where((after >= 0) & (after < size), 1.0, 0.0).astype(BF16)
    value = jnp.dot(byte_hot, parts.astype(BF16), preferred_element_type=F32).astype(jnp.int32)
    index = iota((hyper, lanes), 0)
    offset = index - 30 * ((index * 2185) >> 16)
    bits_ref[...] = (((value >> (offset & 7)) & 1).astype(F32) + weight_lanes).astype(BF16)

    modes_map = map_ref[...]
    modes_map = jnp.concatenate(
        [modes_map.astype(F32), jnp.zeros((2, modes), F32)], axis=0
    ).astype(BF16)
    sums = jnp.zeros((48, wide), F32)
    for n in range(count):
        if n >= kept:
            copies[n - kept].wait()
        source = blocks_ref.at[n] if n < kept else others_ref.at[n - kept]
        part = slice(n * wide, (n + 1) * wide)
        local = [dot_t(modes_map, source[c]) for c in range(6)]
        trace = local[0] + local[1] + local[2]
        third = trace / 3.0
        shaped = [local[c] - third for c in range(3)] + [0.5 * local[c] for c in range(3, 6)]
        weight = weights[:, part]
        shaped = [weight * value for value in shaped]
        weighted_trace = weight * trace
        blocks, adds = [], []
        for i in range(6):
            entry = local[0][i : i + 1] * shaped[0]
            for c in range(1, 6):
                entry = entry + local[c][i : i + 1] * shaped[c]
            blocks.append(entry)
            adds.append(entry + trace[i : i + 1] * weighted_trace)
        sums = sums + jnp.concatenate(adds, axis=0)
        high, low = pieces(jnp.concatenate(blocks, axis=0), 2)
        table_ref[0:48, part] = high
        table_ref[48:96, part] = low
    const_ref[...] = jnp.broadcast_to(jnp.sum(sums, axis=1, keepdims=True), const_ref.shape)


def sides_of(first_ref, second_ref, axis, m, at=None):
    even = lax.rem(lax.axis_index(axis), 2) == 0
    rows = slice(None) if at is None else slice(at, at + 1)
    first, second = first_ref[m, rows, :], second_ref[m, rows, :]
    return jnp.where(even, second, first), jnp.where(even, first, second)


def micro_kernel(
    packed,
    hosts,
    capacity,
    flag_lanes,
    received_ref,
    first_ref,
    second_ref,
    const_ref,
    bits_ref,
    table_ref,
    blocks_ref,
    basis_ref,
    answer_ref,
    *rest,
):
    if packed:
        corners_ref = None
    else:
        corners_ref, *rest = rest
    (
        state_ref,
        hot_ref,
        others_ref,
        flags_ref,
        high_ref,
        low_ref,
        result_ref,
        sems,
    ) = rest
    groups = received_ref.shape[0]
    slots = groups * capacity
    kept, _, block, modes = blocks_ref.shape
    half = modes // 2
    count = kept + others_ref.shape[0]
    copies = []
    for n in range(count - kept):
        part = pl.ds((kept + n) * block, block)
        copies.append(
            pltpu.make_async_copy(basis_ref.at[:, part, :], others_ref.at[n], sems.at[n])
        )
        copies[n].start()

    ids = jnp.zeros((8, half), F32)
    for h in range(groups):
        own = pl.ds(h * capacity, capacity)
        state_ref[own, :half] = received_ref[h, :capacity, :]
        state_ref[own, half:] = received_ref[h, capacity : 2 * capacity, :]
        ids = ids + received_ref[h, 2 * capacity :, :].astype(F32)
    ids = jnp.concatenate([ids[0:1], ids[1:2]], axis=1).astype(jnp.int32)
    hot_ref[...] = jnp.where(iota(hot_ref.shape, 0) == ids, 1.0, 0.0).astype(BF16)

    def solve(*accumulators):
        mains, spares = accumulators[:8], accumulators[8:12]
        tangent_high, tangent_low = accumulators[12:]
        hyper = bits_ref.shape[0]
        both = range(2)
        for unit in both:
            pltpu.matmul_push_rhs(hot_ref[...], 0, unit)
        empty = jnp.zeros((128, modes - bits_ref.shape[1]), BF16)

        def flags_of(j):
            rows = jnp.concatenate([bits_ref[128 * j : 128 * j + 128, :], empty], axis=1)
            pltpu.matmul_acc_lhs(spares[j % 4], rows, load_staged_rhs=0 if j < 2 else None)

        blocks_of_flags = hyper // 128
        for j in range(blocks_of_flags + 2):
            if j < blocks_of_flags:
                flags_of(j)
            if j >= 2:
                flags_ref[128 * (j - 2) : 128 * (j - 1), :] = pltpu.matmul_pop(spares[(j - 2) % 4])
        for unit in both:
            pltpu.matmul_push_rhs(state_ref[...], 0, unit, transpose=True)
        strip = 16
        strips = hyper // strip

        def issue(i):
            n, r = divmod(i * strip, block)
            if n >= kept and r == 0:
                copies[n - kept].wait()
            source = blocks_ref.at[n] if n < kept else others_ref.at[n - kept]
            rows = jnp.concatenate([source[c, r : r + strip, :] for c in range(6)], axis=0)
            pltpu.matmul_acc_lhs(mains[i % 8], rows, load_staged_rhs=0 if i < 2 else None)

        def respond(i, sums):
            strain = pltpu.matmul_pop(mains[i % 8])
            e = [strain[c * strip : (c + 1) * strip] for c in range(6)]
            at = slice(i * strip, (i + 1) * strip)
            volume = e[0] + e[1] + e[2]
            third = volume * (1.0 / 3.0)
            d = [e[c] - third for c in range(3)]
            normal = d[0] * d[0] + d[1] * d[1] + d[2] * d[2]
            shear = e[3] * e[3] + e[4] * e[4] + e[5] * e[5]
            square = jnp.maximum(normal + 0.5 * shear, YIELD_STRESS * YIELD_STRESS)
            factor = (YIELD_STRESS * (1.0 - HARDENING)) * lax.rsqrt(square) + (HARDENING - 1.0)
            change = flags_ref[at, :] * factor
            high = change.astype(BF16)
            high_ref[at, :] = high
            low_ref[at, :] = (change - high.astype(F32)).astype(BF16)
            packed_row = bits_ref[at, :].astype(F32)
            lane = iota(packed_row.shape, 1)
            packed_row = jnp.where((lane >= flag_lanes) & (lane < flag_lanes + 3), packed_row, 0.0)
            weight = jnp.sum(packed_row, axis=1, keepdims=True)
            scaled = weight + weight * change
            terms = [scaled * d[c] for c in range(3)] + [scaled * e[c] for c in range(3, 6)]
            terms.append(weight * volume)
            return [total + (term[:8] + term[8:]) for total, term in zip(sums, terms)]

        sums = [jnp.zeros((8, slots), F32)] * 7
        ahead = 7
        for i in range(ahead):
            issue(i)
        for i in range(strips):
            if i + ahead < strips:
                issue(i + ahead)
            sums = respond(i, sums)
        for n in range(hyper // modes):
            part = slice(n * modes, (n + 1) * modes)
            pltpu.matmul_push_rhs(high_ref[part, :], 0, 0)
            pltpu.matmul_push_rhs(low_ref[part, :], 0, 1)
            pltpu.matmul_acc_lhs(tangent_high, table_ref[:, part], load_staged_rhs=0)
            pltpu.matmul_acc_lhs(tangent_low, table_ref[0:48, part], load_staged_rhs=0)
        both_parts = pltpu.matmul_pop(tangent_high)
        tangent = both_parts[:48] + (both_parts[48:] + pltpu.matmul_pop(tangent_low))
        return tangent, sums

    tangent, sums = pl.run_scoped(
        solve,
        *[pltpu.ACC(n % 2)((96, slots), F32) for n in range(8)],
        *[pltpu.ACC(n % 2)((128, slots), F32) for n in range(4)],
        pltpu.ACC(0)((96, slots), F32),
        pltpu.ACC(1)((48, slots), F32),
    )

    volume = jnp.sum(sums[6], axis=0, keepdims=True)
    for c in range(6):
        total = jnp.sum(sums[c], axis=0, keepdims=True)
        result_ref[c : c + 1, :] = total + volume if c < 3 else 0.5 * total
    const = const_ref[...]
    const = jnp.concatenate([const] * (slots // const.shape[1]), axis=1)
    tangent = tangent + const
    at = 6
    for i in range(6):
        result_ref[at : at + 6 - i, :] = tangent[8 * i + i : 8 * i + 6]
        at += 6 - i
    result_ref[at:, :] = jnp.zeros((ROWS - at, slots), F32)

    last = first_ref.shape[1] - 1

    def corner_rows(write):
        for m in range(4):
            up = sides_of(first_ref, second_ref, "micro", m, last)
            down = sides_of(first_ref, second_ref, "micro", m, 0)
            for n in range(2):
                write(0, 2 * m + n, up[n])
                write(1, 2 * m + n, down[n])

    if packed:
        here = lax.axis_index("macro")
        group_of = iota((8, 128), 1) // capacity
        for h in range(hosts):
            chunk = jnp.zeros((8, 128), F32)
            tile, place = divmod(h * capacity, 128)
            for g in range(4):
                piece = result_ref[8 * g : 8 * g + 8, tile * 128 : (tile + 1) * 128]
                shift = (g * capacity - place) % 128
                if shift:
                    piece = pltpu.roll(piece, shift, 1)
                chunk = jnp.where(group_of == g, piece, chunk)
            answer_ref[h, 0:8, :] = chunk
        chunks = [jnp.minimum(here + 1, hosts - 1), jnp.maximum(here - 1, 0)]

        def write(side, row, value):
            answer_ref[chunks[side], 8 + row : 9 + row, :] = value
    else:
        answer_ref[...] = result_ref[...]

        def write(side, row, value):
            corners_ref[side, row : row + 1, :] = value

    corner_rows(write)


def assemble(stress):
    ready = []
    for here, low in stress:
        ready.append((here, low, previous_z(here), previous_z(low)))

    def at(c, sign_x, sign_y, sign_z):
        here, low, here_z, low_z = ready[c]
        if sign_z:
            near, far = here_z - here, low_z - low
        else:
            near, far = here_z + here, low_z + low
        both = far - near if sign_y else far + near
        return both[:-1] - both[1:] if sign_x else both[:-1] + both[1:]

    force = [
        at(0, 1, 0, 0) + at(5, 0, 1, 0) + at(4, 0, 0, 1),
        at(5, 1, 0, 0) + at(1, 0, 1, 0) + at(3, 0, 0, 1),
        at(4, 1, 0, 0) + at(3, 0, 1, 0) + at(2, 0, 0, 1),
    ]
    return [0.25 * value for value in force]


def elastic_kernel(
    hosts,
    capacity,
    motion_ref,
    stiff_ref,
    elem_ref,
    owner_ref,
    first_ref,
    second_ref,
    force_ref,
    edge_ref,
    index_ref,
    node_ref,
    wide_ref,
    stress_ref,
):
    size_x, size_y, size_z = motion_ref.shape[1:]
    node_ref[...] = jnp.zeros_like(node_ref)
    wide_ref[...] = jnp.zeros_like(wide_ref)
    stiffness = stiff_ref[...].astype(F32)
    elem, owner = elem_ref[...], owner_ref[...]
    points = elem.shape[1]
    column = elem // size_z
    depth = elem - column * size_z
    index_ref[0:1, :] = slots_of(owner, hosts, capacity)[2]
    index_ref[1:2, :] = column
    index_ref[2:3, :] = depth
    index_ref[3:, :] = jnp.zeros((5, points), jnp.int32)
    depth_hot = jnp.where(iota((size_z, points), 0) == depth, 1.0, 0.0).astype(BF16)
    column_hot = jnp.where(iota((size_x * size_y, points), 0) == column, 1.0, 0.0).astype(BF16)
    listed = dot_t(column_hot, depth_hot)
    for i in range(size_x):
        for m in range(3):
            low, high = sides_of(first_ref, second_ref, "micro", m, i)
            node_ref[m, i, 0:1, :] = low
            node_ref[m, i, 1 : size_y + 1, :] = motion_ref[m, i]
            node_ref[m, i, size_y + 1 : size_y + 2, :] = high
        low, _ = sides_of(first_ref, second_ref, "micro", 3, i)
        wide_ref[i, 0:1, :] = low
        keep = 1.0 - listed[i * size_y : (i + 1) * size_y]
        wide_ref[i, 1 : size_y + 1, :] = stiffness[i] * keep
    for m in range(3):
        edge_ref[m] = node_ref[m, 0]
        edge_ref[3 + m] = node_ref[m, size_x - 1]
    edge_ref[6] = wide_ref[size_x - 1]
    strain = block_strains([node_ref[m] for m in range(3)])
    stress = elastic_of(strain, wide_ref[: size_x - 1])
    for c in range(6):
        stress_ref[c, 0] = jnp.zeros(stress_ref.shape[2:], F32)
        stress_ref[c, 1:size_x] = stress[c]
        stress_ref[c, size_x] = jnp.zeros(stress_ref.shape[2:], F32)
    force = assemble(
        [(stress_ref[c, :, 1 : size_y + 1, :], stress_ref[c, :, 0:size_y, :]) for c in range(6)]
    )
    for m in range(3):
        force_ref[m] = force[m]


def final_kernel(packed, hosts, capacity, answer_ref, *rest):
    if packed:
        corners_ref = None
    else:
        corners_ref, *rest = rest
    (
        second_ref,
        first_ref,
        elastic_ref,
        edge_ref,
        index_ref,
        force_ref,
        tangent_ref,
        result_ref,
        node_ref,
        wide_ref,
        stress_ref,
    ) = rest
    size_x, size_y, size_z = elastic_ref.shape[1:]
    slot, column, depth = index_ref[0:1, :], index_ref[1:2, :], index_ref[2:3, :]
    points = slot.shape[1]
    slot_total = hosts * capacity
    if packed:
        group_of = iota((8, 128), 1) // capacity
        per_tile = 128 // capacity
        groups = []
        for g in range(4):
            tiles = []
            for t in range(hosts // per_tile):
                tile = jnp.zeros((8, 128), F32)
                for n in range(per_tile):
                    piece = answer_ref[t * per_tile + n, 0:8, :]
                    shift = ((n - g) * capacity) % 128
                    if shift:
                        piece = pltpu.roll(piece, shift, 1)
                    tile = jnp.where(group_of == n, piece, tile)
                tiles.append(tile)
            groups.append(jnp.concatenate(tiles, axis=1))
        answer = jnp.concatenate(groups, axis=0)
    else:
        answer = answer_ref[...]
    slot_hot = jnp.where(iota((slot_total, points), 0) == slot, 1.0, 0.0).astype(BF16)
    parts = jnp.concatenate(pieces(answer, 3), axis=0)
    chosen = jnp.dot(parts, slot_hot, preferred_element_type=F32)
    result = chosen[:ROWS] + (chosen[ROWS : 2 * ROWS] + chosen[2 * ROWS :])
    result_ref[...] = result
    for i in range(6):
        for j in range(6):
            at = 6 + UPPER.index((min(i, j), max(i, j)))
            tangent_ref[6 * i + j : 6 * i + j + 1, :] = result_ref[at : at + 1, :]

    here = lax.axis_index("macro")
    inner = [here > 0, here < hosts - 1]
    from_chunk = [jnp.maximum(here - 1, 0), jnp.minimum(here + 1, hosts - 1)]

    def corner(side, row):
        if packed:
            value = answer_ref[from_chunk[side], 8 + row : 9 + row, :]
        else:
            value = corners_ref[side, row : row + 1, :]
        return jnp.where(inner[side], value, 0.0)

    node_ref[...] = jnp.zeros_like(node_ref)
    wide_ref[...] = jnp.zeros_like(wide_ref)
    for m in range(3):
        faces = sides_of(first_ref, second_ref, "macro", m)
        for side, at in ((0, 0), (1, 3)):
            node_ref[m, at, 0:1, :] = corner(side, 2 * m)
            node_ref[m, at, 1 : size_y + 1, :] = faces[side]
            node_ref[m, at, size_y + 1 : size_y + 2, :] = corner(side, 2 * m + 1)
        node_ref[m, 1] = edge_ref[m]
        node_ref[m, 2] = edge_ref[3 + m]
    wide_ref[0, 0:1, :] = corner(0, 6)
    wide_ref[0, 1 : size_y + 1, :] = sides_of(first_ref, second_ref, "macro", 3)[0]
    wide_ref[1] = edge_ref[6]
    lower, upper = [], []
    for m in range(3):
        four = corners(node_ref[m])
        lower.append([jnp.stack([value[0], value[2]]) for value in four])
        upper.append([jnp.stack([value[1], value[3]]) for value in four])
    edge = elastic_of(strains(lower, upper), wide_ref[...])
    rows = (size_x - 1) * size_y
    depth_hot = jnp.where(iota((size_z, points), 0) == depth, 1.0, 0.0).astype(BF16)
    column_hot = iota((rows, points), 0) == column
    stress_ref[:, 1:size_x, 0:1, :] = jnp.zeros((6, size_x - 1, 1, size_z), F32)
    placed = [jnp.where(column_hot, result[c : c + 1], 0.0) for c in range(6)]
    placed = jnp.concatenate(pieces(jnp.concatenate(placed, axis=0), 2), axis=0)
    fields = dot_t(placed, depth_hot)
    for c in range(6):
        field = fields[c * rows : (c + 1) * rows] + fields[(6 + c) * rows : (7 + c) * rows]
        stress_ref[c, 1:size_x, 1 : size_y + 1, :] = field.reshape(size_x - 1, size_y, size_z)
        stress_ref[c, 0] = edge[c][0]
        stress_ref[c, size_x] = edge[c][1]
    force = assemble(
        [(stress_ref[c, :, 1 : size_y + 1, :], stress_ref[c, :, 0:size_y, :]) for c in range(6)]
    )
    for m in range(3):
        force_ref[m] = elastic_ref[m] + force[m]


def shape_of(shape, dtype=F32):
    return jax.ShapeDtypeStruct(shape, dtype)


def call(kernel, name, out_shape, args, scratch=(), flops=10**8, raw=0, raw_out=0):
    specs = whole(*args[: len(args) - raw]) + [pl.BlockSpec(memory_space=pl.ANY)] * raw
    return pl.pallas_call(
        kernel,
        grid=(1,),
        out_shape=out_shape,
        in_specs=specs,
        out_specs=[pl.BlockSpec(memory_space=pl.ANY)] * raw_out + whole(*out_shape[raw_out:]),
        scratch_shapes=scratch,
        compiler_params=pltpu.CompilerParams(vmem_limit_bytes=24 * 2**20),
        cost_estimate=pl.CostEstimate(flops=flops, bytes_accessed=2**20, transcendentals=0),
        name=name,
    )(*args)


def on_device(
    motion,
    stiffness,
    point_elem,
    point_owner,
    point_pattern,
    history,
    basis,
    mode_map,
    weights,
    patterns,
):
    size_x, size_y, size_z = motion.shape[1:]
    points = point_elem.shape[0]
    hosts = lax.axis_size("macro")
    capacity = 2 * points // hosts
    slots = capacity * hosts
    modes = mode_map.shape[0]
    half = modes // 2
    hyper = weights.shape[0]
    lanes = 128
    direct = capacity % 16 == 0
    packed = capacity * 4 == lanes and slots % lanes == 0
    motion = in_hbm(motion)
    stiffness = in_hbm(stiffness)
    elem = in_hbm(point_elem.reshape(1, points))
    owner = in_hbm(point_owner.reshape(1, points))
    pattern = in_hbm(point_pattern.reshape(1, points))
    history = in_hbm(history)
    map_rows = in_hbm(mode_map.T)

    rows = in_hbm(basis.reshape(6, hyper, modes))
    wide, kept = 256, 3
    sent = (
        [shape_of((hosts, 2 * capacity + 8, half), BF16)]
        if direct
        else [shape_of((slots, modes), BF16), shape_of((hosts, modes), BF16)]
    )
    swap, x_swap = shape_of((4, size_x, size_z)), shape_of((4, size_y, size_z))
    arguments = (owner, elem, motion, history, pattern, stiffness)
    small = (map_rows, in_hbm(weights.reshape(1, hyper)), in_hbm(patterns.T))
    *payload, first, second, x_first, x_second, blocks, map_here, weights, bit_words = call(
        functools.partial(dispatch_kernel, hosts, capacity, direct),
        "dispatch",
        sent
        + [swap, swap, x_swap, x_swap, shape_of((kept, 6, wide, modes), BF16)]
        + [shape_of(value.shape, value.dtype) for value in small],
        (*arguments, *small, rows),
        [VMEM(value.shape, value.dtype) for value in (*arguments, sent[0])]
        + [pltpu.SemaphoreType.DMA((10 + kept,))],
        raw=10,
        raw_out=1,
    )

    if direct:
        received = lax.all_to_all(payload[0], "macro", 0, 0, tiled=True)
        groups, group = hosts, capacity
    else:
        slot_rows, ids = payload
        joined = jnp.concatenate(
            [
                slot_rows[:, :half].reshape(hosts, capacity, half),
                slot_rows[:, half:].reshape(hosts, capacity, half),
                ids.reshape(hosts, 2, half),
            ],
            axis=1,
        )
        joined = lax.all_to_all(joined, "macro", 0, 0, tiled=True)
        ids = jnp.sum(joined[:, 2 * capacity :].astype(F32), axis=0).astype(BF16)
        received = jnp.concatenate(
            [
                joined[:, :capacity].reshape(1, slots, half),
                joined[:, capacity : 2 * capacity].reshape(1, slots, half),
                jnp.pad(ids, ((0, 6), (0, 0)))[None],
            ],
            axis=1,
        )
        groups, group = 1, slots

    def swapped(value, axis, start):
        pairs = [(i, i + 1) for i in range(start, lax.axis_size(axis) - 1, 2)]
        return lax.ppermute(value, axis, pairs + [(b, a) for a, b in pairs])

    first, second = swapped(first, "micro", 0), swapped(second, "micro", 1)
    x_first, x_second = swapped(x_first, "macro", 0), swapped(x_second, "macro", 1)

    table, const, bits = call(
        table_kernel,
        "tables",
        [
            shape_of((96, hyper), BF16),
            shape_of((48, lanes)),
            shape_of((hyper, lanes), BF16),
        ],
        (blocks, map_here, weights, bit_words, rows),
        [
            VMEM((hyper // wide - kept, 6, wide, modes), BF16),
            pltpu.SemaphoreType.DMA((hyper // wide - kept,)),
        ],
        raw=1,
    )

    answer = call(
        functools.partial(micro_kernel, packed, hosts, group, patterns.shape[0]),
        "micro_response",
        [shape_of((hosts, 16, lanes))]
        if packed
        else [shape_of((ROWS, slots)), shape_of((2, 8, lanes))],
        (
            received,
            first,
            second,
            const,
            bits,
            table,
            blocks,
            rows,
        ),
        [
            VMEM((slots, modes), BF16),
            VMEM((modes, slots), BF16),
            VMEM((hyper // wide - kept, 6, wide, modes), BF16),
            VMEM((hyper, slots), F32),
            *[VMEM((hyper, slots), BF16)] * 2,
            VMEM((ROWS, slots), F32),
            pltpu.SemaphoreType.DMA((hyper // wide - kept,)),
        ],
        raw=1,
    )

    if packed:
        answered = [lax.all_to_all(answer[0], "macro", 0, 0, tiled=True)]
    else:
        result, edges = answer
        here = lax.axis_index("macro")
        order = jnp.arange(hosts)[:, None, None]
        flat = result.reshape(ROWS, hosts, capacity).transpose(1, 0, 2).reshape(hosts, -1)
        tiles = pl.cdiv(flat.shape[1], lanes)
        flat = jnp.pad(flat, ((0, 0), (0, tiles * lanes - flat.shape[1])))
        joined = jnp.concatenate(
            [flat.reshape(hosts, tiles, lanes), jnp.where(order > here, edges[0], edges[1])], axis=1
        )
        joined = lax.all_to_all(joined, "macro", 0, 0, tiled=True)
        flat = joined[:, :tiles].reshape(hosts, -1)[:, : ROWS * capacity]
        result = flat.reshape(hosts, ROWS, capacity).transpose(1, 0, 2).reshape(ROWS, slots)
        low = lax.dynamic_index_in_dim(joined, jnp.maximum(here - 1, 0), 0, False)
        high = lax.dynamic_index_in_dim(joined, jnp.minimum(here + 1, hosts - 1), 0, False)
        answered = [result, jnp.stack([low[tiles:], high[tiles:]])]

    elastic = call(
        functools.partial(elastic_kernel, hosts, capacity),
        "elastic_forces",
        [shape_of(motion.shape), shape_of((7, 16, size_z)), shape_of((8, points), jnp.int32)],
        (motion, stiffness, elem, owner, first, second),
        [
            VMEM((3, size_x, 16, size_z), F32),
            VMEM((size_x, 16, size_z), F32),
            VMEM((6, size_x + 1, 16, size_z), F32),
        ],
    )

    force, tangent = call(
        functools.partial(final_kernel, packed, hosts, capacity),
        "final_forces",
        [shape_of(motion.shape), shape_of((36, points))],
        (*answered, x_second, x_first, *elastic),
        [
            VMEM((ROWS, points), F32),
            VMEM((3, 4, 16, size_z), F32),
            VMEM((2, 16, size_z), F32),
            VMEM((6, size_x + 1, 16, size_z), F32),
        ],
    )
    return (force, tangent)


def solution(mesh):
    return jax.shard_map(
        on_device,
        mesh=mesh,
        in_specs=(
            P(None, "macro", "micro", None),
            P("macro", "micro", None),
            P(("macro", "micro")),
            P(("macro", "micro")),
            P(("macro", "micro")),
            P(None, ("macro", "micro")),
            P("macro", None, None),
            P(),
            P(),
            P(),
        ),
        out_specs=(P(None, "macro", "micro", None), P(None, ("macro", "micro"))),
        check_vma=False,
    )
```

```python
import functools

import jax
import jax.numpy as jnp
from jax import lax
from jax.experimental import pallas as pl
from jax.experimental.pallas import tpu as pltpu
from jax.sharding import PartitionSpec as P

YIELD_STRESS = 1.5
HARDENING = 0.2
F32 = jnp.float32
BF16 = jnp.bfloat16
VMEM = pltpu.VMEM
ROWS = 32
UPPER = [(i, j) for i in range(6) for j in range(i, 6)]


def whole(*arrays):
    return [pl.BlockSpec(value.shape, lambda s, n=len(value.shape): (0,) * n) for value in arrays]


def in_hbm(value):
    return pltpu.with_memory_space_constraint(value, pltpu.HBM)


def iota(shape, dim):
    return lax.broadcasted_iota(jnp.int32, shape, dim)


def dot_t(left, right):
    return lax.dot_general(left, right, (((1,), (1,)), ((), ())), preferred_element_type=F32)


def pieces(value, count):
    out = []
    for _ in range(count):
        piece = value.astype(BF16)
        out.append(piece)
        value = value - piece.astype(F32)
    return out


def next_z(field):
    last = field.ndim - 1
    size = field.shape[last]
    rolled = pltpu.roll(field, size - 1, last)
    return jnp.where(iota(field.shape, last) == size - 1, 0.0, rolled)


def previous_z(field):
    last = field.ndim - 1
    rolled = pltpu.roll(field, 1, last)
    return jnp.where(iota(field.shape, last) == 0, 0.0, rolled)


def corners(field):
    y_up = pltpu.roll(field, field.shape[1] - 1, 1)
    return [field, y_up, next_z(field), next_z(y_up)]


def strains(lower, upper):
    grads = []
    for low, high in zip(lower, upper):
        dx = [b - a for a, b in zip(low, high)]
        grad_x = (dx[0] + dx[1] + dx[2] + dx[3]) * 0.25
        dy = [value[1] - value[0] for value in (low, high)]
        dy_z = [value[3] - value[2] for value in (low, high)]
        grad_y = (dy[0] + dy[1] + dy_z[0] + dy_z[1]) * 0.25
        dz = [value[2] - value[0] for value in (low, high)]
        dz_y = [value[3] - value[1] for value in (low, high)]
        grad_z = (dz[0] + dz[1] + dz_y[0] + dz_y[1]) * 0.25
        grads.append((grad_x, grad_y, grad_z))
    return [
        grads[0][0],
        grads[1][1],
        grads[2][2],
        grads[1][2] + grads[2][1],
        grads[0][2] + grads[2][0],
        grads[0][1] + grads[1][0],
    ]


def block_strains(fields):
    nodes = [corners(field) for field in fields]
    return strains(
        [[value[:-1] for value in four] for four in nodes],
        [[value[1:] for value in four] for four in nodes],
    )


def elastic_of(strain, stiffness):
    volume = strain[0] + strain[1] + strain[2]
    rest = volume - volume * (1.0 / 3.0)
    normal = [stiffness * (rest + strain[c]) for c in range(3)]
    return normal + [stiffness * (0.5 * strain[c]) for c in range(3, 6)]


def slots_of(owner, hosts, capacity):
    points = owner.shape[1]
    chosen = iota((hosts, points), 0) == owner
    host_hot = jnp.where(chosen, 1.0, 0.0)
    before = jnp.where(iota((points, points), 0) < iota((points, points), 1), 1.0, 0.0)
    counts = jnp.dot(host_hot.astype(BF16), before.astype(BF16), preferred_element_type=F32)
    position = jnp.sum(host_hot * counts, axis=0, keepdims=True).astype(jnp.int32)
    return host_hot, position, owner * capacity + position


def dispatch_kernel(hosts, capacity, direct, *refs):
    inputs, basis_ref, payload_out, refs = refs[:9], refs[9], refs[10], list(refs[11:])
    ids_ref = None if direct else refs.pop(0)
    first_ref, second_ref, x_first_ref, x_second_ref, blocks_ref = refs[:5]
    buffers, payload_ref, sems = refs[8:14] + refs[5:8], refs[14], refs[15]
    arrivals = [
        pltpu.make_async_copy(value, buffer, sems.at[n])
        for n, (value, buffer) in enumerate(zip(inputs, buffers))
    ]
    for copy in arrivals:
        copy.start()
    kept, _, wide, _ = blocks_ref.shape
    later = [
        pltpu.make_async_copy(
            basis_ref.at[:, pl.ds(n * wide, wide), :], blocks_ref.at[n], sems.at[10 + n]
        )
        for n in range(kept)
    ]
    for copy in later:
        copy.start()
    owner_ref, elem_ref, motion_ref, history_ref, pattern_ref, stiff_ref, map_ref, _, _ = buffers
    size_x, size_y, size_z = motion_ref.shape[1:]
    for copy in arrivals:
        copy.wait()
    owner = owner_ref[...]
    points = owner.shape[1]
    host_hot, position, slot = slots_of(owner, hosts, capacity)
    slot_total = hosts * capacity
    slot_hot = jnp.where(iota((slot_total, points), 0) == slot, 1.0, 0.0).astype(BF16)
    elem = elem_ref[...]
    column = elem // size_z
    depth = elem - column * size_z
    depth_hot = jnp.where(iota((size_z, points), 0) == depth, 1.0, 0.0).astype(BF16)
    rows = (size_x - 1) * size_y
    column_hot = iota((rows, points), 0) == column
    strain = block_strains([motion_ref[m] for m in range(3)])
    field = jnp.concatenate([value.reshape(rows, size_z) for value in strain], axis=0)
    picked = jnp.dot(field.astype(BF16), depth_hot, preferred_element_type=F32)
    macro_strain = jnp.concatenate(
        [
            jnp.sum(
                jnp.where(column_hot, picked[c * rows : (c + 1) * rows], 0.0),
                axis=0,
                keepdims=True,
            )
            for c in range(6)
        ],
        axis=0,
    ).astype(BF16)
    held = dot_t(slot_hot, history_ref[...])
    slot_strain = dot_t(slot_hot, macro_strain).astype(BF16)
    mapped = jnp.dot(slot_strain, map_ref[...], preferred_element_type=F32)
    sent = (mapped + held).astype(BF16)
    place = position + lax.axis_index("macro") * capacity
    modes = sent.shape[1]
    half = modes // 2
    place_hot = jnp.where(iota((modes, points), 0) == place, 1.0, 0.0).astype(BF16)
    ids = dot_t((host_hot * pattern_ref[...].astype(F32)).astype(BF16), place_hot)
    if direct:
        for h in range(hosts):
            mine = sent[h * capacity : (h + 1) * capacity]
            payload_ref[h, :capacity, :] = mine[:, :half]
            payload_ref[h, capacity : 2 * capacity, :] = mine[:, half:]
            row = iota((8, half), 0)
            low, high = ids[h : h + 1, :half], ids[h : h + 1, half:]
            tile = jnp.where(row == 0, low, jnp.where(row == 1, high, 0.0))
            payload_ref[h, 2 * capacity :, :] = tile.astype(BF16)
    else:
        payload_ref[...] = sent
        ids_ref[...] = ids.astype(BF16)
    leave = pltpu.make_async_copy(payload_ref, payload_out, sems.at[9])
    leave.start()
    stiffness = stiff_ref[...].astype(F32)
    even = lax.rem(lax.axis_index("micro"), 2) == 0
    for i in range(size_x):
        for m in range(4):
            if m < 3:
                up, down = motion_ref[m, i, size_y - 1 : size_y, :], motion_ref[m, i, 0:1, :]
            else:
                up = down = stiffness[i, size_y - 1 : size_y, :]
            first_ref[m, i : i + 1, :] = jnp.where(even, up, down)
            second_ref[m, i : i + 1, :] = jnp.where(even, down, up)
    even = lax.rem(lax.axis_index("macro"), 2) == 0
    for m in range(4):
        if m < 3:
            up, down = motion_ref[m, size_x - 1], motion_ref[m, 0]
        else:
            up = down = stiffness[size_x - 1]
        x_first_ref[m] = jnp.where(even, up, down)
        x_second_ref[m] = jnp.where(even, down, up)
    leave.wait()
    for copy in later:
        copy.wait()


def table_kernel(
    blocks_ref,
    map_ref,
    weights_ref,
    patterns_ref,
    basis_ref,
    table_ref,
    const_ref,
    bits_ref,
    others_ref,
    sems,
):
    hyper = weights_ref.shape[1]
    lanes = 128
    kept, _, wide, modes = blocks_ref.shape
    count = hyper // wide
    copies = []
    for n in range(kept, count):
        copy = pltpu.make_async_copy(
            basis_ref.at[:, pl.ds(n * wide, wide), :], others_ref.at[n - kept], sems.at[n - kept]
        )
        copy.start()
        copies.append(copy)
    weights = weights_ref[...]
    split = [piece.astype(F32) for piece in pieces(weights, 3)]
    row = iota((8, hyper), 0)
    stack = jnp.where(
        row == 0, split[0], jnp.where(row == 1, split[1], jnp.where(row == 2, split[2], 0.0))
    )
    choice = jnp.where(iota((8, lanes), 1) == iota((8, lanes), 0) + patterns_ref.shape[1], 1.0, 0.0)
    weight_lanes = lax.dot_general(
        stack.astype(BF16),
        choice.astype(BF16),
        (((0,), (0,)), ((), ())),
        preferred_element_type=F32,
    )
    patterns = patterns_ref[...]
    words, total = patterns.shape
    parts = [((patterns >> (8 * k)) & 255).astype(F32) for k in range(4)]
    spare = -4 * words % 8
    parts = jnp.concatenate(parts + [jnp.zeros((spare, total), F32)] * (spare > 0), axis=0)
    parts = jnp.concatenate([parts, jnp.zeros((parts.shape[0], lanes - total), F32)], axis=1)
    place = iota((1, 4 * words + spare), 1)
    part = jnp.where(place >= words, 1, 0) + jnp.where(place >= 2 * words, 1, 0)
    part = part + jnp.where(place >= 3 * words, 1, 0)
    start = 30 * (place - words * part) + 8 * part
    size = jnp.where(part == 3, 6, 8)
    after = iota((hyper, 4 * words + spare), 0) - start
    byte_hot = jnp.where((after >= 0) & (after < size), 1.0, 0.0).astype(BF16)
    value = jnp.dot(byte_hot, parts.astype(BF16), preferred_element_type=F32).astype(jnp.int32)
    index = iota((hyper, lanes), 0)
    offset = index - 30 * ((index * 2185) >> 16)
    bits_ref[...] = (((value >> (offset & 7)) & 1).astype(F32) + weight_lanes).astype(BF16)

    modes_map = map_ref[...]
    modes_map = jnp.concatenate(
        [modes_map.astype(F32), jnp.zeros((2, modes), F32)], axis=0
    ).astype(BF16)
    sums = jnp.zeros((48, wide), F32)
    for n in range(count):
        if n >= kept:
            copies[n - kept].wait()
        source = blocks_ref.at[n] if n < kept else others_ref.at[n - kept]
        part = slice(n * wide, (n + 1) * wide)
        local = [dot_t(modes_map, source[c]) for c in range(6)]
        trace = local[0] + local[1] + local[2]
        third = trace / 3.0
        shaped = [local[c] - third for c in range(3)] + [0.5 * local[c] for c in range(3, 6)]
        weight = weights[:, part]
        shaped = [weight * value for value in shaped]
        weighted_trace = weight * trace
        blocks, adds = [], []
        for i in range(6):
            entry = local[0][i : i + 1] * shaped[0]
            for c in range(1, 6):
                entry = entry + local[c][i : i + 1] * shaped[c]
            blocks.append(entry)
            adds.append(entry + trace[i : i + 1] * weighted_trace)
        sums = sums + jnp.concatenate(adds, axis=0)
        high, low = pieces(jnp.concatenate(blocks, axis=0), 2)
        table_ref[0:48, part] = high
        table_ref[48:96, part] = low
    const_ref[...] = jnp.broadcast_to(jnp.sum(sums, axis=1, keepdims=True), const_ref.shape)


def sides_of(first_ref, second_ref, axis, m, at=None):
    even = lax.rem(lax.axis_index(axis), 2) == 0
    rows = slice(None) if at is None else slice(at, at + 1)
    first, second = first_ref[m, rows, :], second_ref[m, rows, :]
    return jnp.where(even, second, first), jnp.where(even, first, second)


def micro_kernel(
    packed,
    hosts,
    capacity,
    flag_lanes,
    received_ref,
    first_ref,
    second_ref,
    const_ref,
    bits_ref,
    table_ref,
    blocks_ref,
    basis_ref,
    answer_ref,
    *rest,
):
    if packed:
        corners_ref = None
    else:
        corners_ref, *rest = rest
    (
        state_ref,
        hot_ref,
        others_ref,
        flags_ref,
        high_ref,
        low_ref,
        result_ref,
        sems,
    ) = rest
    groups = received_ref.shape[0]
    slots = groups * capacity
    kept, _, block, modes = blocks_ref.shape
    half = modes // 2
    count = kept + others_ref.shape[0]
    copies = []
    for n in range(count - kept):
        part = pl.ds((kept + n) * block, block)
        copies.append(
            pltpu.make_async_copy(basis_ref.at[:, part, :], others_ref.at[n], sems.at[n])
        )
        copies[n].start()

    ids = jnp.zeros((8, half), F32)
    for h in range(groups):
        own = pl.ds(h * capacity, capacity)
        state_ref[own, :half] = received_ref[h, :capacity, :]
        state_ref[own, half:] = received_ref[h, capacity : 2 * capacity, :]
        ids = ids + received_ref[h, 2 * capacity :, :].astype(F32)
    ids = jnp.concatenate([ids[0:1], ids[1:2]], axis=1).astype(jnp.int32)
    hot_ref[...] = jnp.where(iota(hot_ref.shape, 0) == ids, 1.0, 0.0).astype(BF16)

    def solve(*accumulators):
        mains = (accumulators[:8], accumulators[8:12])
        spares = accumulators[12:16]
        tangent_high, tangent_low = accumulators[16:]
        hyper = bits_ref.shape[0]
        empty = jnp.zeros((128, modes - bits_ref.shape[1]), BF16)
        blocks_of_flags = hyper // 128

        def flags_of(j):
            rows = jnp.concatenate([bits_ref[128 * j : 128 * j + 128, :], empty], axis=1)
            pltpu.matmul_acc_lhs(spares[j % 4], rows, load_staged_rhs=None if j else 0)

        def keep_flags(j):
            flags_ref[128 * j : 128 * j + 128, :] = pltpu.matmul_pop(spares[j % 4])

        def place(i):
            if i < 8:
                return mains[0][i]
            k = (i - 8) // 2
            return mains[0][k % 8] if i % 2 else mains[1][k % 4]

        strip = 16
        strips = hyper // strip

        def issue(i):
            n, r = divmod(i * strip, block)
            if n >= kept and r == 0:
                copies[n - kept].wait()
            source = blocks_ref.at[n] if n < kept else others_ref.at[n - kept]
            rows = jnp.concatenate([source[c, r : r + strip, :] for c in range(6)], axis=0)
            pltpu.matmul_acc_lhs(place(i), rows, load_staged_rhs=0 if i in (0, 8) else None)

        def respond(i, sums):
            strain = pltpu.matmul_pop(place(i))
            e = [strain[c * strip : (c + 1) * strip] for c in range(6)]
            at = slice(i * strip, (i + 1) * strip)
            volume = e[0] + e[1] + e[2]
            third = volume * (1.0 / 3.0)
            d = [e[c] - third for c in range(3)]
            normal = d[0] * d[0] + d[1] * d[1] + d[2] * d[2]
            shear = e[3] * e[3] + e[4] * e[4] + e[5] * e[5]
            square = jnp.maximum(normal + 0.5 * shear, YIELD_STRESS * YIELD_STRESS)
            factor = (YIELD_STRESS * (1.0 - HARDENING)) * lax.rsqrt(square) + (HARDENING - 1.0)
            change = flags_ref[at, :] * factor
            high = change.astype(BF16)
            high_ref[at, :] = high
            low_ref[at, :] = (change - high.astype(F32)).astype(BF16)
            packed_row = bits_ref[at, :].astype(F32)
            lane = iota(packed_row.shape, 1)
            packed_row = jnp.where((lane >= flag_lanes) & (lane < flag_lanes + 3), packed_row, 0.0)
            weight = jnp.sum(packed_row, axis=1, keepdims=True)
            scaled = weight + weight * change
            terms = [scaled * d[c] for c in range(3)] + [scaled * e[c] for c in range(3, 6)]
            terms.append(weight * volume)
            return [total + (term[:8] + term[8:]) for total, term in zip(sums, terms)]

        sums = [jnp.zeros((8, slots), F32)] * 7
        ahead = 7
        pltpu.matmul_push_rhs(hot_ref[...], 0, 1)
        pltpu.matmul_push_rhs(state_ref[...], 0, 0, transpose=True)
        for j in range(4):
            flags_of(j)
        for i in range(8):
            issue(i)
        for j in range(blocks_of_flags):
            keep_flags(j)
            if j + 4 < blocks_of_flags:
                flags_of(j + 4)
        pltpu.matmul_push_rhs(state_ref[...], 0, 1, transpose=True)
        for i in range(strips):
            if 8 <= i + ahead < strips:
                issue(i + ahead)
            sums = respond(i, sums)
        for n in range(hyper // modes):
            part = slice(n * modes, (n + 1) * modes)
            pltpu.matmul_push_rhs(high_ref[part, :], 0, 0)
            pltpu.matmul_push_rhs(low_ref[part, :], 0, 1)
            pltpu.matmul_acc_lhs(tangent_high, table_ref[:, part], load_staged_rhs=0)
            pltpu.matmul_acc_lhs(tangent_low, table_ref[0:48, part], load_staged_rhs=0)
        both_parts = pltpu.matmul_pop(tangent_high)
        tangent = both_parts[:48] + (both_parts[48:] + pltpu.matmul_pop(tangent_low))
        return tangent, sums

    tangent, sums = pl.run_scoped(
        solve,
        *[pltpu.ACC(0)((96, slots), F32) for _ in range(8)],
        *[pltpu.ACC(1)((96, slots), F32) for _ in range(4)],
        *[pltpu.ACC(1)((128, slots), F32) for _ in range(4)],
        pltpu.ACC(0)((96, slots), F32),
        pltpu.ACC(1)((48, slots), F32),
    )

    volume = jnp.sum(sums[6], axis=0, keepdims=True)
    for c in range(6):
        total = jnp.sum(sums[c], axis=0, keepdims=True)
        result_ref[c : c + 1, :] = total + volume if c < 3 else 0.5 * total
    const = const_ref[...]
    const = jnp.concatenate([const] * (slots // const.shape[1]), axis=1)
    tangent = tangent + const
    at = 6
    for i in range(6):
        result_ref[at : at + 6 - i, :] = tangent[8 * i + i : 8 * i + 6]
        at += 6 - i
    result_ref[at:, :] = jnp.zeros((ROWS - at, slots), F32)

    last = first_ref.shape[1] - 1

    def corner_rows(write):
        for m in range(4):
            up = sides_of(first_ref, second_ref, "micro", m, last)
            down = sides_of(first_ref, second_ref, "micro", m, 0)
            for n in range(2):
                write(0, 2 * m + n, up[n])
                write(1, 2 * m + n, down[n])

    if packed:
        here = lax.axis_index("macro")
        group_of = iota((8, 128), 1) // capacity
        for h in range(hosts):
            chunk = jnp.zeros((8, 128), F32)
            tile, place = divmod(h * capacity, 128)
            for g in range(4):
                piece = result_ref[8 * g : 8 * g + 8, tile * 128 : (tile + 1) * 128]
                shift = (g * capacity - place) % 128
                if shift:
                    piece = pltpu.roll(piece, shift, 1)
                chunk = jnp.where(group_of == g, piece, chunk)
            answer_ref[h, 0:8, :] = chunk
        chunks = [jnp.minimum(here + 1, hosts - 1), jnp.maximum(here - 1, 0)]

        def write(side, row, value):
            answer_ref[chunks[side], 8 + row : 9 + row, :] = value
    else:
        answer_ref[...] = result_ref[...]

        def write(side, row, value):
            corners_ref[side, row : row + 1, :] = value

    corner_rows(write)


def assemble(stress):
    ready = []
    for here, low in stress:
        ready.append((here, low, previous_z(here), previous_z(low)))

    def at(c, sign_x, sign_y, sign_z):
        here, low, here_z, low_z = ready[c]
        if sign_z:
            near, far = here_z - here, low_z - low
        else:
            near, far = here_z + here, low_z + low
        both = far - near if sign_y else far + near
        return both[:-1] - both[1:] if sign_x else both[:-1] + both[1:]

    force = [
        at(0, 1, 0, 0) + at(5, 0, 1, 0) + at(4, 0, 0, 1),
        at(5, 1, 0, 0) + at(1, 0, 1, 0) + at(3, 0, 0, 1),
        at(4, 1, 0, 0) + at(3, 0, 1, 0) + at(2, 0, 0, 1),
    ]
    return [0.25 * value for value in force]


def elastic_kernel(
    hosts,
    capacity,
    motion_ref,
    stiff_ref,
    elem_ref,
    owner_ref,
    first_ref,
    second_ref,
    force_ref,
    edge_ref,
    index_ref,
    node_ref,
    wide_ref,
    stress_ref,
):
    size_x, size_y, size_z = motion_ref.shape[1:]
    node_ref[...] = jnp.zeros_like(node_ref)
    wide_ref[...] = jnp.zeros_like(wide_ref)
    stiffness = stiff_ref[...].astype(F32)
    elem, owner = elem_ref[...], owner_ref[...]
    points = elem.shape[1]
    column = elem // size_z
    depth = elem - column * size_z
    index_ref[0:1, :] = slots_of(owner, hosts, capacity)[2]
    index_ref[1:2, :] = column
    index_ref[2:3, :] = depth
    index_ref[3:, :] = jnp.zeros((5, points), jnp.int32)
    depth_hot = jnp.where(iota((size_z, points), 0) == depth, 1.0, 0.0).astype(BF16)
    column_hot = jnp.where(iota((size_x * size_y, points), 0) == column, 1.0, 0.0).astype(BF16)
    listed = dot_t(column_hot, depth_hot)
    for i in range(size_x):
        for m in range(3):
            low, high = sides_of(first_ref, second_ref, "micro", m, i)
            node_ref[m, i, 0:1, :] = low
            node_ref[m, i, 1 : size_y + 1, :] = motion_ref[m, i]
            node_ref[m, i, size_y + 1 : size_y + 2, :] = high
        low, _ = sides_of(first_ref, second_ref, "micro", 3, i)
        wide_ref[i, 0:1, :] = low
        keep = 1.0 - listed[i * size_y : (i + 1) * size_y]
        wide_ref[i, 1 : size_y + 1, :] = stiffness[i] * keep
    for m in range(3):
        edge_ref[m] = node_ref[m, 0]
        edge_ref[3 + m] = node_ref[m, size_x - 1]
    edge_ref[6] = wide_ref[size_x - 1]
    strain = block_strains([node_ref[m] for m in range(3)])
    stress = elastic_of(strain, wide_ref[: size_x - 1])
    for c in range(6):
        stress_ref[c, 0] = jnp.zeros(stress_ref.shape[2:], F32)
        stress_ref[c, 1:size_x] = stress[c]
        stress_ref[c, size_x] = jnp.zeros(stress_ref.shape[2:], F32)
    force = assemble(
        [(stress_ref[c, :, 1 : size_y + 1, :], stress_ref[c, :, 0:size_y, :]) for c in range(6)]
    )
    for m in range(3):
        force_ref[m] = force[m]


def final_kernel(packed, hosts, capacity, answer_ref, *rest):
    if packed:
        corners_ref = None
    else:
        corners_ref, *rest = rest
    (
        second_ref,
        first_ref,
        elastic_ref,
        edge_ref,
        index_ref,
        force_ref,
        tangent_ref,
        result_ref,
        node_ref,
        wide_ref,
        stress_ref,
    ) = rest
    size_x, size_y, size_z = elastic_ref.shape[1:]
    slot, column, depth = index_ref[0:1, :], index_ref[1:2, :], index_ref[2:3, :]
    points = slot.shape[1]
    slot_total = hosts * capacity
    if packed:
        group_of = iota((8, 128), 1) // capacity
        per_tile = 128 // capacity
        groups = []
        for g in range(4):
            tiles = []
            for t in range(hosts // per_tile):
                tile = jnp.zeros((8, 128), F32)
                for n in range(per_tile):
                    piece = answer_ref[t * per_tile + n, 0:8, :]
                    shift = ((n - g) * capacity) % 128
                    if shift:
                        piece = pltpu.roll(piece, shift, 1)
                    tile = jnp.where(group_of == n, piece, tile)
                tiles.append(tile)
            groups.append(jnp.concatenate(tiles, axis=1))
        answer = jnp.concatenate(groups, axis=0)
    else:
        answer = answer_ref[...]
    slot_hot = jnp.where(iota((slot_total, points), 0) == slot, 1.0, 0.0).astype(BF16)
    parts = jnp.concatenate(pieces(answer, 3), axis=0)
    chosen = jnp.dot(parts, slot_hot, preferred_element_type=F32)
    result = chosen[:ROWS] + (chosen[ROWS : 2 * ROWS] + chosen[2 * ROWS :])
    result_ref[...] = result
    for i in range(6):
        for j in range(6):
            at = 6 + UPPER.index((min(i, j), max(i, j)))
            tangent_ref[6 * i + j : 6 * i + j + 1, :] = result_ref[at : at + 1, :]

    here = lax.axis_index("macro")
    inner = [here > 0, here < hosts - 1]
    from_chunk = [jnp.maximum(here - 1, 0), jnp.minimum(here + 1, hosts - 1)]

    def corner(side, row):
        if packed:
            value = answer_ref[from_chunk[side], 8 + row : 9 + row, :]
        else:
            value = corners_ref[side, row : row + 1, :]
        return jnp.where(inner[side], value, 0.0)

    node_ref[...] = jnp.zeros_like(node_ref)
    wide_ref[...] = jnp.zeros_like(wide_ref)
    for m in range(3):
        faces = sides_of(first_ref, second_ref, "macro", m)
        for side, at in ((0, 0), (1, 3)):
            node_ref[m, at, 0:1, :] = corner(side, 2 * m)
            node_ref[m, at, 1 : size_y + 1, :] = faces[side]
            node_ref[m, at, size_y + 1 : size_y + 2, :] = corner(side, 2 * m + 1)
        node_ref[m, 1] = edge_ref[m]
        node_ref[m, 2] = edge_ref[3 + m]
    wide_ref[0, 0:1, :] = corner(0, 6)
    wide_ref[0, 1 : size_y + 1, :] = sides_of(first_ref, second_ref, "macro", 3)[0]
    wide_ref[1] = edge_ref[6]
    lower, upper = [], []
    for m in range(3):
        four = corners(node_ref[m])
        lower.append([jnp.stack([value[0], value[2]]) for value in four])
        upper.append([jnp.stack([value[1], value[3]]) for value in four])
    edge = elastic_of(strains(lower, upper), wide_ref[...])
    rows = (size_x - 1) * size_y
    depth_hot = jnp.where(iota((size_z, points), 0) == depth, 1.0, 0.0).astype(BF16)
    column_hot = iota((rows, points), 0) == column
    stress_ref[:, 1:size_x, 0:1, :] = jnp.zeros((6, size_x - 1, 1, size_z), F32)
    placed = [jnp.where(column_hot, result[c : c + 1], 0.0) for c in range(6)]
    placed = jnp.concatenate(pieces(jnp.concatenate(placed, axis=0), 2), axis=0)
    fields = dot_t(placed, depth_hot)
    for c in range(6):
        field = fields[c * rows : (c + 1) * rows] + fields[(6 + c) * rows : (7 + c) * rows]
        stress_ref[c, 1:size_x, 1 : size_y + 1, :] = field.reshape(size_x - 1, size_y, size_z)
        stress_ref[c, 0] = edge[c][0]
        stress_ref[c, size_x] = edge[c][1]
    force = assemble(
        [(stress_ref[c, :, 1 : size_y + 1, :], stress_ref[c, :, 0:size_y, :]) for c in range(6)]
    )
    for m in range(3):
        force_ref[m] = elastic_ref[m] + force[m]


def shape_of(shape, dtype=F32):
    return jax.ShapeDtypeStruct(shape, dtype)


def call(kernel, name, out_shape, args, scratch=(), flops=10**8, raw=0, raw_out=0):
    specs = whole(*args[: len(args) - raw]) + [pl.BlockSpec(memory_space=pl.ANY)] * raw
    return pl.pallas_call(
        kernel,
        grid=(1,),
        out_shape=out_shape,
        in_specs=specs,
        out_specs=[pl.BlockSpec(memory_space=pl.ANY)] * raw_out + whole(*out_shape[raw_out:]),
        scratch_shapes=scratch,
        compiler_params=pltpu.CompilerParams(vmem_limit_bytes=24 * 2**20),
        cost_estimate=pl.CostEstimate(flops=flops, bytes_accessed=2**20, transcendentals=0),
        name=name,
    )(*args)


def on_device(
    motion,
    stiffness,
    point_elem,
    point_owner,
    point_pattern,
    history,
    basis,
    mode_map,
    weights,
    patterns,
):
    size_x, size_y, size_z = motion.shape[1:]
    points = point_elem.shape[0]
    hosts = lax.axis_size("macro")
    capacity = 2 * points // hosts
    slots = capacity * hosts
    modes = mode_map.shape[0]
    half = modes // 2
    hyper = weights.shape[0]
    lanes = 128
    direct = capacity % 16 == 0
    packed = capacity * 4 == lanes and slots % lanes == 0
    motion = in_hbm(motion)
    stiffness = in_hbm(stiffness)
    elem = in_hbm(point_elem.reshape(1, points))
    owner = in_hbm(point_owner.reshape(1, points))
    pattern = in_hbm(point_pattern.reshape(1, points))
    history = in_hbm(history)
    map_rows = in_hbm(mode_map.T)

    rows = in_hbm(basis.reshape(6, hyper, modes))
    wide, kept = 256, 3
    sent = (
        [shape_of((hosts, 2 * capacity + 8, half), BF16)]
        if direct
        else [shape_of((slots, modes), BF16), shape_of((hosts, modes), BF16)]
    )
    swap, x_swap = shape_of((4, size_x, size_z)), shape_of((4, size_y, size_z))
    arguments = (owner, elem, motion, history, pattern, stiffness)
    small = (map_rows, in_hbm(weights.reshape(1, hyper)), in_hbm(patterns.T))
    *payload, first, second, x_first, x_second, blocks, map_here, weights, bit_words = call(
        functools.partial(dispatch_kernel, hosts, capacity, direct),
        "dispatch",
        sent
        + [swap, swap, x_swap, x_swap, shape_of((kept, 6, wide, modes), BF16)]
        + [shape_of(value.shape, value.dtype) for value in small],
        (*arguments, *small, rows),
        [VMEM(value.shape, value.dtype) for value in (*arguments, sent[0])]
        + [pltpu.SemaphoreType.DMA((10 + kept,))],
        raw=10,
        raw_out=1,
    )

    if direct:
        received = lax.all_to_all(payload[0], "macro", 0, 0, tiled=True)
        groups, group = hosts, capacity
    else:
        slot_rows, ids = payload
        joined = jnp.concatenate(
            [
                slot_rows[:, :half].reshape(hosts, capacity, half),
                slot_rows[:, half:].reshape(hosts, capacity, half),
                ids.reshape(hosts, 2, half),
            ],
            axis=1,
        )
        joined = lax.all_to_all(joined, "macro", 0, 0, tiled=True)
        ids = jnp.sum(joined[:, 2 * capacity :].astype(F32), axis=0).astype(BF16)
        received = jnp.concatenate(
            [
                joined[:, :capacity].reshape(1, slots, half),
                joined[:, capacity : 2 * capacity].reshape(1, slots, half),
                jnp.pad(ids, ((0, 6), (0, 0)))[None],
            ],
            axis=1,
        )
        groups, group = 1, slots

    def swapped(value, axis, start):
        pairs = [(i, i + 1) for i in range(start, lax.axis_size(axis) - 1, 2)]
        return lax.ppermute(value, axis, pairs + [(b, a) for a, b in pairs])

    first, second = swapped(first, "micro", 0), swapped(second, "micro", 1)
    x_first, x_second = swapped(x_first, "macro", 0), swapped(x_second, "macro", 1)

    table, const, bits = call(
        table_kernel,
        "tables",
        [
            shape_of((96, hyper), BF16),
            shape_of((48, lanes)),
            shape_of((hyper, lanes), BF16),
        ],
        (blocks, map_here, weights, bit_words, rows),
        [
            VMEM((hyper // wide - kept, 6, wide, modes), BF16),
            pltpu.SemaphoreType.DMA((hyper // wide - kept,)),
        ],
        raw=1,
    )

    answer = call(
        functools.partial(micro_kernel, packed, hosts, group, patterns.shape[0]),
        "micro_response",
        [shape_of((hosts, 16, lanes))]
        if packed
        else [shape_of((ROWS, slots)), shape_of((2, 8, lanes))],
        (
            received,
            first,
            second,
            const,
            bits,
            table,
            blocks,
            rows,
        ),
        [
            VMEM((slots, modes), BF16),
            VMEM((modes, slots), BF16),
            VMEM((hyper // wide - kept, 6, wide, modes), BF16),
            VMEM((hyper, slots), F32),
            *[VMEM((hyper, slots), BF16)] * 2,
            VMEM((ROWS, slots), F32),
            pltpu.SemaphoreType.DMA((hyper // wide - kept,)),
        ],
        raw=1,
    )

    if packed:
        answered = [lax.all_to_all(answer[0], "macro", 0, 0, tiled=True)]
    else:
        result, edges = answer
        here = lax.axis_index("macro")
        order = jnp.arange(hosts)[:, None, None]
        flat = result.reshape(ROWS, hosts, capacity).transpose(1, 0, 2).reshape(hosts, -1)
        tiles = pl.cdiv(flat.shape[1], lanes)
        flat = jnp.pad(flat, ((0, 0), (0, tiles * lanes - flat.shape[1])))
        joined = jnp.concatenate(
            [flat.reshape(hosts, tiles, lanes), jnp.where(order > here, edges[0], edges[1])], axis=1
        )
        joined = lax.all_to_all(joined, "macro", 0, 0, tiled=True)
        flat = joined[:, :tiles].reshape(hosts, -1)[:, : ROWS * capacity]
        result = flat.reshape(hosts, ROWS, capacity).transpose(1, 0, 2).reshape(ROWS, slots)
        low = lax.dynamic_index_in_dim(joined, jnp.maximum(here - 1, 0), 0, False)
        high = lax.dynamic_index_in_dim(joined, jnp.minimum(here + 1, hosts - 1), 0, False)
        answered = [result, jnp.stack([low[tiles:], high[tiles:]])]

    elastic = call(
        functools.partial(elastic_kernel, hosts, capacity),
        "elastic_forces",
        [shape_of(motion.shape), shape_of((7, 16, size_z)), shape_of((8, points), jnp.int32)],
        (motion, stiffness, elem, owner, first, second),
        [
            VMEM((3, size_x, 16, size_z), F32),
            VMEM((size_x, 16, size_z), F32),
            VMEM((6, size_x + 1, 16, size_z), F32),
        ],
    )

    force, tangent = call(
        functools.partial(final_kernel, packed, hosts, capacity),
        "final_forces",
        [shape_of(motion.shape), shape_of((36, points))],
        (*answered, x_second, x_first, *elastic),
        [
            VMEM((ROWS, points), F32),
            VMEM((3, 4, 16, size_z), F32),
            VMEM((2, 16, size_z), F32),
            VMEM((6, size_x + 1, 16, size_z), F32),
        ],
    )
    return (force, tangent)


def solution(mesh):
    return jax.shard_map(
        on_device,
        mesh=mesh,
        in_specs=(
            P(None, "macro", "micro", None),
            P("macro", "micro", None),
            P(("macro", "micro")),
            P(("macro", "micro")),
            P(("macro", "micro")),
            P(None, ("macro", "micro")),
            P("macro", None, None),
            P(),
            P(),
            P(),
        ),
        out_specs=(P(None, "macro", "micro", None), P(None, ("macro", "micro"))),
        check_vma=False,
    )
```

```python
import functools

import jax
import jax.numpy as jnp
from jax import lax
from jax.experimental import pallas as pl
from jax.experimental.pallas import tpu as pltpu
from jax.sharding import PartitionSpec as P

YIELD_STRESS = 1.5
HARDENING = 0.2
FACTOR = YIELD_STRESS * (1.0 - HARDENING) * 0.5**0.5
F32 = jnp.float32
BF16 = jnp.bfloat16
VMEM = pltpu.VMEM
ROWS = 32
UPPER = [(i, j) for i in range(6) for j in range(i, 6)]


def whole(*arrays):
    return [pl.BlockSpec(value.shape, lambda s, n=len(value.shape): (0,) * n) for value in arrays]


def in_hbm(value):
    return pltpu.with_memory_space_constraint(value, pltpu.HBM)


def iota(shape, dim):
    return lax.broadcasted_iota(jnp.int32, shape, dim)


def dot_t(left, right):
    return lax.dot_general(left, right, (((1,), (1,)), ((), ())), preferred_element_type=F32)


def pieces(value, count):
    out = []
    for _ in range(count):
        piece = value.astype(BF16)
        out.append(piece)
        value = value - piece.astype(F32)
    return out


def next_z(field):
    last = field.ndim - 1
    size = field.shape[last]
    rolled = pltpu.roll(field, size - 1, last)
    return jnp.where(iota(field.shape, last) == size - 1, 0.0, rolled)


def previous_z(field):
    last = field.ndim - 1
    rolled = pltpu.roll(field, 1, last)
    return jnp.where(iota(field.shape, last) == 0, 0.0, rolled)


def corners(field):
    y_up = pltpu.roll(field, field.shape[1] - 1, 1)
    return [field, y_up, next_z(field), next_z(y_up)]


def strains(lower, upper):
    grads = []
    for low, high in zip(lower, upper):
        dx = [b - a for a, b in zip(low, high)]
        grad_x = (dx[0] + dx[1] + dx[2] + dx[3]) * 0.25
        dy = [value[1] - value[0] for value in (low, high)]
        dy_z = [value[3] - value[2] for value in (low, high)]
        grad_y = (dy[0] + dy[1] + dy_z[0] + dy_z[1]) * 0.25
        dz = [value[2] - value[0] for value in (low, high)]
        dz_y = [value[3] - value[1] for value in (low, high)]
        grad_z = (dz[0] + dz[1] + dz_y[0] + dz_y[1]) * 0.25
        grads.append((grad_x, grad_y, grad_z))
    return [
        grads[0][0],
        grads[1][1],
        grads[2][2],
        grads[1][2] + grads[2][1],
        grads[0][2] + grads[2][0],
        grads[0][1] + grads[1][0],
    ]


def block_strains(fields):
    nodes = [corners(field) for field in fields]
    return strains(
        [[value[:-1] for value in four] for four in nodes],
        [[value[1:] for value in four] for four in nodes],
    )


def elastic_of(strain, stiffness):
    volume = strain[0] + strain[1] + strain[2]
    rest = volume - volume * (1.0 / 3.0)
    normal = [stiffness * (rest + strain[c]) for c in range(3)]
    return normal + [stiffness * (0.5 * strain[c]) for c in range(3, 6)]


def slots_of(owner, hosts, capacity):
    points = owner.shape[1]
    chosen = iota((hosts, points), 0) == owner
    host_hot = jnp.where(chosen, 1.0, 0.0)
    before = jnp.where(iota((points, points), 0) < iota((points, points), 1), 1.0, 0.0)
    counts = jnp.dot(host_hot.astype(BF16), before.astype(BF16), preferred_element_type=F32)
    position = jnp.sum(host_hot * counts, axis=0, keepdims=True).astype(jnp.int32)
    return host_hot, position, owner * capacity + position


def dispatch_kernel(hosts, capacity, direct, *refs):
    inputs, basis_ref, payload_out, refs = refs[:9], refs[9], refs[10], list(refs[11:])
    ids_ref = None if direct else refs.pop(0)
    first_ref, second_ref, x_first_ref, x_second_ref, blocks_ref = refs[:5]
    buffers, payload_ref, sems = refs[8:14] + refs[5:8], refs[14], refs[15]
    arrivals = [
        pltpu.make_async_copy(value, buffer, sems.at[n])
        for n, (value, buffer) in enumerate(zip(inputs, buffers))
    ]
    for copy in arrivals:
        copy.start()
    kept, _, wide, _ = blocks_ref.shape
    later = [
        pltpu.make_async_copy(
            basis_ref.at[:, pl.ds(n * wide, wide), :], blocks_ref.at[n], sems.at[10 + n]
        )
        for n in range(kept)
    ]
    for copy in later:
        copy.start()
    owner_ref, elem_ref, motion_ref, history_ref, pattern_ref, stiff_ref, map_ref, _, _ = buffers
    size_x, size_y, size_z = motion_ref.shape[1:]
    for copy in arrivals:
        copy.wait()
    owner = owner_ref[...]
    points = owner.shape[1]
    host_hot, position, slot = slots_of(owner, hosts, capacity)
    slot_total = hosts * capacity
    slot_hot = jnp.where(iota((slot_total, points), 0) == slot, 1.0, 0.0).astype(BF16)
    elem = elem_ref[...]
    column = elem // size_z
    depth = elem - column * size_z
    depth_hot = jnp.where(iota((size_z, points), 0) == depth, 1.0, 0.0).astype(BF16)
    rows = (size_x - 1) * size_y
    column_hot = iota((rows, points), 0) == column
    strain = block_strains([motion_ref[m] for m in range(3)])
    field = jnp.concatenate([value.reshape(rows, size_z) for value in strain], axis=0)
    picked = jnp.dot(field.astype(BF16), depth_hot, preferred_element_type=F32)
    macro_strain = jnp.concatenate(
        [
            jnp.sum(
                jnp.where(column_hot, picked[c * rows : (c + 1) * rows], 0.0),
                axis=0,
                keepdims=True,
            )
            for c in range(6)
        ],
        axis=0,
    ).astype(BF16)
    held = dot_t(slot_hot, history_ref[...])
    slot_strain = dot_t(slot_hot, macro_strain).astype(BF16)
    mapped = jnp.dot(slot_strain, map_ref[...], preferred_element_type=F32)
    sent = (mapped + held).astype(BF16)
    place = position + lax.axis_index("macro") * capacity
    modes = sent.shape[1]
    half = modes // 2
    place_hot = jnp.where(iota((modes, points), 0) == place, 1.0, 0.0).astype(BF16)
    ids = dot_t((host_hot * pattern_ref[...].astype(F32)).astype(BF16), place_hot)
    if direct:
        for h in range(hosts):
            mine = sent[h * capacity : (h + 1) * capacity]
            payload_ref[h, :capacity, :] = mine[:, :half]
            payload_ref[h, capacity : 2 * capacity, :] = mine[:, half:]
            row = iota((8, half), 0)
            low, high = ids[h : h + 1, :half], ids[h : h + 1, half:]
            tile = jnp.where(row == 0, low, jnp.where(row == 1, high, 0.0))
            payload_ref[h, 2 * capacity :, :] = tile.astype(BF16)
    else:
        payload_ref[...] = sent
        ids_ref[...] = ids.astype(BF16)
    leave = pltpu.make_async_copy(payload_ref, payload_out, sems.at[9])
    leave.start()
    stiffness = stiff_ref[...].astype(F32)
    even = lax.rem(lax.axis_index("micro"), 2) == 0
    for i in range(size_x):
        for m in range(4):
            if m < 3:
                up, down = motion_ref[m, i, size_y - 1 : size_y, :], motion_ref[m, i, 0:1, :]
            else:
                up = down = stiffness[i, size_y - 1 : size_y, :]
            first_ref[m, i : i + 1, :] = jnp.where(even, up, down)
            second_ref[m, i : i + 1, :] = jnp.where(even, down, up)
    even = lax.rem(lax.axis_index("macro"), 2) == 0
    for m in range(4):
        if m < 3:
            up, down = motion_ref[m, size_x - 1], motion_ref[m, 0]
        else:
            up = down = stiffness[size_x - 1]
        x_first_ref[m] = jnp.where(even, up, down)
        x_second_ref[m] = jnp.where(even, down, up)
    leave.wait()
    for copy in later:
        copy.wait()


def table_kernel(
    blocks_ref,
    map_ref,
    weights_ref,
    patterns_ref,
    basis_ref,
    table_ref,
    const_ref,
    bits_ref,
    others_ref,
    sems,
):
    hyper = weights_ref.shape[1]
    lanes = 128
    kept, _, wide, modes = blocks_ref.shape
    count = hyper // wide
    copies = []
    for n in range(kept, count):
        copy = pltpu.make_async_copy(
            basis_ref.at[:, pl.ds(n * wide, wide), :], others_ref.at[n - kept], sems.at[n - kept]
        )
        copy.start()
        copies.append(copy)
    weights = weights_ref[...]
    split = [piece.astype(F32) for piece in pieces(weights, 3)]
    row = iota((8, hyper), 0)
    stack = jnp.where(
        row == 0, split[0], jnp.where(row == 1, split[1], jnp.where(row == 2, split[2], 0.0))
    )
    choice = jnp.where(iota((8, lanes), 1) == iota((8, lanes), 0) + patterns_ref.shape[1], 1.0, 0.0)
    weight_lanes = lax.dot_general(
        stack.astype(BF16),
        choice.astype(BF16),
        (((0,), (0,)), ((), ())),
        preferred_element_type=F32,
    )
    patterns = patterns_ref[...]
    words, total = patterns.shape
    parts = [((patterns >> (8 * k)) & 255).astype(F32) for k in range(4)]
    spare = -4 * words % 8
    parts = jnp.concatenate(parts + [jnp.zeros((spare, total), F32)] * (spare > 0), axis=0)
    parts = jnp.concatenate([parts, jnp.zeros((parts.shape[0], lanes - total), F32)], axis=1)
    place = iota((1, 4 * words + spare), 1)
    part = jnp.where(place >= words, 1, 0) + jnp.where(place >= 2 * words, 1, 0)
    part = part + jnp.where(place >= 3 * words, 1, 0)
    start = 30 * (place - words * part) + 8 * part
    size = jnp.where(part == 3, 6, 8)
    after = iota((hyper, 4 * words + spare), 0) - start
    byte_hot = jnp.where((after >= 0) & (after < size), 1.0, 0.0).astype(BF16)
    value = jnp.dot(byte_hot, parts.astype(BF16), preferred_element_type=F32).astype(jnp.int32)
    index = iota((hyper, lanes), 0)
    offset = index - 30 * ((index * 2185) >> 16)
    bits_ref[...] = (((value >> (offset & 7)) & 1).astype(F32) + weight_lanes).astype(BF16)

    modes_map = map_ref[...]
    modes_map = jnp.concatenate(
        [modes_map.astype(F32), jnp.zeros((2, modes), F32)], axis=0
    ).astype(BF16)
    sums = jnp.zeros((48, wide), F32)
    for n in range(count):
        if n >= kept:
            copies[n - kept].wait()
        source = blocks_ref.at[n] if n < kept else others_ref.at[n - kept]
        part = slice(n * wide, (n + 1) * wide)
        local = [dot_t(modes_map, source[c]) for c in range(6)]
        trace = local[0] + local[1] + local[2]
        third = trace / 3.0
        shaped = [local[c] - third for c in range(3)] + [0.5 * local[c] for c in range(3, 6)]
        weight = weights[:, part]
        shaped = [weight * value for value in shaped]
        weighted_trace = weight * trace
        blocks, adds = [], []
        for i in range(6):
            entry = local[0][i : i + 1] * shaped[0]
            for c in range(1, 6):
                entry = entry + local[c][i : i + 1] * shaped[c]
            blocks.append(entry)
            adds.append(entry + trace[i : i + 1] * weighted_trace)
        sums = sums + jnp.concatenate(adds, axis=0)
        high, low = pieces(jnp.concatenate(blocks, axis=0), 2)
        table_ref[0:48, part] = high
        table_ref[48:96, part] = low
    const_ref[...] = jnp.broadcast_to(jnp.sum(sums, axis=1, keepdims=True), const_ref.shape)


def sides_of(first_ref, second_ref, axis, m, at=None):
    even = lax.rem(lax.axis_index(axis), 2) == 0
    rows = slice(None) if at is None else slice(at, at + 1)
    first, second = first_ref[m, rows, :], second_ref[m, rows, :]
    return jnp.where(even, second, first), jnp.where(even, first, second)


def micro_kernel(
    packed,
    hosts,
    capacity,
    flag_lanes,
    received_ref,
    x_face_ref,
    first_ref,
    second_ref,
    const_ref,
    bits_ref,
    table_ref,
    blocks_ref,
    basis_ref,
    answer_ref,
    *rest,
):
    del x_face_ref
    if packed:
        corners_ref = None
    else:
        corners_ref, *rest = rest
    (
        state_ref,
        hot_ref,
        others_ref,
        flags_ref,
        high_ref,
        low_ref,
        result_ref,
        sems,
    ) = rest
    groups = received_ref.shape[0]
    slots = groups * capacity
    kept, _, block, modes = blocks_ref.shape
    half = modes // 2
    count = kept + others_ref.shape[0]
    copies = []
    for n in range(count - kept):
        part = pl.ds((kept + n) * block, block)
        copies.append(
            pltpu.make_async_copy(basis_ref.at[:, part, :], others_ref.at[n], sems.at[n])
        )
        copies[n].start()

    ids = jnp.zeros((8, half), F32)
    for h in range(groups):
        own = pl.ds(h * capacity, capacity)
        state_ref[own, :half] = received_ref[h, :capacity, :]
        state_ref[own, half:] = received_ref[h, capacity : 2 * capacity, :]
        ids = ids + received_ref[h, 2 * capacity :, :].astype(F32)
    ids = jnp.concatenate([ids[0:1], ids[1:2]], axis=1).astype(jnp.int32)
    hot_ref[...] = jnp.where(iota(hot_ref.shape, 0) == ids, 1.0, 0.0).astype(BF16)

    def solve(*accumulators):
        mains = (accumulators[:8], accumulators[8:12])
        spares = accumulators[12:16]
        tangent_high, tangent_low = accumulators[16:]
        hyper = bits_ref.shape[0]
        empty = jnp.zeros((128, modes - bits_ref.shape[1]), BF16)
        blocks_of_flags = hyper // 128

        def flags_of(j):
            rows = jnp.concatenate([bits_ref[128 * j : 128 * j + 128, :], empty], axis=1)
            pltpu.matmul_acc_lhs(spares[j % 4], rows, load_staged_rhs=None if j else 0)

        def keep_flags(j):
            flags_ref[128 * j : 128 * j + 128, :] = pltpu.matmul_pop(spares[j % 4])

        def place(i):
            if i < 8:
                return mains[0][i]
            k = (i - 8) // 2
            return mains[0][k % 8] if i % 2 else mains[1][k % 4]

        strip = 16
        strips = hyper // strip

        def issue(i):
            n, r = divmod(i * strip, block)
            if n >= kept and r == 0:
                copies[n - kept].wait()
            source = blocks_ref.at[n] if n < kept else others_ref.at[n - kept]
            rows = jnp.concatenate([source[c, r : r + strip, :] for c in range(6)], axis=0)
            pltpu.matmul_acc_lhs(place(i), rows, load_staged_rhs=0 if i in (0, 8) else None)

        def respond(i, sums):
            strain = pltpu.matmul_pop(place(i))
            e = [strain[c * strip : (c + 1) * strip] for c in range(6)]
            at = slice(i * strip, (i + 1) * strip)
            volume = e[0] + e[1] + e[2]
            third = volume * (1.0 / 3.0)
            d = [e[c] - third for c in range(2)]
            normal = d[0] * (d[0] + d[1]) + d[1] * d[1]
            shear = e[3] * e[3] + e[4] * e[4] + e[5] * e[5]
            square = jnp.maximum(normal + 0.25 * shear, 0.5 * YIELD_STRESS * YIELD_STRESS)
            factor = FACTOR * lax.rsqrt(square) + (HARDENING - 1.0)
            change = flags_ref[at, :] * factor
            high = change.astype(BF16)
            high_ref[at, :] = high
            low_ref[at, :] = (change - high.astype(F32)).astype(BF16)
            packed_row = bits_ref[at, :].astype(F32)
            lane = iota(packed_row.shape, 1)
            packed_row = jnp.where((lane >= flag_lanes) & (lane < flag_lanes + 3), packed_row, 0.0)
            weight = jnp.sum(packed_row, axis=1, keepdims=True)
            scaled = weight + weight * change
            terms = [scaled * d[c] for c in range(2)] + [scaled * e[c] for c in range(3, 6)]
            terms.append(weight * volume)
            return [total + (term[:8] + term[8:]) for total, term in zip(sums, terms)]

        sums = [jnp.zeros((8, slots), F32)] * 6
        ahead = 6
        pltpu.matmul_push_rhs(hot_ref[...], 0, 1)
        pltpu.matmul_push_rhs(state_ref[...], 0, 0, transpose=True)
        for j in range(4):
            flags_of(j)
        for i in range(8):
            issue(i)
        for j in range(blocks_of_flags):
            keep_flags(j)
            if j + 4 < blocks_of_flags:
                flags_of(j + 4)
        pltpu.matmul_push_rhs(state_ref[...], 0, 1, transpose=True)
        for i in range(strips):
            if 8 <= i + ahead < strips:
                issue(i + ahead)
            sums = respond(i, sums)
        for n in range(hyper // modes):
            part = slice(n * modes, (n + 1) * modes)
            pltpu.matmul_push_rhs(high_ref[part, :], 0, 0)
            pltpu.matmul_push_rhs(low_ref[part, :], 0, 1)
            pltpu.matmul_acc_lhs(tangent_high, table_ref[:, part], load_staged_rhs=0)
            pltpu.matmul_acc_lhs(tangent_low, table_ref[0:48, part], load_staged_rhs=0)
        both_parts = pltpu.matmul_pop(tangent_high)
        tangent = both_parts[:48] + (both_parts[48:] + pltpu.matmul_pop(tangent_low))
        return tangent, sums

    tangent, sums = pl.run_scoped(
        solve,
        *[pltpu.ACC(0)((96, slots), F32) for _ in range(8)],
        *[pltpu.ACC(1)((96, slots), F32) for _ in range(4)],
        *[pltpu.ACC(1)((128, slots), F32) for _ in range(4)],
        pltpu.ACC(0)((96, slots), F32),
        pltpu.ACC(1)((48, slots), F32),
    )

    totals = [jnp.sum(value, axis=0, keepdims=True) for value in sums]
    normals = [totals[0], totals[1], -(totals[0] + totals[1])]
    for c in range(6):
        value = normals[c] + totals[5] if c < 3 else 0.5 * totals[c - 1]
        result_ref[c : c + 1, :] = value
    const = const_ref[...]
    const = jnp.concatenate([const] * (slots // const.shape[1]), axis=1)
    tangent = tangent + const
    at = 6
    for i in range(6):
        result_ref[at : at + 6 - i, :] = tangent[8 * i + i : 8 * i + 6]
        at += 6 - i
    result_ref[at:, :] = jnp.zeros((ROWS - at, slots), F32)

    last = first_ref.shape[1] - 1

    def corner_rows(write):
        for m in range(4):
            up = sides_of(first_ref, second_ref, "micro", m, last)
            down = sides_of(first_ref, second_ref, "micro", m, 0)
            for n in range(2):
                write(0, 2 * m + n, up[n])
                write(1, 2 * m + n, down[n])

    if packed:
        here = lax.axis_index("macro")
        group_of = iota((8, 128), 1) // capacity
        for h in range(hosts):
            chunk = jnp.zeros((8, 128), F32)
            tile, place = divmod(h * capacity, 128)
            for g in range(4):
                piece = result_ref[8 * g : 8 * g + 8, tile * 128 : (tile + 1) * 128]
                shift = (g * capacity - place) % 128
                if shift:
                    piece = pltpu.roll(piece, shift, 1)
                chunk = jnp.where(group_of == g, piece, chunk)
            answer_ref[h, 0:8, :] = chunk
        chunks = [jnp.minimum(here + 1, hosts - 1), jnp.maximum(here - 1, 0)]

        def write(side, row, value):
            answer_ref[chunks[side], 8 + row : 9 + row, :] = value
    else:
        answer_ref[...] = result_ref[...]

        def write(side, row, value):
            corners_ref[side, row : row + 1, :] = value

    corner_rows(write)


def assemble(stress):
    ready = []
    for here, low in stress:
        ready.append((here, low, previous_z(here), previous_z(low)))

    def at(c, sign_x, sign_y, sign_z):
        here, low, here_z, low_z = ready[c]
        if sign_z:
            near, far = here_z - here, low_z - low
        else:
            near, far = here_z + here, low_z + low
        both = far - near if sign_y else far + near
        return both[:-1] - both[1:] if sign_x else both[:-1] + both[1:]

    force = [
        at(0, 1, 0, 0) + at(5, 0, 1, 0) + at(4, 0, 0, 1),
        at(5, 1, 0, 0) + at(1, 0, 1, 0) + at(3, 0, 0, 1),
        at(4, 1, 0, 0) + at(3, 0, 1, 0) + at(2, 0, 0, 1),
    ]
    return [0.25 * value for value in force]


def elastic_kernel(
    hosts,
    capacity,
    motion_ref,
    stiff_ref,
    elem_ref,
    owner_ref,
    first_ref,
    second_ref,
    force_ref,
    edge_ref,
    index_ref,
    slot_hot_ref,
    depth_hot_ref,
    node_ref,
    wide_ref,
    stress_ref,
):
    size_x, size_y, size_z = motion_ref.shape[1:]
    node_ref[...] = jnp.zeros_like(node_ref)
    wide_ref[...] = jnp.zeros_like(wide_ref)
    stiffness = stiff_ref[...].astype(F32)
    elem, owner = elem_ref[...], owner_ref[...]
    points = elem.shape[1]
    column = elem // size_z
    depth = elem - column * size_z
    slot = slots_of(owner, hosts, capacity)[2]
    slot_hot = iota(slot_hot_ref.shape, 0) == slot
    slot_hot_ref[...] = jnp.where(slot_hot, 1.0, 0.0).astype(BF16)
    index_ref[...] = jnp.broadcast_to(column, index_ref.shape)
    depth_hot = jnp.where(iota((size_z, points), 0) == depth, 1.0, 0.0).astype(BF16)
    depth_hot_ref[...] = depth_hot
    column_hot = jnp.where(iota((size_x * size_y, points), 0) == column, 1.0, 0.0).astype(BF16)
    listed = dot_t(column_hot, depth_hot)
    for i in range(size_x):
        for m in range(3):
            low, high = sides_of(first_ref, second_ref, "micro", m, i)
            node_ref[m, i, 0:1, :] = low
            node_ref[m, i, 1 : size_y + 1, :] = motion_ref[m, i]
            node_ref[m, i, size_y + 1 : size_y + 2, :] = high
        low, _ = sides_of(first_ref, second_ref, "micro", 3, i)
        wide_ref[i, 0:1, :] = low
        keep = 1.0 - listed[i * size_y : (i + 1) * size_y]
        wide_ref[i, 1 : size_y + 1, :] = stiffness[i] * keep
    for m in range(3):
        edge_ref[m] = node_ref[m, 0]
        edge_ref[3 + m] = node_ref[m, size_x - 1]
    edge_ref[6] = wide_ref[size_x - 1]
    strain = block_strains([node_ref[m] for m in range(3)])
    stress = elastic_of(strain, wide_ref[: size_x - 1])
    for c in range(6):
        stress_ref[c, 0] = jnp.zeros(stress_ref.shape[2:], F32)
        stress_ref[c, 1:size_x] = stress[c]
        stress_ref[c, size_x] = jnp.zeros(stress_ref.shape[2:], F32)
    force = assemble(
        [(stress_ref[c, :, 1 : size_y + 1, :], stress_ref[c, :, 0:size_y, :]) for c in range(6)]
    )
    for m in range(3):
        force_ref[m] = force[m]


def final_kernel(packed, hosts, capacity, answer_ref, *rest):
    if packed:
        corners_ref = None
    else:
        corners_ref, *rest = rest
    (
        second_ref,
        first_ref,
        elastic_ref,
        edge_ref,
        index_ref,
        slot_hot_ref,
        depth_hot_ref,
        force_ref,
        tangent_ref,
        result_ref,
        node_ref,
        wide_ref,
        stress_ref,
    ) = rest
    size_x, size_y, size_z = elastic_ref.shape[1:]
    column = index_ref[0:1, :]
    points = column.shape[1]
    if packed:
        group_of = iota((8, 128), 1) // capacity
        per_tile = 128 // capacity
        groups = []
        for g in range(4):
            tiles = []
            for t in range(hosts // per_tile):
                tile = jnp.zeros((8, 128), F32)
                for n in range(per_tile):
                    piece = answer_ref[t * per_tile + n, 0:8, :]
                    shift = ((n - g) * capacity) % 128
                    if shift:
                        piece = pltpu.roll(piece, shift, 1)
                    tile = jnp.where(group_of == n, piece, tile)
                tiles.append(tile)
            groups.append(jnp.concatenate(tiles, axis=1))
        answer = jnp.concatenate(groups, axis=0)
    else:
        answer = answer_ref[...]
    parts = jnp.concatenate(pieces(answer, 3), axis=0)
    chosen = jnp.dot(parts, slot_hot_ref[...], preferred_element_type=F32)
    result = chosen[:ROWS] + (chosen[ROWS : 2 * ROWS] + chosen[2 * ROWS :])
    result_ref[...] = result
    for i in range(6):
        for j in range(6):
            at = 6 + UPPER.index((min(i, j), max(i, j)))
            tangent_ref[6 * i + j : 6 * i + j + 1, :] = result_ref[at : at + 1, :]

    here = lax.axis_index("macro")
    inner = [here > 0, here < hosts - 1]
    from_chunk = [jnp.maximum(here - 1, 0), jnp.minimum(here + 1, hosts - 1)]

    def corner(side, row):
        if packed:
            value = answer_ref[from_chunk[side], 8 + row : 9 + row, :]
        else:
            value = corners_ref[side, row : row + 1, :]
        return jnp.where(inner[side], value, 0.0)

    node_ref[...] = jnp.zeros_like(node_ref)
    wide_ref[...] = jnp.zeros_like(wide_ref)
    for m in range(3):
        faces = sides_of(first_ref, second_ref, "macro", m)
        for side, at in ((0, 0), (1, 3)):
            node_ref[m, at, 0:1, :] = corner(side, 2 * m)
            node_ref[m, at, 1 : size_y + 1, :] = faces[side]
            node_ref[m, at, size_y + 1 : size_y + 2, :] = corner(side, 2 * m + 1)
        node_ref[m, 1] = edge_ref[m]
        node_ref[m, 2] = edge_ref[3 + m]
    wide_ref[0, 0:1, :] = corner(0, 6)
    wide_ref[0, 1 : size_y + 1, :] = sides_of(first_ref, second_ref, "macro", 3)[0]
    wide_ref[1] = edge_ref[6]
    lower, upper = [], []
    for m in range(3):
        four = corners(node_ref[m])
        lower.append([jnp.stack([value[0], value[2]]) for value in four])
        upper.append([jnp.stack([value[1], value[3]]) for value in four])
    edge = elastic_of(strains(lower, upper), wide_ref[...])
    rows = (size_x - 1) * size_y
    column_hot = iota((rows, points), 0) == column
    stress_ref[:, 1:size_x, 0:1, :] = jnp.zeros((6, size_x - 1, 1, size_z), F32)
    placed = [jnp.where(column_hot, result[c : c + 1], 0.0) for c in range(6)]
    placed = jnp.concatenate(pieces(jnp.concatenate(placed, axis=0), 2), axis=0)
    fields = dot_t(placed, depth_hot_ref[...])
    for c in range(6):
        field = fields[c * rows : (c + 1) * rows] + fields[(6 + c) * rows : (7 + c) * rows]
        stress_ref[c, 1:size_x, 1 : size_y + 1, :] = field.reshape(size_x - 1, size_y, size_z)
        stress_ref[c, 0] = edge[c][0]
        stress_ref[c, size_x] = edge[c][1]
    force = assemble(
        [(stress_ref[c, :, 1 : size_y + 1, :], stress_ref[c, :, 0:size_y, :]) for c in range(6)]
    )
    for m in range(3):
        force_ref[m] = elastic_ref[m] + force[m]


def shape_of(shape, dtype=F32):
    return jax.ShapeDtypeStruct(shape, dtype)


def call(kernel, name, out_shape, args, scratch=(), flops=10**8, raw=0, raw_out=0):
    specs = whole(*args[: len(args) - raw]) + [pl.BlockSpec(memory_space=pl.ANY)] * raw
    return pl.pallas_call(
        kernel,
        grid=(1,),
        out_shape=out_shape,
        in_specs=specs,
        out_specs=[pl.BlockSpec(memory_space=pl.ANY)] * raw_out + whole(*out_shape[raw_out:]),
        scratch_shapes=scratch,
        compiler_params=pltpu.CompilerParams(vmem_limit_bytes=24 * 2**20),
        cost_estimate=pl.CostEstimate(flops=flops, bytes_accessed=2**20, transcendentals=0),
        name=name,
    )(*args)


def on_device(
    motion,
    stiffness,
    point_elem,
    point_owner,
    point_pattern,
    history,
    basis,
    mode_map,
    weights,
    patterns,
):
    size_x, size_y, size_z = motion.shape[1:]
    points = point_elem.shape[0]
    hosts = lax.axis_size("macro")
    capacity = 2 * points // hosts
    slots = capacity * hosts
    modes = mode_map.shape[0]
    half = modes // 2
    hyper = weights.shape[0]
    lanes = 128
    direct = capacity % 16 == 0
    packed = capacity * 4 == lanes and slots % lanes == 0
    motion = in_hbm(motion)
    stiffness = in_hbm(stiffness)
    elem = in_hbm(point_elem.reshape(1, points))
    owner = in_hbm(point_owner.reshape(1, points))
    pattern = in_hbm(point_pattern.reshape(1, points))
    history = in_hbm(history)
    map_rows = in_hbm(mode_map.T)

    rows = in_hbm(basis.reshape(6, hyper, modes))
    wide, kept = 256, 3
    sent = (
        [shape_of((hosts, 2 * capacity + 8, half), BF16)]
        if direct
        else [shape_of((slots, modes), BF16), shape_of((hosts, modes), BF16)]
    )
    swap, x_swap = shape_of((4, size_x, size_z)), shape_of((4, size_y, size_z))
    arguments = (owner, elem, motion, history, pattern, stiffness)
    small = (map_rows, in_hbm(weights.reshape(1, hyper)), in_hbm(patterns.T))
    *payload, first, second, x_first, x_second, blocks, map_here, weights, bit_words = call(
        functools.partial(dispatch_kernel, hosts, capacity, direct),
        "dispatch",
        sent
        + [swap, swap, x_swap, x_swap, shape_of((kept, 6, wide, modes), BF16)]
        + [shape_of(value.shape, value.dtype) for value in small],
        (*arguments, *small, rows),
        [VMEM(value.shape, value.dtype) for value in (*arguments, sent[0])]
        + [pltpu.SemaphoreType.DMA((10 + kept,))],
        raw=10,
        raw_out=1,
    )

    if direct:
        received = lax.all_to_all(payload[0], "macro", 0, 0, tiled=True)
        groups, group = hosts, capacity
    else:
        slot_rows, ids = payload
        joined = jnp.concatenate(
            [
                slot_rows[:, :half].reshape(hosts, capacity, half),
                slot_rows[:, half:].reshape(hosts, capacity, half),
                ids.reshape(hosts, 2, half),
            ],
            axis=1,
        )
        joined = lax.all_to_all(joined, "macro", 0, 0, tiled=True)
        ids = jnp.sum(joined[:, 2 * capacity :].astype(F32), axis=0).astype(BF16)
        received = jnp.concatenate(
            [
                joined[:, :capacity].reshape(1, slots, half),
                joined[:, capacity : 2 * capacity].reshape(1, slots, half),
                jnp.pad(ids, ((0, 6), (0, 0)))[None],
            ],
            axis=1,
        )
        groups, group = 1, slots

    def swapped(value, axis, start):
        pairs = [(i, i + 1) for i in range(start, lax.axis_size(axis) - 1, 2)]
        return lax.ppermute(value, axis, pairs + [(b, a) for a, b in pairs])

    first, second = swapped(first, "micro", 0), swapped(second, "micro", 1)
    x_first, x_second = swapped(x_first, "macro", 0), swapped(x_second, "macro", 1)

    table, const, bits = call(
        table_kernel,
        "tables",
        [
            shape_of((96, hyper), BF16),
            shape_of((48, lanes)),
            shape_of((hyper, lanes), BF16),
        ],
        (blocks, map_here, weights, bit_words, rows),
        [
            VMEM((hyper // wide - kept, 6, wide, modes), BF16),
            pltpu.SemaphoreType.DMA((hyper // wide - kept,)),
        ],
        raw=1,
    )

    answer = call(
        functools.partial(micro_kernel, packed, hosts, group, patterns.shape[0]),
        "micro_response",
        [shape_of((hosts, 16, lanes))]
        if packed
        else [shape_of((ROWS, slots)), shape_of((2, 8, lanes))],
        (
            received,
            x_first,
            first,
            second,
            const,
            bits,
            table,
            blocks,
            rows,
        ),
        [
            VMEM((slots, modes), BF16),
            VMEM((modes, slots), BF16),
            VMEM((hyper // wide - kept, 6, wide, modes), BF16),
            VMEM((hyper, slots), F32),
            *[VMEM((hyper, slots), BF16)] * 2,
            VMEM((ROWS, slots), F32),
            pltpu.SemaphoreType.DMA((hyper // wide - kept,)),
        ],
        raw=1,
    )

    if packed:
        answered = [lax.all_to_all(answer[0], "macro", 0, 0, tiled=True)]
    else:
        result, edges = answer
        here = lax.axis_index("macro")
        order = jnp.arange(hosts)[:, None, None]
        flat = result.reshape(ROWS, hosts, capacity).transpose(1, 0, 2).reshape(hosts, -1)
        tiles = pl.cdiv(flat.shape[1], lanes)
        flat = jnp.pad(flat, ((0, 0), (0, tiles * lanes - flat.shape[1])))
        joined = jnp.concatenate(
            [flat.reshape(hosts, tiles, lanes), jnp.where(order > here, edges[0], edges[1])], axis=1
        )
        joined = lax.all_to_all(joined, "macro", 0, 0, tiled=True)
        flat = joined[:, :tiles].reshape(hosts, -1)[:, : ROWS * capacity]
        result = flat.reshape(hosts, ROWS, capacity).transpose(1, 0, 2).reshape(ROWS, slots)
        low = lax.dynamic_index_in_dim(joined, jnp.maximum(here - 1, 0), 0, False)
        high = lax.dynamic_index_in_dim(joined, jnp.minimum(here + 1, hosts - 1), 0, False)
        answered = [result, jnp.stack([low[tiles:], high[tiles:]])]

    elastic = call(
        functools.partial(elastic_kernel, hosts, capacity),
        "elastic_forces",
        [
            shape_of(motion.shape),
            shape_of((7, 16, size_z)),
            shape_of((8, points), jnp.int32),
            shape_of((slots, points), BF16),
            shape_of((size_z, points), BF16),
        ],
        (motion, stiffness, elem, owner, first, second),
        [
            VMEM((3, size_x, 16, size_z), F32),
            VMEM((size_x, 16, size_z), F32),
            VMEM((6, size_x + 1, 16, size_z), F32),
        ],
    )

    force, tangent = call(
        functools.partial(final_kernel, packed, hosts, capacity),
        "final_forces",
        [shape_of(motion.shape), shape_of((36, points))],
        (*answered, x_second, x_first, *elastic),
        [
            VMEM((ROWS, points), F32),
            VMEM((3, 4, 16, size_z), F32),
            VMEM((2, 16, size_z), F32),
            VMEM((6, size_x + 1, 16, size_z), F32),
        ],
    )
    return (force, tangent)


def solution(mesh):
    return jax.shard_map(
        on_device,
        mesh=mesh,
        in_specs=(
            P(None, "macro", "micro", None),
            P("macro", "micro", None),
            P(("macro", "micro")),
            P(("macro", "micro")),
            P(("macro", "micro")),
            P(None, ("macro", "micro")),
            P("macro", None, None),
            P(),
            P(),
            P(),
        ),
        out_specs=(P(None, "macro", "micro", None), P(None, ("macro", "micro"))),
        check_vma=False,
    )
```

```python
import functools

import jax
import jax.numpy as jnp
from jax import lax
from jax.experimental import pallas as pl
from jax.experimental.pallas import tpu as pltpu
from jax.sharding import PartitionSpec as P

YIELD_STRESS = 1.5
HARDENING = 0.2
FACTOR = YIELD_STRESS * (1.0 - HARDENING) * 0.5**0.5
F32 = jnp.float32
BF16 = jnp.bfloat16
VMEM = pltpu.VMEM
ROWS = 32
UPPER = [(i, j) for i in range(6) for j in range(i, 6)]


def whole(*arrays):
    return [pl.BlockSpec(value.shape, lambda s, n=len(value.shape): (0,) * n) for value in arrays]


def in_hbm(value):
    return pltpu.with_memory_space_constraint(value, pltpu.HBM)


def iota(shape, dim):
    return lax.broadcasted_iota(jnp.int32, shape, dim)


def dot_t(left, right):
    return lax.dot_general(left, right, (((1,), (1,)), ((), ())), preferred_element_type=F32)


def pieces(value, count):
    out = []
    for _ in range(count):
        piece = value.astype(BF16)
        out.append(piece)
        value = value - piece.astype(F32)
    return out


def next_z(field):
    last = field.ndim - 1
    size = field.shape[last]
    rolled = pltpu.roll(field, size - 1, last)
    return jnp.where(iota(field.shape, last) == size - 1, 0.0, rolled)


def previous_z(field):
    last = field.ndim - 1
    rolled = pltpu.roll(field, 1, last)
    return jnp.where(iota(field.shape, last) == 0, 0.0, rolled)


def corners(field):
    y_up = pltpu.roll(field, field.shape[1] - 1, 1)
    return [field, y_up, next_z(field), next_z(y_up)]


def strains(lower, upper):
    grads = []
    for low, high in zip(lower, upper):
        dx = [b - a for a, b in zip(low, high)]
        grad_x = (dx[0] + dx[1] + dx[2] + dx[3]) * 0.25
        dy = [value[1] - value[0] for value in (low, high)]
        dy_z = [value[3] - value[2] for value in (low, high)]
        grad_y = (dy[0] + dy[1] + dy_z[0] + dy_z[1]) * 0.25
        dz = [value[2] - value[0] for value in (low, high)]
        dz_y = [value[3] - value[1] for value in (low, high)]
        grad_z = (dz[0] + dz[1] + dz_y[0] + dz_y[1]) * 0.25
        grads.append((grad_x, grad_y, grad_z))
    return [
        grads[0][0],
        grads[1][1],
        grads[2][2],
        grads[1][2] + grads[2][1],
        grads[0][2] + grads[2][0],
        grads[0][1] + grads[1][0],
    ]


def block_strains(fields):
    nodes = [corners(field) for field in fields]
    return strains(
        [[value[:-1] for value in four] for four in nodes],
        [[value[1:] for value in four] for four in nodes],
    )


def elastic_of(strain, stiffness):
    volume = strain[0] + strain[1] + strain[2]
    rest = volume - volume * (1.0 / 3.0)
    normal = [stiffness * (rest + strain[c]) for c in range(3)]
    return normal + [stiffness * (0.5 * strain[c]) for c in range(3, 6)]


def slots_of(owner, hosts, capacity):
    points = owner.shape[1]
    chosen = iota((hosts, points), 0) == owner
    host_hot = jnp.where(chosen, 1.0, 0.0)
    before = jnp.where(iota((points, points), 0) < iota((points, points), 1), 1.0, 0.0)
    counts = jnp.dot(host_hot.astype(BF16), before.astype(BF16), preferred_element_type=F32)
    position = jnp.sum(host_hot * counts, axis=0, keepdims=True).astype(jnp.int32)
    return host_hot, position, owner * capacity + position


def dispatch_kernel(hosts, capacity, direct, *refs):
    inputs, basis_ref, payload_out, refs = refs[:9], refs[9], refs[10], list(refs[11:])
    ids_ref = None if direct else refs.pop(0)
    first_ref, second_ref, x_first_ref, x_second_ref, blocks_ref = refs[:5]
    buffers, payload_ref, sems = refs[8:13] + [refs[5], refs[13]] + refs[6:8], refs[14], refs[15]
    arrivals = [
        pltpu.make_async_copy(value, buffer, sems.at[n])
        for n, (value, buffer) in enumerate(zip(inputs, buffers))
    ]
    for copy in arrivals:
        copy.start()
    kept, _, wide, _ = blocks_ref.shape
    later = [
        pltpu.make_async_copy(
            basis_ref.at[:, pl.ds(n * wide, wide), :], blocks_ref.at[n], sems.at[10 + n]
        )
        for n in range(kept)
    ]
    for copy in later:
        copy.start()
    motion_ref, elem_ref, owner_ref, history_ref, pattern_ref, map_ref, stiff_ref, _, _ = buffers
    size_x, size_y, size_z = motion_ref.shape[1:]
    for copy in arrivals[:6]:
        copy.wait()
    owner = owner_ref[...]
    points = owner.shape[1]
    host_hot, position, slot = slots_of(owner, hosts, capacity)
    slot_total = hosts * capacity
    slot_hot = jnp.where(iota((slot_total, points), 0) == slot, 1.0, 0.0).astype(BF16)
    elem = elem_ref[...]
    column = elem // size_z
    depth = elem - column * size_z
    depth_hot = jnp.where(iota((size_z, points), 0) == depth, 1.0, 0.0).astype(BF16)
    rows = (size_x - 1) * size_y
    column_hot = iota((rows, points), 0) == column
    strain = block_strains([motion_ref[m] for m in range(3)])
    field = jnp.concatenate([value.reshape(rows, size_z) for value in strain], axis=0)
    picked = jnp.dot(field.astype(BF16), depth_hot, preferred_element_type=F32)
    macro_strain = jnp.concatenate(
        [
            jnp.sum(
                jnp.where(column_hot, picked[c * rows : (c + 1) * rows], 0.0),
                axis=0,
                keepdims=True,
            )
            for c in range(6)
        ],
        axis=0,
    ).astype(BF16)
    held = dot_t(slot_hot, history_ref[...])
    slot_strain = dot_t(slot_hot, macro_strain).astype(BF16)
    mapped = jnp.dot(slot_strain, map_ref[...], preferred_element_type=F32)
    sent = (mapped + held).astype(BF16)
    place = position + lax.axis_index("macro") * capacity
    modes = sent.shape[1]
    half = modes // 2
    place_hot = jnp.where(iota((modes, points), 0) == place, 1.0, 0.0).astype(BF16)
    ids = dot_t((host_hot * pattern_ref[...].astype(F32)).astype(BF16), place_hot)
    if direct:
        for h in range(hosts):
            mine = sent[h * capacity : (h + 1) * capacity]
            payload_ref[h, :capacity, :] = mine[:, :half]
            payload_ref[h, capacity : 2 * capacity, :] = mine[:, half:]
            row = iota((8, half), 0)
            low, high = ids[h : h + 1, :half], ids[h : h + 1, half:]
            tile = jnp.where(row == 0, low, jnp.where(row == 1, high, 0.0))
            payload_ref[h, 2 * capacity :, :] = tile.astype(BF16)
    else:
        payload_ref[...] = sent
        ids_ref[...] = ids.astype(BF16)
    leave = pltpu.make_async_copy(payload_ref, payload_out, sems.at[9])
    leave.start()
    for copy in arrivals[6:]:
        copy.wait()
    stiffness = stiff_ref[...].astype(F32)
    even = lax.rem(lax.axis_index("micro"), 2) == 0
    for i in range(size_x):
        for m in range(4):
            if m < 3:
                up, down = motion_ref[m, i, size_y - 1 : size_y, :], motion_ref[m, i, 0:1, :]
            else:
                up = down = stiffness[i, size_y - 1 : size_y, :]
            first_ref[m, i : i + 1, :] = jnp.where(even, up, down)
            second_ref[m, i : i + 1, :] = jnp.where(even, down, up)
    even = lax.rem(lax.axis_index("macro"), 2) == 0
    for m in range(4):
        if m < 3:
            up, down = motion_ref[m, size_x - 1], motion_ref[m, 0]
        else:
            up = down = stiffness[size_x - 1]
        x_first_ref[m] = jnp.where(even, up, down)
        x_second_ref[m] = jnp.where(even, down, up)
    leave.wait()
    for copy in later:
        copy.wait()


def table_kernel(
    blocks_ref,
    map_ref,
    weights_ref,
    patterns_ref,
    basis_ref,
    table_ref,
    const_ref,
    bits_ref,
    others_ref,
    sems,
):
    hyper = weights_ref.shape[1]
    lanes = 128
    kept, _, wide, modes = blocks_ref.shape
    count = hyper // wide
    copies = []
    for n in range(kept, count):
        copy = pltpu.make_async_copy(
            basis_ref.at[:, pl.ds(n * wide, wide), :], others_ref.at[n - kept], sems.at[n - kept]
        )
        copy.start()
        copies.append(copy)
    weights = weights_ref[...]
    split = [piece.astype(F32) for piece in pieces(weights, 3)]
    row = iota((8, hyper), 0)
    stack = jnp.where(
        row == 0, split[0], jnp.where(row == 1, split[1], jnp.where(row == 2, split[2], 0.0))
    )
    choice = jnp.where(iota((8, lanes), 1) == iota((8, lanes), 0) + patterns_ref.shape[1], 1.0, 0.0)
    weight_lanes = lax.dot_general(
        stack.astype(BF16),
        choice.astype(BF16),
        (((0,), (0,)), ((), ())),
        preferred_element_type=F32,
    )
    patterns = patterns_ref[...]
    words, total = patterns.shape
    parts = [((patterns >> (8 * k)) & 255).astype(F32) for k in range(4)]
    spare = -4 * words % 8
    parts = jnp.concatenate(parts + [jnp.zeros((spare, total), F32)] * (spare > 0), axis=0)
    parts = jnp.concatenate([parts, jnp.zeros((parts.shape[0], lanes - total), F32)], axis=1)
    place = iota((1, 4 * words + spare), 1)
    part = jnp.where(place >= words, 1, 0) + jnp.where(place >= 2 * words, 1, 0)
    part = part + jnp.where(place >= 3 * words, 1, 0)
    start = 30 * (place - words * part) + 8 * part
    size = jnp.where(part == 3, 6, 8)
    after = iota((hyper, 4 * words + spare), 0) - start
    byte_hot = jnp.where((after >= 0) & (after < size), 1.0, 0.0).astype(BF16)
    value = jnp.dot(byte_hot, parts.astype(BF16), preferred_element_type=F32).astype(jnp.int32)
    index = iota((hyper, lanes), 0)
    offset = index - 30 * ((index * 2185) >> 16)
    bits_ref[...] = (((value >> (offset & 7)) & 1).astype(F32) + weight_lanes).astype(BF16)

    modes_map = map_ref[...]
    modes_map = jnp.concatenate(
        [modes_map.astype(F32), jnp.zeros((2, modes), F32)], axis=0
    ).astype(BF16)
    sums = jnp.zeros((48, wide), F32)
    for n in range(count):
        if n >= kept:
            copies[n - kept].wait()
        source = blocks_ref.at[n] if n < kept else others_ref.at[n - kept]
        part = slice(n * wide, (n + 1) * wide)
        local = [dot_t(modes_map, source[c]) for c in range(6)]
        trace = local[0] + local[1] + local[2]
        third = trace / 3.0
        shaped = [local[c] - third for c in range(3)] + [0.5 * local[c] for c in range(3, 6)]
        weight = weights[:, part]
        shaped = [weight * value for value in shaped]
        weighted_trace = weight * trace
        blocks, adds = [], []
        for i in range(6):
            entry = local[0][i : i + 1] * shaped[0]
            for c in range(1, 6):
                entry = entry + local[c][i : i + 1] * shaped[c]
            blocks.append(entry)
            adds.append(entry + trace[i : i + 1] * weighted_trace)
        sums = sums + jnp.concatenate(adds, axis=0)
        high, low = pieces(jnp.concatenate(blocks, axis=0), 2)
        table_ref[0:48, part] = high
        table_ref[48:96, part] = low
    const_ref[...] = jnp.broadcast_to(jnp.sum(sums, axis=1, keepdims=True), const_ref.shape)


def sides_of(first_ref, second_ref, axis, m, at=None):
    even = lax.rem(lax.axis_index(axis), 2) == 0
    rows = slice(None) if at is None else slice(at, at + 1)
    first, second = first_ref[m, rows, :], second_ref[m, rows, :]
    return jnp.where(even, second, first), jnp.where(even, first, second)


def micro_kernel(
    packed,
    hosts,
    capacity,
    flag_lanes,
    received_ref,
    x_face_ref,
    first_ref,
    second_ref,
    const_ref,
    bits_ref,
    table_ref,
    blocks_ref,
    basis_ref,
    answer_ref,
    *rest,
):
    del x_face_ref
    if packed:
        corners_ref = None
    else:
        corners_ref, *rest = rest
    (
        state_ref,
        hot_ref,
        others_ref,
        flags_ref,
        high_ref,
        low_ref,
        result_ref,
        sems,
    ) = rest
    groups = received_ref.shape[0]
    slots = groups * capacity
    kept, _, block, modes = blocks_ref.shape
    half = modes // 2
    count = kept + others_ref.shape[0]
    copies = []
    for n in range(count - kept):
        part = pl.ds((kept + n) * block, block)
        copies.append(
            pltpu.make_async_copy(basis_ref.at[:, part, :], others_ref.at[n], sems.at[n])
        )
        copies[n].start()

    ids = jnp.zeros((8, half), F32)
    for h in range(groups):
        own = pl.ds(h * capacity, capacity)
        state_ref[own, :half] = received_ref[h, :capacity, :]
        state_ref[own, half:] = received_ref[h, capacity : 2 * capacity, :]
        ids = ids + received_ref[h, 2 * capacity :, :].astype(F32)
    ids = jnp.concatenate([ids[0:1], ids[1:2]], axis=1).astype(jnp.int32)
    hot_ref[...] = jnp.where(iota(hot_ref.shape, 0) == ids, 1.0, 0.0).astype(BF16)

    def solve(*accumulators):
        mains = (accumulators[:8], accumulators[8:12])
        spares = accumulators[12:16]
        tangent_high, tangent_low = accumulators[16:]
        hyper = bits_ref.shape[0]
        empty = jnp.zeros((128, modes - bits_ref.shape[1]), BF16)
        blocks_of_flags = hyper // 128

        def flags_of(j):
            rows = jnp.concatenate([bits_ref[128 * j : 128 * j + 128, :], empty], axis=1)
            pltpu.matmul_acc_lhs(spares[j % 4], rows, load_staged_rhs=None if j else 0)

        def keep_flags(j):
            flags_ref[128 * j : 128 * j + 128, :] = pltpu.matmul_pop(spares[j % 4])

        def place(i):
            if i < 8:
                return mains[0][i]
            k = (i - 8) // 2
            return mains[0][k % 8] if i % 2 else mains[1][k % 4]

        strip = 16
        strips = hyper // strip

        def issue(i):
            n, r = divmod(i * strip, block)
            if n >= kept and r == 0:
                copies[n - kept].wait()
            source = blocks_ref.at[n] if n < kept else others_ref.at[n - kept]
            rows = jnp.concatenate([source[c, r : r + strip, :] for c in range(6)], axis=0)
            pltpu.matmul_acc_lhs(place(i), rows, load_staged_rhs=0 if i in (0, 8) else None)

        def respond(i, sums):
            strain = pltpu.matmul_pop(place(i))
            e = [strain[c * strip : (c + 1) * strip] for c in range(6)]
            at = slice(i * strip, (i + 1) * strip)
            volume = e[0] + e[1] + e[2]
            third = volume * (1.0 / 3.0)
            d = [e[c] - third for c in range(2)]
            normal = d[0] * (d[0] + d[1]) + d[1] * d[1]
            shear = e[3] * e[3] + e[4] * e[4] + e[5] * e[5]
            square = jnp.maximum(normal + 0.25 * shear, 0.5 * YIELD_STRESS * YIELD_STRESS)
            factor = FACTOR * lax.rsqrt(square) + (HARDENING - 1.0)
            change = flags_ref[at, :] * factor
            high = change.astype(BF16)
            high_ref[at, :] = high
            low_ref[at, :] = (change - high.astype(F32)).astype(BF16)
            packed_row = bits_ref[at, :].astype(F32)
            lane = iota(packed_row.shape, 1)
            packed_row = jnp.where((lane >= flag_lanes) & (lane < flag_lanes + 3), packed_row, 0.0)
            weight = jnp.sum(packed_row, axis=1, keepdims=True)
            scaled = weight + weight * change
            terms = [scaled * d[c] for c in range(2)] + [scaled * e[c] for c in range(3, 6)]
            terms.append(weight * volume)
            return [total + (term[:8] + term[8:]) for total, term in zip(sums, terms)]

        sums = [jnp.zeros((8, slots), F32)] * 6
        ahead = 6
        pltpu.matmul_push_rhs(hot_ref[...], 0, 1)
        pltpu.matmul_push_rhs(state_ref[...], 0, 0, transpose=True)
        for j in range(4):
            flags_of(j)
        for i in range(8):
            issue(i)
        for j in range(blocks_of_flags):
            keep_flags(j)
            if j + 4 < blocks_of_flags:
                flags_of(j + 4)
        pltpu.matmul_push_rhs(state_ref[...], 0, 1, transpose=True)
        for i in range(strips):
            if 8 <= i + ahead < strips:
                issue(i + ahead)
            sums = respond(i, sums)
        for n in range(hyper // modes):
            part = slice(n * modes, (n + 1) * modes)
            pltpu.matmul_push_rhs(high_ref[part, :], 0, 0)
            pltpu.matmul_push_rhs(low_ref[part, :], 0, 1)
            pltpu.matmul_acc_lhs(tangent_high, table_ref[:, part], load_staged_rhs=0)
            pltpu.matmul_acc_lhs(tangent_low, table_ref[0:48, part], load_staged_rhs=0)
        both_parts = pltpu.matmul_pop(tangent_high)
        tangent = both_parts[:48] + (both_parts[48:] + pltpu.matmul_pop(tangent_low))
        return tangent, sums

    tangent, sums = pl.run_scoped(
        solve,
        *[pltpu.ACC(0)((96, slots), F32) for _ in range(8)],
        *[pltpu.ACC(1)((96, slots), F32) for _ in range(4)],
        *[pltpu.ACC(1)((128, slots), F32) for _ in range(4)],
        pltpu.ACC(0)((96, slots), F32),
        pltpu.ACC(1)((48, slots), F32),
    )

    totals = [jnp.sum(value, axis=0, keepdims=True) for value in sums]
    normals = [totals[0], totals[1], -(totals[0] + totals[1])]
    for c in range(6):
        value = normals[c] + totals[5] if c < 3 else 0.5 * totals[c - 1]
        result_ref[c : c + 1, :] = value
    const = const_ref[...]
    const = jnp.concatenate([const] * (slots // const.shape[1]), axis=1)
    tangent = tangent + const
    at = 6
    for i in range(6):
        result_ref[at : at + 6 - i, :] = tangent[8 * i + i : 8 * i + 6]
        at += 6 - i
    result_ref[at:, :] = jnp.zeros((ROWS - at, slots), F32)

    last = first_ref.shape[1] - 1

    def corner_rows(write):
        for m in range(4):
            up = sides_of(first_ref, second_ref, "micro", m, last)
            down = sides_of(first_ref, second_ref, "micro", m, 0)
            for n in range(2):
                write(0, 2 * m + n, up[n])
                write(1, 2 * m + n, down[n])

    if packed:
        here = lax.axis_index("macro")
        group_of = iota((8, 128), 1) // capacity
        for h in range(hosts):
            chunk = jnp.zeros((8, 128), F32)
            tile, place = divmod(h * capacity, 128)
            for g in range(4):
                piece = result_ref[8 * g : 8 * g + 8, tile * 128 : (tile + 1) * 128]
                shift = (g * capacity - place) % 128
                if shift:
                    piece = pltpu.roll(piece, shift, 1)
                chunk = jnp.where(group_of == g, piece, chunk)
            answer_ref[h, 0:8, :] = chunk
        chunks = [jnp.minimum(here + 1, hosts - 1), jnp.maximum(here - 1, 0)]

        def write(side, row, value):
            answer_ref[chunks[side], 8 + row : 9 + row, :] = value
    else:
        answer_ref[...] = result_ref[...]

        def write(side, row, value):
            corners_ref[side, row : row + 1, :] = value

    corner_rows(write)


def assemble(stress):
    ready = []
    for here, low in stress:
        ready.append((here, low, previous_z(here), previous_z(low)))

    def at(c, sign_x, sign_y, sign_z):
        here, low, here_z, low_z = ready[c]
        if sign_z:
            near, far = here_z - here, low_z - low
        else:
            near, far = here_z + here, low_z + low
        both = far - near if sign_y else far + near
        return both[:-1] - both[1:] if sign_x else both[:-1] + both[1:]

    force = [
        at(0, 1, 0, 0) + at(5, 0, 1, 0) + at(4, 0, 0, 1),
        at(5, 1, 0, 0) + at(1, 0, 1, 0) + at(3, 0, 0, 1),
        at(4, 1, 0, 0) + at(3, 0, 1, 0) + at(2, 0, 0, 1),
    ]
    return [0.25 * value for value in force]


def elastic_kernel(
    hosts,
    capacity,
    motion_ref,
    stiff_ref,
    elem_ref,
    owner_ref,
    first_ref,
    second_ref,
    force_ref,
    edge_ref,
    index_ref,
    slot_hot_ref,
    depth_hot_ref,
    node_ref,
    wide_ref,
    stress_ref,
):
    size_x, size_y, size_z = motion_ref.shape[1:]
    node_ref[...] = jnp.zeros_like(node_ref)
    wide_ref[...] = jnp.zeros_like(wide_ref)
    stiffness = stiff_ref[...].astype(F32)
    elem, owner = elem_ref[...], owner_ref[...]
    points = elem.shape[1]
    column = elem // size_z
    depth = elem - column * size_z
    slot = slots_of(owner, hosts, capacity)[2]
    slot_hot = iota(slot_hot_ref.shape, 0) == slot
    slot_hot_ref[...] = jnp.where(slot_hot, 1.0, 0.0).astype(BF16)
    index_ref[...] = jnp.broadcast_to(column, index_ref.shape)
    depth_hot = jnp.where(iota((size_z, points), 0) == depth, 1.0, 0.0).astype(BF16)
    depth_hot_ref[...] = depth_hot
    column_hot = jnp.where(iota((size_x * size_y, points), 0) == column, 1.0, 0.0).astype(BF16)
    listed = dot_t(column_hot, depth_hot)
    for i in range(size_x):
        for m in range(3):
            low, high = sides_of(first_ref, second_ref, "micro", m, i)
            node_ref[m, i, 0:1, :] = low
            node_ref[m, i, 1 : size_y + 1, :] = motion_ref[m, i]
            node_ref[m, i, size_y + 1 : size_y + 2, :] = high
        low, _ = sides_of(first_ref, second_ref, "micro", 3, i)
        wide_ref[i, 0:1, :] = low
        keep = 1.0 - listed[i * size_y : (i + 1) * size_y]
        wide_ref[i, 1 : size_y + 1, :] = stiffness[i] * keep
    for m in range(3):
        edge_ref[m] = node_ref[m, 0]
        edge_ref[3 + m] = node_ref[m, size_x - 1]
    edge_ref[6] = wide_ref[size_x - 1]
    strain = block_strains([node_ref[m] for m in range(3)])
    stress = elastic_of(strain, wide_ref[: size_x - 1])
    for c in range(6):
        stress_ref[c, 0] = jnp.zeros(stress_ref.shape[2:], F32)
        stress_ref[c, 1:size_x] = stress[c]
        stress_ref[c, size_x] = jnp.zeros(stress_ref.shape[2:], F32)
    force = assemble(
        [(stress_ref[c, :, 1 : size_y + 1, :], stress_ref[c, :, 0:size_y, :]) for c in range(6)]
    )
    for m in range(3):
        force_ref[m] = force[m]


def final_kernel(packed, hosts, capacity, answer_ref, *rest):
    if packed:
        corners_ref = None
    else:
        corners_ref, *rest = rest
    (
        second_ref,
        first_ref,
        elastic_ref,
        edge_ref,
        index_ref,
        slot_hot_ref,
        depth_hot_ref,
        force_ref,
        tangent_ref,
        result_ref,
        node_ref,
        wide_ref,
        stress_ref,
    ) = rest
    size_x, size_y, size_z = elastic_ref.shape[1:]
    column = index_ref[0:1, :]
    points = column.shape[1]
    if packed:
        group_of = iota((8, 128), 1) // capacity
        per_tile = 128 // capacity
        groups = []
        for g in range(4):
            tiles = []
            for t in range(hosts // per_tile):
                tile = jnp.zeros((8, 128), F32)
                for n in range(per_tile):
                    piece = answer_ref[t * per_tile + n, 0:8, :]
                    shift = ((n - g) * capacity) % 128
                    if shift:
                        piece = pltpu.roll(piece, shift, 1)
                    tile = jnp.where(group_of == n, piece, tile)
                tiles.append(tile)
            groups.append(jnp.concatenate(tiles, axis=1))
        answer = jnp.concatenate(groups, axis=0)
    else:
        answer = answer_ref[...]
    parts = jnp.concatenate(pieces(answer, 3), axis=0)
    chosen = jnp.dot(parts, slot_hot_ref[...], preferred_element_type=F32)
    result = chosen[:ROWS] + (chosen[ROWS : 2 * ROWS] + chosen[2 * ROWS :])
    result_ref[...] = result
    for i in range(6):
        for j in range(6):
            at = 6 + UPPER.index((min(i, j), max(i, j)))
            tangent_ref[6 * i + j : 6 * i + j + 1, :] = result_ref[at : at + 1, :]

    here = lax.axis_index("macro")
    inner = [here > 0, here < hosts - 1]
    from_chunk = [jnp.maximum(here - 1, 0), jnp.minimum(here + 1, hosts - 1)]

    def corner(side, row):
        if packed:
            value = answer_ref[from_chunk[side], 8 + row : 9 + row, :]
        else:
            value = corners_ref[side, row : row + 1, :]
        return jnp.where(inner[side], value, 0.0)

    node_ref[...] = jnp.zeros_like(node_ref)
    wide_ref[...] = jnp.zeros_like(wide_ref)
    for m in range(3):
        faces = sides_of(first_ref, second_ref, "macro", m)
        for side, at in ((0, 0), (1, 3)):
            node_ref[m, at, 0:1, :] = corner(side, 2 * m)
            node_ref[m, at, 1 : size_y + 1, :] = faces[side]
            node_ref[m, at, size_y + 1 : size_y + 2, :] = corner(side, 2 * m + 1)
        node_ref[m, 1] = edge_ref[m]
        node_ref[m, 2] = edge_ref[3 + m]
    wide_ref[0, 0:1, :] = corner(0, 6)
    wide_ref[0, 1 : size_y + 1, :] = sides_of(first_ref, second_ref, "macro", 3)[0]
    wide_ref[1] = edge_ref[6]
    lower, upper = [], []
    for m in range(3):
        four = corners(node_ref[m])
        lower.append([jnp.stack([value[0], value[2]]) for value in four])
        upper.append([jnp.stack([value[1], value[3]]) for value in four])
    edge = elastic_of(strains(lower, upper), wide_ref[...])
    rows = (size_x - 1) * size_y
    column_hot = iota((rows, points), 0) == column
    stress_ref[:, 1:size_x, 0:1, :] = jnp.zeros((6, size_x - 1, 1, size_z), F32)
    placed = [jnp.where(column_hot, result[c : c + 1], 0.0) for c in range(6)]
    placed = jnp.concatenate(pieces(jnp.concatenate(placed, axis=0), 2), axis=0)
    fields = dot_t(placed, depth_hot_ref[...])
    for c in range(6):
        field = fields[c * rows : (c + 1) * rows] + fields[(6 + c) * rows : (7 + c) * rows]
        stress_ref[c, 1:size_x, 1 : size_y + 1, :] = field.reshape(size_x - 1, size_y, size_z)
        stress_ref[c, 0] = edge[c][0]
        stress_ref[c, size_x] = edge[c][1]
    force = assemble(
        [(stress_ref[c, :, 1 : size_y + 1, :], stress_ref[c, :, 0:size_y, :]) for c in range(6)]
    )
    for m in range(3):
        force_ref[m] = elastic_ref[m] + force[m]


def shape_of(shape, dtype=F32):
    return jax.ShapeDtypeStruct(shape, dtype)


def call(kernel, name, out_shape, args, scratch=(), flops=10**8, raw=0, raw_out=0):
    specs = whole(*args[: len(args) - raw]) + [pl.BlockSpec(memory_space=pl.ANY)] * raw
    return pl.pallas_call(
        kernel,
        grid=(1,),
        out_shape=out_shape,
        in_specs=specs,
        out_specs=[pl.BlockSpec(memory_space=pl.ANY)] * raw_out + whole(*out_shape[raw_out:]),
        scratch_shapes=scratch,
        compiler_params=pltpu.CompilerParams(vmem_limit_bytes=24 * 2**20),
        cost_estimate=pl.CostEstimate(flops=flops, bytes_accessed=2**20, transcendentals=0),
        name=name,
    )(*args)


def on_device(
    motion,
    stiffness,
    point_elem,
    point_owner,
    point_pattern,
    history,
    basis,
    mode_map,
    weights,
    patterns,
):
    size_x, size_y, size_z = motion.shape[1:]
    points = point_elem.shape[0]
    hosts = lax.axis_size("macro")
    capacity = 2 * points // hosts
    slots = capacity * hosts
    modes = mode_map.shape[0]
    half = modes // 2
    hyper = weights.shape[0]
    lanes = 128
    direct = capacity % 16 == 0
    packed = capacity * 4 == lanes and slots % lanes == 0
    motion = in_hbm(motion)
    stiffness = in_hbm(stiffness)
    elem = in_hbm(point_elem.reshape(1, points))
    owner = in_hbm(point_owner.reshape(1, points))
    pattern = in_hbm(point_pattern.reshape(1, points))
    history = in_hbm(history)
    map_rows = in_hbm(mode_map.T)

    rows = in_hbm(basis.reshape(6, hyper, modes))
    wide, kept = 256, 3
    sent = (
        [shape_of((hosts, 2 * capacity + 8, half), BF16)]
        if direct
        else [shape_of((slots, modes), BF16), shape_of((hosts, modes), BF16)]
    )
    swap, x_swap = shape_of((4, size_x, size_z)), shape_of((4, size_y, size_z))
    arguments = (motion, elem, owner, history, pattern, map_rows, stiffness)
    small = (map_rows, in_hbm(weights.reshape(1, hyper)), in_hbm(patterns.T))
    *payload, first, second, x_first, x_second, blocks, map_here, weights, bit_words = call(
        functools.partial(dispatch_kernel, hosts, capacity, direct),
        "dispatch",
        sent
        + [swap, swap, x_swap, x_swap, shape_of((kept, 6, wide, modes), BF16)]
        + [shape_of(value.shape, value.dtype) for value in small],
        (*arguments, *small[1:], rows),
        [VMEM(value.shape, value.dtype) for value in (*arguments[:5], stiffness, sent[0])]
        + [pltpu.SemaphoreType.DMA((10 + kept,))],
        raw=10,
        raw_out=1,
    )

    if direct:
        received = lax.all_to_all(payload[0], "macro", 0, 0, tiled=True)
        groups, group = hosts, capacity
    else:
        slot_rows, ids = payload
        joined = jnp.concatenate(
            [
                slot_rows[:, :half].reshape(hosts, capacity, half),
                slot_rows[:, half:].reshape(hosts, capacity, half),
                ids.reshape(hosts, 2, half),
            ],
            axis=1,
        )
        joined = lax.all_to_all(joined, "macro", 0, 0, tiled=True)
        ids = jnp.sum(joined[:, 2 * capacity :].astype(F32), axis=0).astype(BF16)
        received = jnp.concatenate(
            [
                joined[:, :capacity].reshape(1, slots, half),
                joined[:, capacity : 2 * capacity].reshape(1, slots, half),
                jnp.pad(ids, ((0, 6), (0, 0)))[None],
            ],
            axis=1,
        )
        groups, group = 1, slots

    def swapped(value, axis, start):
        pairs = [(i, i + 1) for i in range(start, lax.axis_size(axis) - 1, 2)]
        return lax.ppermute(value, axis, pairs + [(b, a) for a, b in pairs])

    first, second = swapped(first, "micro", 0), swapped(second, "micro", 1)
    x_first, x_second = swapped(x_first, "macro", 0), swapped(x_second, "macro", 1)

    table, const, bits = call(
        table_kernel,
        "tables",
        [
            shape_of((96, hyper), BF16),
            shape_of((48, lanes)),
            shape_of((hyper, lanes), BF16),
        ],
        (blocks, map_here, weights, bit_words, rows),
        [
            VMEM((hyper // wide - kept, 6, wide, modes), BF16),
            pltpu.SemaphoreType.DMA((hyper // wide - kept,)),
        ],
        raw=1,
    )

    answer = call(
        functools.partial(micro_kernel, packed, hosts, group, patterns.shape[0]),
        "micro_response",
        [shape_of((hosts, 16, lanes))]
        if packed
        else [shape_of((ROWS, slots)), shape_of((2, 8, lanes))],
        (
            received,
            x_first,
            first,
            second,
            const,
            bits,
            table,
            blocks,
            rows,
        ),
        [
            VMEM((slots, modes), BF16),
            VMEM((modes, slots), BF16),
            VMEM((hyper // wide - kept, 6, wide, modes), BF16),
            VMEM((hyper, slots), F32),
            *[VMEM((hyper, slots), BF16)] * 2,
            VMEM((ROWS, slots), F32),
            pltpu.SemaphoreType.DMA((hyper // wide - kept,)),
        ],
        raw=1,
    )

    if packed:
        answered = [lax.all_to_all(answer[0], "macro", 0, 0, tiled=True)]
    else:
        result, edges = answer
        here = lax.axis_index("macro")
        order = jnp.arange(hosts)[:, None, None]
        flat = result.reshape(ROWS, hosts, capacity).transpose(1, 0, 2).reshape(hosts, -1)
        tiles = pl.cdiv(flat.shape[1], lanes)
        flat = jnp.pad(flat, ((0, 0), (0, tiles * lanes - flat.shape[1])))
        joined = jnp.concatenate(
            [flat.reshape(hosts, tiles, lanes), jnp.where(order > here, edges[0], edges[1])], axis=1
        )
        joined = lax.all_to_all(joined, "macro", 0, 0, tiled=True)
        flat = joined[:, :tiles].reshape(hosts, -1)[:, : ROWS * capacity]
        result = flat.reshape(hosts, ROWS, capacity).transpose(1, 0, 2).reshape(ROWS, slots)
        low = lax.dynamic_index_in_dim(joined, jnp.maximum(here - 1, 0), 0, False)
        high = lax.dynamic_index_in_dim(joined, jnp.minimum(here + 1, hosts - 1), 0, False)
        answered = [result, jnp.stack([low[tiles:], high[tiles:]])]

    elastic = call(
        functools.partial(elastic_kernel, hosts, capacity),
        "elastic_forces",
        [
            shape_of(motion.shape),
            shape_of((7, 16, size_z)),
            shape_of((8, points), jnp.int32),
            shape_of((slots, points), BF16),
            shape_of((size_z, points), BF16),
        ],
        (motion, stiffness, elem, owner, first, second),
        [
            VMEM((3, size_x, 16, size_z), F32),
            VMEM((size_x, 16, size_z), F32),
            VMEM((6, size_x + 1, 16, size_z), F32),
        ],
    )

    force, tangent = call(
        functools.partial(final_kernel, packed, hosts, capacity),
        "final_forces",
        [shape_of(motion.shape), shape_of((36, points))],
        (*answered, x_second, x_first, *elastic),
        [
            VMEM((ROWS, points), F32),
            VMEM((3, 4, 16, size_z), F32),
            VMEM((2, 16, size_z), F32),
            VMEM((6, size_x + 1, 16, size_z), F32),
        ],
    )
    return (force, tangent)


def solution(mesh):
    return jax.shard_map(
        on_device,
        mesh=mesh,
        in_specs=(
            P(None, "macro", "micro", None),
            P("macro", "micro", None),
            P(("macro", "micro")),
            P(("macro", "micro")),
            P(("macro", "micro")),
            P(None, ("macro", "micro")),
            P("macro", None, None),
            P(),
            P(),
            P(),
        ),
        out_specs=(P(None, "macro", "micro", None), P(None, ("macro", "micro"))),
        check_vma=False,
    )
```
